128 devices in a mesh: seq: 8 (over x_lo, z), clip: 16 (over y, x_hi, core).
Axes of the slice: x: 4 (x_hi: 2, x_lo: 2; x = x_hi * 2 + x_lo), y: 4, z: 4, core: 2. Of those that a mesh axis runs over, the one named last changes fastest.
Arguments:
- clip_features: bfloat16 [16, 4, 16, 64, 384], P('clip', None, 'seq'), may hold values from -6 to 6
- enc_weight: bfloat16 [3, 3, 3, 384, 16], replicated, may hold values from -0.0625 to 0.0625
- noise_field: float32 [16, 4, 16, 64, 16], P('clip', None, 'seq'), may hold values from -6 to 6
- flow_times: int32 [16, 2], P('clip'), may hold values from 0 to 1000, as said below
- embed_weight: bfloat16 [64, 5120], replicated, may hold values from -0.75 to 0.75
- time_weight: bfloat16 [256, 5120], replicated, may hold values from -0.375 to 0.375
- norm_gain: float32 [5120], replicated, may hold values from 0.25 to 1.75
- qkv_weight: bfloat16 [5120, 3, 3072], P('clip', None, 'seq'), may hold values from -0.078125 to 0.078125
Outputs:
- attn_out: bfloat16 [16, 1024, 3072], P('clip', 'seq')
- attn_tangent: bfloat16 [16, 1024, 3072], P('clip', 'seq')
The draws below stay inside these ranges and needn't reach their ends.
Inputs may be any that keep to these rules, and one draw needn't show every extreme that they name: flow_times[c] = (index of r, index of t) with the index of r at most that of t; some clip has r index 0 and some t index 1000.
All inputs are finite; a program needn't handle non-finite values.
Results may differ from the reference program's by a relative error of at most 0.0044.
Values may be sent and summed in bfloat16 or wider, within the bound.
No kernel may reach another device: no remote copies, remote signals or barrier semaphores. Data moves between devices by JAX's collectives and lax.ppermute only.
A program may use at most 128 MiB of HBM per device.

```python
import jax
import jax.numpy as jnp
from jax import lax

D = 5120
Z = 16
C = 384
HD = 128
HEADS = 24
TFEAT = 256
TGRID = 1000
FR = 4
WL = 64
INNER = 3072
PATCH = 64
HT = 16
CLIPS = 16


def draw_flow_times(key, part):
    key_one, key_two = jax.random.split(jax.random.fold_in(key, 17))
    draw_one = jax.random.randint(key_one, (CLIPS,), 0, TGRID + 1)
    draw_two = jax.random.randint(key_two, (CLIPS,), 0, TGRID + 1)
    start_idx = jnp.minimum(draw_one, draw_two).at[0].set(0)
    finish_idx = jnp.maximum(draw_one, draw_two).at[CLIPS - 1].set(TGRID)
    return jnp.stack([start_idx, finish_idx], axis=1).astype(jnp.int32)


def steps_of(key, shape, cuts, smallest, largest):
    def one(axis_at, blocks):
        steps = jax.random.uniform(jax.random.fold_in(jax.random.fold_in(key, 6), axis_at), (blocks,), jnp.float32, smallest / len(cuts), largest / len(cuts))
        return jnp.repeat(jnp.exp(steps), shape[axis_at] // blocks).reshape((-1,) + (1,) * (len(shape) - axis_at - 1))

    factor_of = one(*cuts[0])
    for cut in cuts[1:]:
        factor_of = factor_of * one(*cut)
    return factor_of


def scatter_about(own_key, shape, width, limit, pieces=(), kind=jnp.bfloat16):
    entries = jax.random.normal(own_key, shape, jnp.float32) * width
    if len(pieces) > 0:
        entries = steps_of(own_key, shape, pieces, -0.22, 0.18) * entries
    return jnp.clip(entries, min=-limit, max=limit).astype(kind)


def setup_inputs(seed: int = 0) -> dict:
    seeds = jax.random.split(jax.random.key(seed), 9)
    clip_features = scatter_about(seeds[0], (CLIPS, FR, HT, WL, C), 1.0, 6.0, ((0, 16), (2, 8)))
    enc_weight = scatter_about(seeds[1], (3, 3, 3, C, Z), (27 * C) ** -0.5, 0.0625)
    noise_field = scatter_about(seeds[2], (CLIPS, FR, HT, WL, Z), 1.0, 6.0, ((0, 16), (2, 8)), jnp.float32)
    flow_times = draw_flow_times(jax.random.fold_in(seeds[8], 71), 0)
    embed_weight = scatter_about(seeds[4], (PATCH, D), PATCH ** -0.5, 0.75)
    time_weight = scatter_about(seeds[5], (TFEAT, D), TFEAT ** -0.5, 0.375)
    norm_gain = jnp.clip(1.0 + 0.15 * jax.random.normal(seeds[6], (D,), jnp.float32), 0.25, 1.75)
    qkv_weight = scatter_about(seeds[7], (D, 3, INNER), D ** -0.5, 0.078125, ((0, 16), (2, 8)))
    return {"clip_features": clip_features, "enc_weight": enc_weight, "noise_field": noise_field, "flow_times": flow_times, "embed_weight": embed_weight, "time_weight": time_weight, "norm_gain": norm_gain, "qkv_weight": qkv_weight}


EPSILON = 1e-06

def time_features(flow_t, flow_h):
    quarter = TFEAT // 4
    freqs_omega = 8.0 * jnp.exp(-jnp.log(100.0) * jnp.arange(quarter, dtype=jnp.float32) / quarter)
    angle_t = freqs_omega * flow_t
    angle_h = freqs_omega * flow_h
    values = jnp.concatenate([jnp.sin(angle_t), jnp.cos(angle_t), jnp.sin(angle_h), jnp.cos(angle_h)])
    tangent = jnp.concatenate([freqs_omega * jnp.cos(angle_t), -freqs_omega * jnp.sin(angle_t), freqs_omega * jnp.cos(angle_h), -freqs_omega * jnp.sin(angle_h)])
    return (values[None, :], tangent[None, :])

def encode(padded, enc_weight):
    frames = padded.shape[0] - 2
    rows = padded.shape[1] - 2
    columns = padded.shape[2] - 2
    latent = jnp.zeros((frames, rows, columns, enc_weight.shape[4]), jnp.float32)
    for tap_time in range(3):
        for tap_row in range(3):
            for tap_col in range(3):
                window = padded[tap_time:tap_time + frames, tap_row:tap_row + rows, tap_col:tap_col + columns]
                latent = latent + jnp.einsum('fhwc,cz->fhwz', window.astype(jnp.float32), enc_weight[tap_time, tap_row, tap_col].astype(jnp.float32))
    return latent

def patchify(field):
    frames, rows, columns, chans = field.shape
    shaped = field.reshape(frames, rows // 2, 2, columns // 2, 2, chans)
    return shaped.transpose(1, 0, 3, 2, 4, 5).reshape(-1, 4 * chans)

def embed(patches, patch_tangent, values, tangent, embed_weight, time_weight, norm_gain):
    high = lax.Precision.HIGHEST
    embed_full = embed_weight.astype(jnp.float32)
    time_full = time_weight.astype(jnp.float32)
    hidden = jnp.dot(patches, embed_full, precision=high) + jnp.dot(values, time_full, precision=high)
    hidden_t = jnp.dot(patch_tangent, embed_full, precision=high) + jnp.dot(tangent, time_full, precision=high)
    inv_rms = lax.rsqrt(lax.optimization_barrier(jnp.mean(hidden * hidden, axis=-1, keepdims=True)) + EPSILON)
    cross = lax.optimization_barrier(jnp.mean(hidden * hidden_t, axis=-1, keepdims=True))
    normed = (hidden * inv_rms * norm_gain).astype(jnp.bfloat16)
    normed_t = (norm_gain * (hidden_t * inv_rms - hidden * inv_rms ** 3 * cross)).astype(jnp.bfloat16)
    return (normed, normed_t)

def attend(query, keys, vals, query_t, keys_t, vals_t):
    score_scale = query.shape[-1] ** (-0.5)
    qf, kf, vf = (query.astype(jnp.float32), keys.astype(jnp.float32), vals.astype(jnp.float32))
    qtf, ktf, vtf = (query_t.astype(jnp.float32), keys_t.astype(jnp.float32), vals_t.astype(jnp.float32))
    scores = jnp.einsum('hqd,hkd->hqk', qf, kf) * score_scale
    score_t = (jnp.einsum('hqd,hkd->hqk', qtf, kf) + jnp.einsum('hqd,hkd->hqk', qf, ktf)) * score_scale
    peak = lax.optimization_barrier(jnp.max(scores, axis=-1, keepdims=True))
    expo = jnp.exp(scores - peak)
    probs = expo / lax.optimization_barrier(jnp.sum(expo, axis=-1, keepdims=True))
    prob_t = probs * (score_t - lax.optimization_barrier(jnp.sum(probs * score_t, axis=-1, keepdims=True)))
    probs_b = probs.astype(jnp.bfloat16).astype(jnp.float32)
    prob_tb = prob_t.astype(jnp.bfloat16).astype(jnp.float32)
    output = jnp.einsum('hqk,hkd->hqd', probs_b, vf).astype(jnp.bfloat16)
    output_t = (jnp.einsum('hqk,hkd->hqd', prob_tb, vf) + jnp.einsum('hqk,hkd->hqd', probs_b, vtf)).astype(jnp.bfloat16)
    return (output, output_t)

def reference(clip_features, enc_weight, noise_field, flow_times, embed_weight, time_weight, norm_gain, qkv_weight):
    weight_flat = qkv_weight.reshape(D, 3 * HEADS * HD)

    def one_clip(inputs):
        feature_map, noise_one, pair = inputs
        padded = jnp.pad(feature_map, ((2, 0), (1, 1), (1, 1), (0, 0)))
        latent = encode(padded, enc_weight)
        start_t = pair[0].astype(jnp.float32) / TGRID
        flow_t = pair[1].astype(jnp.float32) / TGRID
        noisy = (1.0 - flow_t) * latent + flow_t * noise_one
        velocity = noise_one - latent
        values, tangent = time_features(flow_t, flow_t - start_t)
        normed, normed_t = embed(patchify(noisy), patchify(velocity), values, tangent, embed_weight, time_weight, norm_gain)
        projected = jnp.dot(normed, weight_flat, preferred_element_type=jnp.float32).astype(jnp.bfloat16)
        projected_t = jnp.dot(normed_t, weight_flat, preferred_element_type=jnp.float32).astype(jnp.bfloat16)
        tokens_all = normed.shape[0]
        heads_p = projected.reshape(tokens_all, 3, HEADS, HD).transpose(1, 2, 0, 3)
        heads_t = projected_t.reshape(tokens_all, 3, HEADS, HD).transpose(1, 2, 0, 3)
        output, output_t = attend(heads_p[0], heads_p[1], heads_p[2], heads_t[0], heads_t[1], heads_t[2])
        return (output.transpose(1, 0, 2).reshape(tokens_all, HEADS * HD), output_t.transpose(1, 0, 2).reshape(tokens_all, HEADS * HD))
    return lax.map(one_clip, (clip_features, noise_field, flow_times))
```

```python
import jax
import jax.numpy as jnp
import numpy as np
from jax import lax
from jax.experimental import pallas as pl
from jax.experimental.pallas import tpu as pltpu
from jax.sharding import PartitionSpec as P

D = 5120
HD = 128
TFEAT = 256
TGRID = 1000
EPSILON = 1e-06
QUARTER = TFEAT // 4
F32 = jnp.float32
BF = jnp.bfloat16
HIGH = lax.Precision.HIGHEST
LOG2E = 1.4426950408889634
LN2 = 0.6931471805599453
VMEM = pl.BlockSpec(memory_space=pltpu.VMEM)
SMEM = pl.BlockSpec(memory_space=pltpu.SMEM)


def params(limit=48):
    return pltpu.CompilerParams(vmem_limit_bytes=limit * 1024 * 1024)


def dot(a, b, dims=((1,), (0,)), precision=None):
    return lax.dot_general(a, b, (dims, ((), ())), preferred_element_type=F32, precision=precision)


def split(x):
    hi = x.astype(BF)
    return hi, (x - hi.astype(F32)).astype(BF)


def iota(shape, axis):
    return lax.broadcasted_iota(jnp.int32, shape, axis)


def fold_kernel(flow_ref, embed_ref, gain_ref, weight_ref, out_ref):
    rows = out_ref.shape[0]
    scaled_hi, scaled_lo = split(embed_ref[...].astype(F32) * gain_ref[...])
    first = (iota((rows, 1), 0) // 4) % 2 == 0
    width = weight_ref.shape[2]
    for i in range(3):
        w = weight_ref[i]
        total = dot(scaled_hi, w) + dot(scaled_lo, w)
        hi = total.astype(BF).astype(F32)
        out_ref[:, i * width : (i + 1) * width] = jnp.where(first, hi, total - hi).astype(BF)
    lane = iota((rows, 128), 1)
    start, finish = flow_ref[0, 0], flow_ref[0, 1]
    coded = jnp.where(
        lane == 0,
        start // 256,
        jnp.where(lane == 1, start % 256, jnp.where(lane == 2, finish // 256, finish % 256)),
    )
    out_ref[:, 3 * width :] = coded.astype(F32).astype(BF)


def time_kernel(got_ref, time_ref, gain_ref, freq_ref, weight_ref, out_ref):
    rows = out_ref.shape[0]
    groups = rows // 8
    width = weight_ref.shape[2]
    total = got_ref[...].astype(F32)
    codes = total[:, 3 * width :]
    start = (codes[:, 0:1] * 256.0 + codes[:, 1:2]) / TGRID
    finish = (codes[:, 2:3] * 256.0 + codes[:, 3:4]) / TGRID
    freqs = freq_ref[...]
    angle_t = freqs * finish
    angle_h = freqs * (finish - start)
    angle = jnp.concatenate([angle_t, angle_h], axis=1)
    freqs2 = jnp.concatenate([freqs, freqs], axis=1)
    sines, cosines = jnp.sin(angle), jnp.cos(angle)
    place = iota((rows, 1), 0) % 8
    is_value = (place == 4) | (place == 5)
    is_tangent = place >= 6
    first = jnp.where(is_value, sines, jnp.where(is_tangent, freqs2 * cosines, 0.0))
    second = jnp.where(is_value, cosines, jnp.where(is_tangent, -freqs2 * sines, 0.0))
    first_hi, first_lo = split(first)
    second_hi, second_lo = split(second)
    t_first, t_second = time_ref[0], time_ref[1]
    tau = dot(first_hi, t_first) + dot(first_lo, t_first) + dot(second_hi, t_second) + dot(second_lo, t_second)
    tau_hi, tau_lo = split(tau * gain_ref[...])
    summed = total[:, : 3 * width].reshape(groups, 8, 3 * width).sum(axis=0)
    summed = summed + jnp.concatenate([summed[4:], summed[:4]], axis=0)
    keep_hi = place % 2 == 0
    for i in range(3):
        w = weight_ref[i]
        part = dot(tau_hi, w) + dot(tau_lo, w)
        hi = part.astype(BF).astype(F32)
        part = jnp.where(keep_hi, hi, part - hi)
        mine = jnp.concatenate([summed[:, i * width : (i + 1) * width]] * groups, axis=0)
        out_ref[:, i * width : (i + 1) * width] = jnp.where(place < 4, mine, part).astype(BF)


def gather_rows_kernel(got_ref, out_ref):
    rows = got_ref.shape[0]
    row, col = iota((80, rows), 0), iota((80, rows), 1)
    patch = (row < 64) & (col == (row // 4) * 8 + row % 4)
    place = col % 8
    value = (row >= 64) & (row < 68) & ((place == 4) | (place == 5))
    tangent = (row >= 68) & (row < 72) & (place >= 6)
    pick = jnp.where(patch | value | tangent, 1.0, 0.0).astype(BF)
    total = dot(pick, got_ref[...])
    hi = total.astype(BF).astype(F32)
    which = iota((80, 1), 0)
    low = (which == 67) | (which == 71)
    out = jnp.where(low, total - hi, hi).astype(BF)
    for i in range(out_ref.shape[0]):
        out_ref[i] = out


def conv_kernel(x_ref, w_ref, noise_ref, out_ref, xp_ref, wt_ref):
    chans = x_ref.shape[2]
    row, col = iota((128, 128), 0), iota((128, 128), 1)
    row_w = 2 * (row % 32) + (row // 32) % 2
    same = (row // 64) == (col // 64)
    for e in range(3):
        perm = jnp.where(same & (col % 64 == row_w + (e - 1)), 1.0, 0.0).astype(BF)
        for f in range(4):
            moved = dot(perm, x_ref[f]).astype(BF)
            for g in range(4):
                xp_ref[g * 128 + f * 32 : g * 128 + f * 32 + 32, e * chans : (e + 1) * chans] = moved[
                    g * 32 : g * 32 + 32
                ]
        for ab in range(9):
            tap = (ab * 3 + e) * 16
            wt_ref[ab * 16 : ab * 16 + 16, e * chans : (e + 1) * chans] = w_ref[tap : tap + 16, :]
    y = dot(wt_ref[...], xp_ref[...], ((1,), (1,)))
    lane = iota((16, 128), 1)

    def part(a, b, p, q):
        at = (a * 3 + b) * 16
        g = p * 2 + q
        return y[at : at + 16, g * 128 : (g + 1) * 128]

    def frames(of):
        one = jnp.where(lane >= 32, pltpu.roll(of(1), 32, 1), 0.0)
        two = jnp.where(lane >= 64, pltpu.roll(of(0), 64, 1), 0.0)
        return of(2) + one + two

    for q in range(2):
        own0 = frames(lambda a: part(a, 1, 0, q) + part(a, 2, 1, q))
        own1 = frames(lambda a: part(a, 0, 0, q) + part(a, 1, 1, q))
        down = frames(lambda a: part(a, 0, 1, q))
        up = frames(lambda a: part(a, 2, 0, q))
        out_ref[q * 16 : q * 16 + 16, :] = own0
        out_ref[32 + q * 16 : 48 + q * 16, :] = own1
        out_ref[64 + q * 16 : 80 + q * 16, :] = down
        out_ref[96 + q * 16 : 112 + q * 16, :] = up
    r2, c2 = iota((256, 256), 0), iota((256, 256), 1)
    spread = ((r2 // 64) == (c2 // 32) % 4) & (r2 % 64 == 2 * (c2 % 32) + c2 // 128)
    spread = jnp.where(spread, 1.0, 0.0)
    noise = jnp.concatenate(
        [jnp.concatenate([noise_ref[f, p] for f in range(4)], axis=1) for p in range(2)], axis=0
    )
    moved = dot(noise, spread, precision=HIGH)
    for p in range(2):
        for q in range(2):
            at = 128 + (p * 2 + q) * 16
            out_ref[at : at + 16, :] = moved[p * 16 : p * 16 + 16, q * 128 : (q + 1) * 128]


def gram_kernel(embed_ref, time_ref, feat_ref, gram_ref, cross_ref, square_ref):
    feats = feat_ref[...]
    tau = dot(feats, time_ref[...].astype(F32), precision=HIGH)
    embed = embed_ref[...]
    gram_ref[...] = dot(embed, embed, ((1,), (1,)))
    cross_ref[...] = dot(embed.astype(F32), tau, ((1,), (1,)), precision=HIGH)
    tau0 = tau[0:1]
    square_ref[...] = jnp.sum(tau * tau0, axis=1, keepdims=True) + jnp.zeros((8, 128), F32)


def feature_kernel(pos_ref, flow_ref, *refs):
    slots = refs[:8]
    gram_ref, cross_ref, square_ref, aq_ref, s_ref, d_ref, v_ref = refs[8:]
    here = pos_ref[0]
    flow_t = flow_ref[0]
    patches, tangents = [], []
    for k in range(8):
        owner = lax.rem(here - k + 8, 8)
        before = slots[(k + 1) % 8][64:96, :]
        after = slots[(k + 7) % 8][96:128, :]
        halo = jnp.concatenate(
            [jnp.where(owner > 0, before, 0.0), jnp.where(owner < 7, after, 0.0)], axis=0
        )
        latent = slots[k][0:64, :] + halo
        noise = slots[k][128:192, :]
        patches.append((1.0 - flow_t) * latent + flow_t * noise)
        tangents.append(noise - latent)
    p = jnp.concatenate(patches, axis=1)
    dp = jnp.concatenate(tangents, axis=1)
    gp = dot(gram_ref[...], p, precision=HIGH)
    cross = cross_ref[...]
    e_tau, e_dtau = cross[:, 0:1], cross[:, 1:2]
    square = square_ref[...]
    mean_sq = jnp.sum(p * (gp + 2.0 * e_tau), axis=0, keepdims=True) + square[0:1, 0:1]
    mean_sq = jnp.maximum(mean_sq * (1.0 / D), 0.0)
    mixed = jnp.sum(gp * dp + p * e_dtau + dp * e_tau, axis=0, keepdims=True) + square[1:2, 0:1]
    s = lax.rsqrt(mean_sq + EPSILON)
    c = -(s * s * s) * (mixed * (1.0 / D))
    a = p * s
    da = dp * s + p * c
    up = lambda x: x.astype(BF).astype(F32)
    a_hi, da_hi = up(a), up(da)
    a_lo, da_lo = a - a_hi, da - da_hi
    s_hi, c_hi = up(s), up(c)
    s_lo, c_lo = s - s_hi, c - c_hi
    tokens = p.shape[1]
    r = iota((8, tokens), 0)

    def coefs(high, low, kind):
        if kind == 0:
            return jnp.where((r % 4 == 0) | (r % 4 == 3), high, jnp.where(r % 4 == 1, low, 0.0))
        return jnp.where(r % 4 == 2, low, high)

    def misc(kind):
        plain = jnp.where(r < 4, coefs(s_hi, s_lo, kind), 0.0)
        tangent = jnp.where(r < 4, coefs(c_hi, c_lo, kind), coefs(s_hi, s_lo, kind))
        return plain, tangent

    zeros = lambda n: jnp.zeros((n, tokens), F32)
    cat = lambda xs: jnp.concatenate(xs, axis=0)
    m_s, m_d = misc(1)
    v_s, v_d = misc(0)
    s_ref[...] = cat([a_hi, a_hi, a_lo, m_s, zeros(56)]).astype(BF)
    d_ref[...] = cat([da_hi, da_hi, da_lo, m_d, zeros(56)]).astype(BF)
    v_ref[...] = cat([a_hi, da_hi, a_lo, v_s, v_d, zeros(48)]).astype(BF)
    own = lambda x: x[:, :128]
    z = jnp.zeros((120, 128), F32)
    aq_ref[0:128, :] = cat([own(a_hi), own(a_lo), own(v_s), z]).T.astype(BF)
    aq_ref[128:256, :] = cat([own(da_hi), own(da_lo), own(v_d), z]).T.astype(BF)


def attention_kernel(n_ref, aq_ref, as_ref, ad_ref, av_ref, out_ref, dout_ref, s_ref, d_ref, e_ref, t_ref, l_ref):
    n = n_ref[0]
    m, misc = n[:64], n[64:80]
    width = n.shape[1] // 3
    heads = width // HD
    zero = lambda r, c: jnp.zeros((r, c), BF)
    nq = jnp.concatenate([m[:, :width], m[:, :width], misc[:, :width], zero(112, width)], axis=0)
    q_all = dot(aq_ref[...], nq) * (LOG2E * HD ** -0.5)
    lane = iota((256, 256), 1)
    low_lane = ((lane >= 64) & (lane < 128)) | (lane == 193) | (lane == 197)
    for h in range(heads):
        cols = slice(h * HD, (h + 1) * HD)
        mk, misck = m[:, width:][:, cols], misc[:, width:][:, cols]
        nk = jnp.concatenate([mk, mk, mk, misck, zero(48, HD)], axis=0)
        q_hi, q_lo = split(q_all[:, cols])
        absorbed = dot(
            jnp.concatenate([q_hi, q_lo], axis=1), jnp.concatenate([nk, nk], axis=1), ((1,), (1,))
        )
        hi = absorbed.astype(BF).astype(F32)
        x = jnp.where(low_lane, absorbed - hi, hi).astype(BF)
        s_ref[h] = dot(x[:128], as_ref[...])
        d_ref[h] = dot(x[128:], as_ref[...]) + dot(x[:128], ad_ref[...])
    for h in range(heads):
        for i in range(8):
            r = slice(i * 16, (i + 1) * 16)
            s = s_ref[h, r]
            e = jnp.exp2(s - jnp.max(s, axis=1, keepdims=True))
            d = d_ref[h, r]
            inv = 1.0 / jnp.sum(e, axis=1, keepdims=True)
            mean = jnp.sum(e * d, axis=1, keepdims=True) * inv
            e_ref[h, r] = e.astype(BF)
            t_ref[h, r] = (e * (d - mean)).astype(BF)
            l_ref[h, r] = jnp.broadcast_to(inv, (16, 128))
    for h in range(heads):
        cols = slice(h * HD, (h + 1) * HD)
        mv, miscv = m[:, 2 * width :][:, cols], misc[:, 2 * width :][:, cols]
        inv = l_ref[h][:, 0:1]
        mix = dot(e_ref[h], av_ref[...], ((1,), (1,))) * inv
        mix_t = dot(t_ref[h], av_ref[...], ((1,), (1,))) * (inv * LN2)
        nx = jnp.concatenate([mv, zero(64, HD), mv, miscv, zero(48, HD)], axis=0)
        ny = jnp.concatenate([zero(64, HD), mv, zero(64, HD), zero(8, HD), miscv[:8], zero(48, HD)], axis=0)
        hi, lo = split(mix)
        hi_t, lo_t = split(mix_t)
        out_ref[:, cols] = (dot(hi, nx) + dot(lo, nx)).astype(BF)
        dout_ref[:, cols] = (dot(hi_t, nx) + dot(lo_t, nx) + dot(hi, ny) + dot(lo, ny)).astype(BF)


def time_features(flow_t, flow_h):
    freqs = 8.0 * jnp.exp(-jnp.log(100.0) * jnp.arange(QUARTER, dtype=F32) / QUARTER)
    angle_t = freqs * flow_t
    angle_h = freqs * flow_h
    values = jnp.concatenate([jnp.sin(angle_t), jnp.cos(angle_t), jnp.sin(angle_h), jnp.cos(angle_h)])
    tangent = jnp.concatenate(
        [freqs * jnp.cos(angle_t), -freqs * jnp.sin(angle_t), freqs * jnp.cos(angle_h), -freqs * jnp.sin(angle_h)]
    )
    return jnp.stack([values, tangent])


def local(clip_features, enc_weight, noise_field, flow_times, embed_weight, time_weight, norm_gain, qkv_weight):
    clips = lax.axis_size("clip")
    peers = lax.axis_size("seq")
    at_clip = lax.axis_index("clip")
    at_seq = lax.axis_index("seq")
    depth = qkv_weight.shape[0]
    width = qkv_weight.shape[2]
    weight = qkv_weight.transpose(1, 0, 2)
    own = at_clip * depth
    shape = jax.ShapeDtypeStruct

    embed_own = lax.dynamic_slice_in_dim(embed_weight, own, depth, axis=1)
    embed_own = jnp.broadcast_to(embed_own.reshape(clips, 1, 4, depth), (clips, 2, 4, depth)).reshape(8 * clips, depth)
    gain_own = lax.dynamic_slice_in_dim(norm_gain, own, depth, axis=0)[None]
    freqs = 8.0 * jnp.exp(-jnp.log(100.0) * jnp.arange(QUARTER, dtype=F32) / QUARTER)[None]
    rows = 8 * clips
    partial = pl.pallas_call(
        fold_kernel,
        out_shape=shape((rows, 3 * width + 128), BF),
        in_specs=[SMEM, VMEM, VMEM, VMEM],
        out_specs=VMEM,
        compiler_params=params(),
        name="fold",
    )(flow_times, embed_own, gain_own, weight)
    got = lax.all_to_all(partial.reshape(clips, 8, -1), "clip", 0, 0, tiled=True).reshape(rows, -1)

    time_own = lax.dynamic_slice_in_dim(time_weight, own, depth, axis=1)
    time_own = time_own.reshape(2, 2, QUARTER, depth).transpose(1, 0, 2, 3).reshape(2, 2 * QUARTER, depth)
    second = pl.pallas_call(
        time_kernel,
        out_shape=shape((rows, 3 * width), BF),
        in_specs=[VMEM] * 5,
        out_specs=VMEM,
        compiler_params=params(),
        name="time_rows",
    )(got, time_own, gain_own, freqs, weight)
    got2 = lax.all_to_all(second.reshape(clips, 8, -1), "clip", 0, 0, tiled=True).reshape(rows, -1)
    folded = pl.pallas_call(
        gather_rows_kernel,
        out_shape=shape((peers, 80, 3 * width), BF),
        in_specs=[VMEM],
        out_specs=VMEM,
        compiler_params=params(),
        name="folded_rows",
    )(got2)
    folded = lax.all_to_all(folded, "seq", 0, 0, tiled=True)

    conv = pl.pallas_call(
        conv_kernel,
        out_shape=shape((192, 128), F32),
        in_specs=[VMEM] * 3,
        out_specs=VMEM,
        scratch_shapes=[pltpu.VMEM((512, 3 * 384), BF), pltpu.VMEM((144, 3 * 384), BF)],
        compiler_params=params(),
        name="conv",
    )(
        clip_features.reshape(4, 128, 384),
        enc_weight.transpose(0, 1, 2, 4, 3).reshape(432, 384),
        noise_field[0].transpose(0, 1, 3, 2),
    )
    slots = [conv] + [
        lax.ppermute(conv, "seq", [(i, (i + k) % peers) for i in range(peers)]) for k in range(1, peers)
    ]
    flow = flow_times[0].astype(F32) / TGRID
    flow_t = flow[1]
    feats = time_features(flow_t, flow_t - flow[0])
    feats = jnp.concatenate([feats, jnp.zeros((6, TFEAT), F32)], axis=0)
    gram, cross, square = pl.pallas_call(
        gram_kernel,
        out_shape=[shape((64, 64), F32), shape((64, 8), F32), shape((8, 128), F32)],
        in_specs=[VMEM] * 3,
        out_specs=[VMEM] * 3,
        compiler_params=params(),
        name="gram",
    )(embed_weight, time_weight, feats)
    tokens = 128 * peers
    aq, a_s, a_d, a_v = pl.pallas_call(
        feature_kernel,
        out_shape=[shape((256, 256), BF)] + [shape((256, tokens), BF)] * 3,
        in_specs=[SMEM, SMEM] + [VMEM] * 11,
        out_specs=[VMEM] * 4,
        compiler_params=params(),
        name="features",
    )(at_seq[None], flow_t[None], *slots, gram, cross, square)

    whole = lambda shp: pl.BlockSpec(shp, lambda i: (0, 0))
    heads = width // HD
    out, dout = pl.pallas_call(
        attention_kernel,
        grid=(peers,),
        out_shape=[shape((128, peers * width), BF)] * 2,
        in_specs=[
            pl.BlockSpec((1, 80, 3 * width), lambda i: (i, 0, 0)),
            whole((256, 256)),
            whole((256, tokens)),
            whole((256, tokens)),
            whole((256, tokens)),
        ],
        out_specs=[pl.BlockSpec((128, width), lambda i: (0, i))] * 2,
        scratch_shapes=[
            pltpu.VMEM((heads, 128, tokens), F32),
            pltpu.VMEM((heads, 128, tokens), F32),
            pltpu.VMEM((heads, 128, tokens), BF),
            pltpu.VMEM((heads, 128, tokens), BF),
            pltpu.VMEM((heads, 128, 128), F32),
        ],
        compiler_params=params(),
        name="attention",
    )(folded, aq, a_s, a_d, a_v)
    return (out[None], dout[None])


def solution(mesh):
    placed = (
        P("clip", None, "seq", None, None),
        P(),
        P("clip", None, "seq", None, None),
        P("clip", None),
        P(),
        P(),
        P(),
        P("clip", None, "seq"),
    )
    return jax.shard_map(
        local,
        mesh=mesh,
        in_specs=placed,
        out_specs=(P("clip", "seq", None), P("clip", "seq", None)),
        check_vma=False,
    )
```

```python
import jax
import jax.numpy as jnp
import numpy as np
from jax import lax
from jax.experimental import pallas as pl
from jax.experimental.pallas import tpu as pltpu
from jax.sharding import PartitionSpec as P

D = 5120
HD = 128
TFEAT = 256
TGRID = 1000
EPSILON = 1e-06
QUARTER = TFEAT // 4
F32 = jnp.float32
BF = jnp.bfloat16
HIGH = lax.Precision.HIGHEST
LOG2E = 1.4426950408889634
LN2 = 0.6931471805599453
VMEM = pl.BlockSpec(memory_space=pltpu.VMEM)
SMEM = pl.BlockSpec(memory_space=pltpu.SMEM)
ANY = pl.BlockSpec(memory_space=pl.ANY)


def params(limit=48):
    return pltpu.CompilerParams(vmem_limit_bytes=limit * 1024 * 1024)


def dot(a, b, dims=((1,), (0,)), precision=None):
    return lax.dot_general(a, b, (dims, ((), ())), preferred_element_type=F32, precision=precision)


def split(x):
    hi = x.astype(BF)
    return hi, (x - hi.astype(F32)).astype(BF)


def iota(shape, axis):
    return lax.broadcasted_iota(jnp.int32, shape, axis)


def fold_kernel(clip_ref, flow_ref, embed_ref, gain_ref, weight_ref, out_ref, e_ref, g_ref, w_ref, sems):
    rows = out_ref.shape[0]
    _, depth, width = weight_ref.shape
    window = e_ref.shape[1]
    at_clip = clip_ref[0]
    odd = at_clip % 2
    base = pl.multiple_of(at_clip * depth - odd * 64, 128)
    copies = [
        pltpu.make_async_copy(embed_ref.at[:, pl.ds(base, window)], e_ref, sems.at[0]),
        pltpu.make_async_copy(gain_ref.at[:, pl.ds(base, window)], g_ref, sems.at[1]),
    ] + [pltpu.make_async_copy(weight_ref.at[i], w_ref.at[i], sems.at[2 + i]) for i in range(3)]
    for copy in copies:
        copy.start()
    lane = iota((rows, 128), 1)
    start, finish = flow_ref[0, 0], flow_ref[0, 1]
    coded = jnp.where(
        lane == 0,
        start // 256,
        jnp.where(lane == 1, start % 256, jnp.where(lane == 2, finish // 256, finish % 256)),
    )
    out_ref[:, 3 * width :] = coded.astype(F32).astype(BF)
    row, col = iota((rows, 64), 0), iota((rows, 64), 1)
    twice = jnp.where(col == (row // 8) * 4 + row % 4, 1.0, 0.0).astype(BF)
    copies[0].wait()
    copies[1].wait()
    scaled = dot(twice, e_ref[...]) * g_ref[...]
    scaled = jnp.where(odd == 1, scaled[:, 64 : 64 + depth], scaled[:, :depth])
    scaled_hi, scaled_lo = split(scaled)
    first = (iota((rows, 1), 0) // 4) % 2 == 0
    for i in range(3):
        copies[2 + i].wait()
        w = w_ref[i]
        total = dot(scaled_hi, w) + dot(scaled_lo, w)
        hi = total.astype(BF).astype(F32)
        out_ref[:, i * width : (i + 1) * width] = jnp.where(first, hi, total - hi).astype(BF)


def time_kernel(got_ref, time_ref, gain_ref, freq_ref, weight_ref, out_ref):
    rows = out_ref.shape[0]
    groups = rows // 8
    width = weight_ref.shape[2]
    total = got_ref[...].astype(F32)
    codes = total[:, 3 * width :]
    start = (codes[:, 0:1] * 256.0 + codes[:, 1:2]) / TGRID
    finish = (codes[:, 2:3] * 256.0 + codes[:, 3:4]) / TGRID
    freqs = freq_ref[...]
    angle_t = freqs * finish
    angle_h = freqs * (finish - start)
    angle = jnp.concatenate([angle_t, angle_h], axis=1)
    freqs2 = jnp.concatenate([freqs, freqs], axis=1)
    sines, cosines = jnp.sin(angle), jnp.cos(angle)
    place = iota((rows, 1), 0) % 8
    is_value = (place == 4) | (place == 5)
    is_tangent = place >= 6
    first = jnp.where(is_value, sines, jnp.where(is_tangent, freqs2 * cosines, 0.0))
    second = jnp.where(is_value, cosines, jnp.where(is_tangent, -freqs2 * sines, 0.0))
    first_hi, first_lo = split(first)
    second_hi, second_lo = split(second)
    t_first, t_second = time_ref[0], time_ref[1]
    tau = dot(first_hi, t_first) + dot(first_lo, t_first) + dot(second_hi, t_second) + dot(second_lo, t_second)
    tau_hi, tau_lo = split(tau * gain_ref[...])
    summed = total[:, : 3 * width].reshape(groups, 8, 3 * width).sum(axis=0)
    summed = summed + jnp.concatenate([summed[4:], summed[:4]], axis=0)
    keep_hi = place % 2 == 0
    for i in range(3):
        w = weight_ref[i]
        part = dot(tau_hi, w) + dot(tau_lo, w)
        hi = part.astype(BF).astype(F32)
        part = jnp.where(keep_hi, hi, part - hi)
        mine = jnp.concatenate([summed[:, i * width : (i + 1) * width]] * groups, axis=0)
        out_ref[:, i * width : (i + 1) * width] = jnp.where(place < 4, mine, part).astype(BF)


def gather_rows_kernel(got_ref, out_ref):
    rows = got_ref.shape[0]
    row, col = iota((80, rows), 0), iota((80, rows), 1)
    patch = (row < 64) & (col == (row // 4) * 8 + row % 4)
    place = col % 8
    value = (row >= 64) & (row < 68) & ((place == 4) | (place == 5))
    tangent = (row >= 68) & (row < 72) & (place >= 6)
    pick = jnp.where(patch | value | tangent, 1.0, 0.0).astype(BF)
    total = dot(pick, got_ref[...])
    hi = total.astype(BF).astype(F32)
    which = iota((80, 1), 0)
    low = (which == 67) | (which == 71)
    out = jnp.where(low, total - hi, hi).astype(BF)
    for i in range(out_ref.shape[0]):
        out_ref[i] = out


def conv_kernel(x_ref, w_ref, noise_ref, out_ref, xp_ref, wt_ref):
    chans = x_ref.shape[2]
    row, col = iota((128, 128), 0), iota((128, 128), 1)
    row_w = 2 * (row % 32) + (row // 32) % 2
    same = (row // 64) == (col // 64)
    for e in range(3):
        perm = jnp.where(same & (col % 64 == row_w + (e - 1)), 1.0, 0.0).astype(BF)
        for f in range(4):
            moved = dot(perm, x_ref[f]).astype(BF)
            for g in range(4):
                xp_ref[g * 128 + f * 32 : g * 128 + f * 32 + 32, e * chans : (e + 1) * chans] = moved[
                    g * 32 : g * 32 + 32
                ]
        for ab in range(9):
            tap = (ab * 3 + e) * 16
            wt_ref[ab * 16 : ab * 16 + 16, e * chans : (e + 1) * chans] = w_ref[tap : tap + 16, :]
    y = dot(wt_ref[...], xp_ref[...], ((1,), (1,)))
    lane = iota((16, 128), 1)

    def part(a, b, p, q):
        at = (a * 3 + b) * 16
        g = p * 2 + q
        return y[at : at + 16, g * 128 : (g + 1) * 128]

    def frames(of):
        one = jnp.where(lane >= 32, pltpu.roll(of(1), 32, 1), 0.0)
        two = jnp.where(lane >= 64, pltpu.roll(of(0), 64, 1), 0.0)
        return of(2) + one + two

    for q in range(2):
        own0 = frames(lambda a: part(a, 1, 0, q) + part(a, 2, 1, q))
        own1 = frames(lambda a: part(a, 0, 0, q) + part(a, 1, 1, q))
        down = frames(lambda a: part(a, 0, 1, q))
        up = frames(lambda a: part(a, 2, 0, q))
        out_ref[q * 16 : q * 16 + 16, :] = own0
        out_ref[32 + q * 16 : 48 + q * 16, :] = own1
        out_ref[64 + q * 16 : 80 + q * 16, :] = down
        out_ref[96 + q * 16 : 112 + q * 16, :] = up
    r2, c2 = iota((256, 256), 0), iota((256, 256), 1)
    spread = ((r2 // 64) == (c2 // 32) % 4) & (r2 % 64 == 2 * (c2 % 32) + c2 // 128)
    spread = jnp.where(spread, 1.0, 0.0)
    noise = jnp.concatenate(
        [jnp.concatenate([noise_ref[f, p] for f in range(4)], axis=1) for p in range(2)], axis=0
    )
    moved = dot(noise, spread, precision=HIGH)
    for p in range(2):
        for q in range(2):
            at = 128 + (p * 2 + q) * 16
            out_ref[at : at + 16, :] = moved[p * 16 : p * 16 + 16, q * 128 : (q + 1) * 128]


def gram_kernel(embed_ref, time_ref, feat_ref, out_ref):
    feat_hi, feat_lo = split(feat_ref[...])
    feat_mid = (feat_ref[...] - feat_hi.astype(F32) - feat_lo.astype(F32)).astype(BF)
    feats = jnp.concatenate([feat_hi, feat_lo, feat_mid, jnp.zeros_like(feat_hi)], axis=0)
    tau = dot(feats, time_ref[...])
    tau = tau[0:8] + tau[8:16] + tau[16:24]
    embed = embed_ref[...]
    out_ref[0:64, 0:64] = dot(embed, embed, ((1,), (1,)))
    tau_hi, tau_lo = split(tau)
    tau_mid = (tau - tau_hi.astype(F32) - tau_lo.astype(F32)).astype(BF)
    taus = jnp.concatenate([tau_hi, tau_lo, tau_mid, jnp.zeros_like(tau_hi)], axis=0)
    cross = dot(embed, taus, ((1,), (1,)))
    out_ref[0:64, 64:128] = jnp.concatenate(
        [cross[:, 0:8] + cross[:, 8:16] + cross[:, 16:24], jnp.zeros((64, 56), F32)], axis=1
    )
    out_ref[64:72, :] = jnp.sum(tau * tau[0:1], axis=1, keepdims=True) + jnp.zeros((8, 128), F32)


def feature_kernel(pos_ref, flow_ref, *refs):
    arrived = refs[:8]
    gram_ref, aq_ref, s_ref, d_ref, v_ref, slots, sems = refs[8:]
    copies = [pltpu.make_async_copy(arrived[k], slots.at[k], sems.at[k]) for k in range(8)]
    for copy in copies:
        copy.start()
    for copy in copies:
        copy.wait()
    here = pos_ref[0]
    flow_t = flow_ref[0]
    patches, tangents = [], []
    for k in range(8):
        owner = lax.rem(here - k + 8, 8)
        before = slots[(k + 1) % 8, 64:96, :]
        after = slots[(k + 7) % 8, 96:128, :]
        halo = jnp.concatenate(
            [jnp.where(owner > 0, before, 0.0), jnp.where(owner < 7, after, 0.0)], axis=0
        )
        latent = slots[k, 0:64, :] + halo
        noise = slots[k, 128:192, :]
        patches.append((1.0 - flow_t) * latent + flow_t * noise)
        tangents.append(noise - latent)
    p = jnp.concatenate(patches, axis=1)
    dp = jnp.concatenate(tangents, axis=1)
    gp = dot(gram_ref[0:64, 0:64], p, precision=HIGH)
    e_tau, e_dtau = gram_ref[0:64, 64:65], gram_ref[0:64, 65:66]
    mean_sq = jnp.sum(p * (gp + 2.0 * e_tau), axis=0, keepdims=True) + gram_ref[64:65, 0:1]
    mean_sq = jnp.maximum(mean_sq * (1.0 / D), 0.0)
    mixed = jnp.sum(gp * dp + p * e_dtau + dp * e_tau, axis=0, keepdims=True) + gram_ref[65:66, 0:1]
    s = lax.rsqrt(mean_sq + EPSILON)
    c = -(s * s * s) * (mixed * (1.0 / D))
    a = p * s
    da = dp * s + p * c
    up = lambda x: x.astype(BF).astype(F32)
    a_hi, da_hi = up(a), up(da)
    a_lo, da_lo = a - a_hi, da - da_hi
    s_hi, c_hi = up(s), up(c)
    s_lo, c_lo = s - s_hi, c - c_hi
    tokens = p.shape[1]
    r = iota((8, tokens), 0)

    def coefs(high, low, kind):
        if kind == 0:
            return jnp.where((r % 4 == 0) | (r % 4 == 3), high, jnp.where(r % 4 == 1, low, 0.0))
        return jnp.where(r % 4 == 2, low, high)

    def misc(kind):
        plain = jnp.where(r < 4, coefs(s_hi, s_lo, kind), 0.0)
        tangent = jnp.where(r < 4, coefs(c_hi, c_lo, kind), coefs(s_hi, s_lo, kind))
        return plain, tangent

    zeros = lambda n: jnp.zeros((n, tokens), F32)
    cat = lambda xs: jnp.concatenate(xs, axis=0)
    m_s, m_d = misc(1)
    v_s, v_d = misc(0)
    s_ref[...] = cat([a_hi, a_hi, a_lo, m_s, zeros(56)]).astype(BF)
    d_ref[...] = cat([a_hi, da_hi, a_hi, m_s, zeros(8), m_d, zeros(40)]).astype(BF)
    v_ref[...] = cat([a_hi, a_hi, da_hi, v_s, v_d, v_s, v_d, zeros(32)]).astype(BF)
    own = lambda x: x[:, :128]
    z = jnp.zeros((120, 128), F32)
    aq_ref[0:128, :] = cat([own(a_hi), own(a_lo), own(v_s), z]).T.astype(BF)
    aq_ref[128:256, :] = cat([own(da_hi), own(da_lo), own(v_d), z]).T.astype(BF)


def attention_kernel(n_ref, aq_ref, as_ref, ad_ref, av_ref, out_ref, dout_ref, s_ref, d_ref, et_ref, l_ref):
    n = n_ref[0]
    m, misc = n[:64], n[64:80]
    width = n.shape[1] // 3
    heads = width // HD
    rows = heads * 128
    zero = lambda r, c=HD: jnp.zeros((r, c), BF)
    lane = iota((128, 256), 1)
    low_s = ((lane >= 64) & (lane < 128)) | (lane == 193) | (lane == 197)
    low_d = ((lane >= 128) & (lane < 192)) | (lane == 193) | (lane == 209) | (lane == 213)
    from_q = ((lane >= 64) & (lane < 128)) | (lane >= 200)
    lane = iota((256, 256), 1)
    low_r = ((lane >= 64) & (lane < 128)) | (lane >= 208)
    nq = jnp.concatenate([m[:, :width], m[:, :width], misc[:, :width], zero(112, width)], axis=0)
    q_all = dot(aq_ref[...], nq) * (LOG2E * HD ** -0.5)
    xs, xd = [], []
    for h in range(heads):
        cols = slice(width + h * HD, width + (h + 1) * HD)
        mk, misck = m[:, cols], misc[:, cols]
        nk = jnp.concatenate([mk, mk, mk, misck, misck, zero(32)], axis=0)
        q_hi, q_lo = split(q_all[:, h * HD : (h + 1) * HD])
        absorbed = dot(
            jnp.concatenate([q_hi, q_lo], axis=1), jnp.concatenate([nk, nk], axis=1), ((1,), (1,))
        )
        hi = absorbed.astype(BF).astype(F32)
        lo = absorbed - hi
        xs.append(jnp.where(low_s, lo[:128], hi[:128]).astype(BF))
        low = jnp.where(from_q, lo[:128], lo[128:])
        high = jnp.where(from_q, hi[:128], hi[128:])
        xd.append(jnp.where(low_d, low, high).astype(BF))
    s_ref[...] = dot(jnp.concatenate(xs, axis=0), as_ref[...])
    d_ref[...] = dot(jnp.concatenate(xd, axis=0), ad_ref[...])
    for i in range(rows // 16):
        r = slice(i * 16, (i + 1) * 16)
        s = s_ref[r]
        e = jnp.exp2(s - jnp.max(s, axis=1, keepdims=True))
        d = d_ref[r]
        inv = 1.0 / jnp.sum(e, axis=1, keepdims=True)
        mean = jnp.sum(e * d, axis=1, keepdims=True) * inv
        et_ref[r] = e.astype(BF)
        et_ref[rows + i * 16 : rows + (i + 1) * 16] = (e * (d - mean)).astype(BF)
        l_ref[r] = jnp.broadcast_to(inv, (16, 128))
    mixes = dot(et_ref[...], av_ref[...], ((1,), (1,)))
    for h in range(heads):
        cols = slice(2 * width + h * HD, 2 * width + (h + 1) * HD)
        mv, miscv = m[:, cols], misc[:, cols]
        inv = l_ref[h * 128 : (h + 1) * 128, 0:1]
        mix = mixes[h * 128 : (h + 1) * 128] * inv
        mix_t = mixes[rows + h * 128 : rows + (h + 1) * 128] * (inv * LN2)
        nx = jnp.concatenate([mv, mv, zero(64), miscv, miscv, zero(32)], axis=0)
        late = jnp.concatenate([zero(8), miscv[:8]], axis=0)
        ny = jnp.concatenate([zero(128), mv, late, late, zero(32)], axis=0)
        both = jnp.concatenate([mix, mix_t], axis=0)
        hi = both.astype(BF).astype(F32)
        both = jnp.where(low_r, both - hi, hi).astype(BF)
        z = dot(both, jnp.concatenate([nx, ny], axis=1))
        out_ref[:, h * HD : (h + 1) * HD] = z[:128, :HD].astype(BF)
        dout_ref[:, h * HD : (h + 1) * HD] = (z[128:, :HD] + z[:128, HD:]).astype(BF)


def time_features(flow_t, flow_h):
    freqs = 8.0 * jnp.exp(-jnp.log(100.0) * jnp.arange(QUARTER, dtype=F32) / QUARTER)
    angle_t = freqs * flow_t
    angle_h = freqs * flow_h
    values = jnp.concatenate([jnp.sin(angle_t), jnp.cos(angle_t), jnp.sin(angle_h), jnp.cos(angle_h)])
    tangent = jnp.concatenate(
        [freqs * jnp.cos(angle_t), -freqs * jnp.sin(angle_t), freqs * jnp.cos(angle_h), -freqs * jnp.sin(angle_h)]
    )
    return jnp.stack([values, tangent])


def local(clip_features, enc_weight, noise_field, flow_times, embed_weight, time_weight, norm_gain, qkv_weight):
    clips = lax.axis_size("clip")
    peers = lax.axis_size("seq")
    at_clip = lax.axis_index("clip")
    at_seq = lax.axis_index("seq")
    depth = qkv_weight.shape[0]
    width = qkv_weight.shape[2]
    weight = qkv_weight.transpose(1, 0, 2)
    own = at_clip * depth
    shape = jax.ShapeDtypeStruct

    gain_own = lax.dynamic_slice_in_dim(norm_gain, own, depth, axis=0)[None]
    freqs = 8.0 * jnp.exp(-jnp.log(100.0) * jnp.arange(QUARTER, dtype=F32) / QUARTER)[None]
    rows = 8 * clips
    partial = pl.pallas_call(
        fold_kernel,
        out_shape=shape((rows, 3 * width + 128), BF),
        in_specs=[SMEM, SMEM, ANY, ANY, ANY],
        out_specs=VMEM,
        scratch_shapes=[
            pltpu.VMEM((64, depth + 64), BF),
            pltpu.VMEM((1, depth + 64), F32),
            pltpu.VMEM((3, depth, width), BF),
            pltpu.SemaphoreType.DMA((5,)),
        ],
        compiler_params=params(),
        name="fold",
    )(at_clip[None], flow_times, embed_weight, norm_gain[None], weight)
    got = lax.all_to_all(partial.reshape(clips, 8, -1), "clip", 0, 0, tiled=True).reshape(rows, -1)

    conv = pl.pallas_call(
        conv_kernel,
        out_shape=shape((192, 128), F32),
        in_specs=[VMEM] * 3,
        out_specs=VMEM,
        scratch_shapes=[pltpu.VMEM((512, 3 * 384), BF), pltpu.VMEM((144, 3 * 384), BF)],
        compiler_params=params(),
        name="conv",
    )(
        clip_features.reshape(4, 128, 384),
        enc_weight.transpose(0, 1, 2, 4, 3).reshape(432, 384),
        noise_field[0].transpose(0, 1, 3, 2),
    )
    slots = [conv] + [
        lax.ppermute(conv, "seq", [(i, (i + k) % peers) for i in range(peers)]) for k in range(1, peers)
    ]
    flow = flow_times[0].astype(F32) / TGRID
    flow_t = flow[1]
    feats = time_features(flow_t, flow_t - flow[0])
    feats = jnp.concatenate([feats, jnp.zeros((6, TFEAT), F32)], axis=0)
    gram = pl.pallas_call(
        gram_kernel,
        out_shape=shape((72, 128), F32),
        in_specs=[VMEM] * 3,
        out_specs=VMEM,
        compiler_params=params(),
        name="gram",
    )(embed_weight, time_weight, feats)
    got, slots[1], slots[2], slots[3] = lax.optimization_barrier((got, slots[1], slots[2], slots[3]))

    time_own = lax.dynamic_slice_in_dim(time_weight, own, depth, axis=1)
    time_own = time_own.reshape(2, 2, QUARTER, depth).transpose(1, 0, 2, 3).reshape(2, 2 * QUARTER, depth)
    second = pl.pallas_call(
        time_kernel,
        out_shape=shape((rows, 3 * width), BF),
        in_specs=[VMEM] * 5,
        out_specs=VMEM,
        compiler_params=params(),
        name="time_rows",
    )(got, time_own, gain_own, freqs, weight)
    got2 = lax.all_to_all(second.reshape(clips, 8, -1), "clip", 0, 0, tiled=True).reshape(rows, -1)
    got2, gram, *slots[4:] = lax.optimization_barrier((got2, gram, *slots[4:]))
    folded = pl.pallas_call(
        gather_rows_kernel,
        out_shape=shape((peers, 80, 3 * width), BF),
        in_specs=[VMEM],
        out_specs=VMEM,
        compiler_params=params(),
        name="folded_rows",
    )(got2)
    folded = lax.all_to_all(folded, "seq", 0, 0, tiled=True)

    tokens = 128 * peers
    aq, a_s, a_d, a_v = pl.pallas_call(
        feature_kernel,
        out_shape=[shape((256, 256), BF)] + [shape((256, tokens), BF)] * 3,
        in_specs=[SMEM, SMEM] + [ANY] * 8 + [VMEM],
        out_specs=[VMEM] * 4,
        scratch_shapes=[pltpu.VMEM((8, 192, 128), F32), pltpu.SemaphoreType.DMA((8,))],
        compiler_params=params(),
        name="features",
    )(at_seq[None], flow_t[None], *slots, gram)

    whole = lambda shp: pl.BlockSpec(shp, lambda i: (0, 0))
    heads = width // HD
    out, dout = pl.pallas_call(
        attention_kernel,
        grid=(peers,),
        out_shape=[shape((128, peers * width), BF)] * 2,
        in_specs=[
            pl.BlockSpec((1, 80, 3 * width), lambda i: (i, 0, 0)),
            whole((256, 256)),
            whole((256, tokens)),
            whole((256, tokens)),
            whole((256, tokens)),
        ],
        out_specs=[pl.BlockSpec((128, width), lambda i: (0, i))] * 2,
        scratch_shapes=[
            pltpu.VMEM((heads * 128, tokens), F32),
            pltpu.VMEM((heads * 128, tokens), F32),
            pltpu.VMEM((2 * heads * 128, tokens), BF),
            pltpu.VMEM((heads * 128, 128), F32),
        ],
        compiler_params=params(),
        name="attention",
    )(folded, aq, a_s, a_d, a_v)
    return (out[None], dout[None])


def solution(mesh):
    placed = (
        P("clip", None, "seq", None, None),
        P(),
        P("clip", None, "seq", None, None),
        P("clip", None),
        P(),
        P(),
        P(),
        P("clip", None, "seq"),
    )
    return jax.shard_map(
        local,
        mesh=mesh,
        in_specs=placed,
        out_specs=(P("clip", "seq", None), P("clip", "seq", None)),
        check_vma=False,
    )
```

```python
import jax
import jax.numpy as jnp
import numpy as np
from jax import lax
from jax.experimental import pallas as pl
from jax.experimental.pallas import tpu as pltpu
from jax.sharding import PartitionSpec as P

D = 5120
HD = 128
TFEAT = 256
TGRID = 1000
EPSILON = 1e-06
QUARTER = TFEAT // 4
F32 = jnp.float32
BF = jnp.bfloat16
HIGH = lax.Precision.HIGHEST
LOG2E = 1.4426950408889634
LN2 = 0.6931471805599453
VMEM = pl.BlockSpec(memory_space=pltpu.VMEM)
SMEM = pl.BlockSpec(memory_space=pltpu.SMEM)
ANY = pl.BlockSpec(memory_space=pl.ANY)
HBM = pl.BlockSpec(memory_space=pltpu.HBM)


def whole(shape):
    return pl.BlockSpec(shape, lambda i: (0,) * len(shape))


def params(limit=63):
    return pltpu.CompilerParams(vmem_limit_bytes=limit * 1024 * 1024)


def dot(a, b, dims=((1,), (0,)), precision=None):
    return lax.dot_general(a, b, (dims, ((), ())), preferred_element_type=F32, precision=precision)


def split(x):
    hi = x.astype(BF)
    return hi, (x - hi.astype(F32)).astype(BF)


def iota(shape, axis):
    return lax.broadcasted_iota(jnp.int32, shape, axis)


def fold_kernel(flow_ref, embed_ref, gain_ref, weight_ref, out_ref, e_ref, g_ref, w_ref, sems):
    rows = out_ref.shape[0]
    _, depth, width = weight_ref.shape
    window = e_ref.shape[1]
    at_clip = lax.axis_index("clip")
    odd = at_clip % 2
    base = pl.multiple_of(at_clip * depth - odd * 64, 128)
    copies = [
        pltpu.make_async_copy(embed_ref.at[:, pl.ds(base, window)], e_ref, sems.at[0]),
        pltpu.make_async_copy(gain_ref.at[:, pl.ds(base, window)], g_ref, sems.at[1]),
    ] + [pltpu.make_async_copy(weight_ref.at[i], w_ref.at[i], sems.at[2 + i]) for i in range(3)]
    for copy in copies:
        copy.start()
    lane = iota((rows, 128), 1)
    start, finish = flow_ref[0, 0], flow_ref[0, 1]
    coded = jnp.where(
        lane == 0,
        start // 256,
        jnp.where(lane == 1, start % 256, jnp.where(lane == 2, finish // 256, finish % 256)),
    )
    out_ref[:, 3 * width :] = coded.astype(F32).astype(BF)
    row, col = iota((rows, 64), 0), iota((rows, 64), 1)
    twice = jnp.where(col == (row // 8) * 4 + row % 4, 1.0, 0.0).astype(BF)
    copies[0].wait()
    copies[1].wait()
    scaled = dot(twice, e_ref[...]) * g_ref[...]
    scaled = jnp.where(odd == 1, scaled[:, 64 : 64 + depth], scaled[:, :depth])
    scaled_hi, scaled_lo = split(scaled)
    first = (iota((rows, 1), 0) // 4) % 2 == 0
    for i in range(3):
        copies[2 + i].wait()
        w = w_ref[i]
        total = dot(scaled_hi, w) + dot(scaled_lo, w)
        hi = total.astype(BF).astype(F32)
        out_ref[:, i * width : (i + 1) * width] = jnp.where(first, hi, total - hi).astype(BF)


def frequencies():
    k = iota((1, 128), 1) % QUARTER
    return 8.0 * jnp.exp(k.astype(F32) * np.float32(-np.log(100.0) / QUARTER))


def time_kernel(got_ref, time_ref, gain_ref, weight_ref, out_ref, r_ref, t_ref, g_ref, w_ref, sems):
    rows = out_ref.shape[0]
    groups = rows // 8
    _, depth, width = weight_ref.shape
    window = t_ref.shape[1]
    at_clip = lax.axis_index("clip")
    odd = at_clip % 2
    base = pl.multiple_of(at_clip * depth - odd * 64, 128)
    copies = [
        pltpu.make_async_copy(got_ref, r_ref, sems.at[0]),
        pltpu.make_async_copy(gain_ref.at[:, pl.ds(base, window)], g_ref, sems.at[1]),
        pltpu.make_async_copy(time_ref.at[:, pl.ds(base, window)], t_ref, sems.at[2]),
    ] + [pltpu.make_async_copy(weight_ref.at[i], w_ref.at[i], sems.at[3 + i]) for i in range(3)]
    for copy in copies:
        copy.start()
    freqs = frequencies()
    copies[0].wait()
    codes = r_ref[:, 3 * width :].astype(F32)
    start = (codes[:, 0:1] * 256.0 + codes[:, 1:2]) / TGRID
    finish = (codes[:, 2:3] * 256.0 + codes[:, 3:4]) / TGRID
    half = iota((rows, 128), 1) < QUARTER
    angle = freqs * jnp.where(half, finish, finish - start)
    sines, cosines = jnp.sin(angle), jnp.cos(angle)
    place = iota((rows, 1), 0) % 8
    is_value = (place == 4) | (place == 5)
    is_tangent = place >= 6
    first = jnp.where(is_value, sines, jnp.where(is_tangent, freqs * cosines, 0.0))
    second = jnp.where(is_value, cosines, jnp.where(is_tangent, -freqs * sines, 0.0))
    first_hi, first_lo = split(first)
    second_hi, second_lo = split(second)
    copies[1].wait()
    copies[2].wait()
    q = QUARTER
    t_first = jnp.concatenate([t_ref[0:q], t_ref[2 * q : 3 * q]], axis=0)
    t_second = jnp.concatenate([t_ref[q : 2 * q], t_ref[3 * q : 4 * q]], axis=0)
    tau = dot(first_hi, t_first) + dot(first_lo, t_first) + dot(second_hi, t_second) + dot(second_lo, t_second)
    tau = tau * g_ref[...]
    tau = jnp.where(odd == 1, tau[:, 64 : 64 + depth], tau[:, :depth])
    tau_hi, tau_lo = split(tau)
    keep_hi = place % 2 == 0
    for i in range(3):
        cols = slice(i * width, (i + 1) * width)
        summed = r_ref[:, cols].astype(F32).reshape(groups, 8, width).sum(axis=0)
        summed = summed + jnp.concatenate([summed[4:], summed[:4]], axis=0)
        copies[3 + i].wait()
        w = w_ref[i]
        part = dot(tau_hi, w) + dot(tau_lo, w)
        hi = part.astype(BF).astype(F32)
        part = jnp.where(keep_hi, hi, part - hi)
        mine = jnp.concatenate([summed] * groups, axis=0)
        out_ref[:, cols] = jnp.where(place < 4, mine, part).astype(BF)


def head_rows_kernel(got_ref, out_ref):
    rows = got_ref.shape[0]
    heads = out_ref.shape[2] // (2 * HD)
    row, col = iota((128, rows), 0), iota((128, rows), 1)
    patch = (row < 64) & (col == (row // 4) * 8 + row % 4)
    place = col % 8
    value = (row >= 64) & (row < 68) & ((place == 4) | (place == 5))
    tangent = (row >= 68) & (row < 72) & (place >= 6)
    pick = jnp.where(patch | value | tangent, 1.0, 0.0).astype(BF)
    total = dot(pick, got_ref[...])
    width = total.shape[1] // 3
    low_row = lambda r: (r == 67) | (r == 71)
    r, l = iota((80, HD), 0), iota((80, HD), 1)
    for h in range(heads):
        part = lambda i: total[:, i * width + h * HD : i * width + (h + 1) * HD]
        q_hi, q_lo = split(part(0)[:80])
        k_hi, k_lo = split(part(1))
        nt = ((1,), (1,))
        product = dot(q_hi, k_hi, nt) + dot(q_lo, k_hi, nt) + dot(q_hi, k_lo, nt)
        hi = product.astype(BF).astype(F32)
        lo = product - hi
        product = jnp.where(
            low_row(l), jnp.where(r < 64, lo, 0.0), jnp.where(low_row(r), lo, hi)
        ).astype(BF)
        v = part(2)[:80]
        v_hi = v.astype(BF).astype(F32)
        v = jnp.where(low_row(r), v - v_hi, v_hi).astype(BF)
        for i in range(out_ref.shape[0]):
            out_ref[i, :, h * HD : (h + 1) * HD] = product
            out_ref[i, :, (heads + h) * HD : (heads + h + 1) * HD] = v


def conv_kernel(x_hbm, w_hbm, noise_hbm, after_ref, out_ref, xp_ref, wt_ref, x_ref, w_ref, noise_ref, sems):
    copies = [
        pltpu.make_async_copy(x_hbm, x_ref, sems.at[0]),
        pltpu.make_async_copy(w_hbm, w_ref, sems.at[1]),
        pltpu.make_async_copy(noise_hbm, noise_ref, sems.at[2]),
    ]
    for copy in copies:
        copy.start()
    for copy in copies:
        copy.wait()
    chans = x_ref.shape[2]
    row, col = iota((128, 128), 0), iota((128, 128), 1)
    row_w = 2 * (row % 32) + (row // 32) % 2
    same = (row // 64) == (col // 64)
    for e in range(3):
        perm = jnp.where(same & (col % 64 == row_w + (e - 1)), 1.0, 0.0).astype(BF)
        for f in range(4):
            moved = dot(perm, x_ref[f]).astype(BF)
            for g in range(4):
                xp_ref[g * 128 + f * 32 : g * 128 + f * 32 + 32, e * chans : (e + 1) * chans] = moved[
                    g * 32 : g * 32 + 32
                ]
        for ab in range(9):
            tap = (ab * 3 + e) * 16
            wt_ref[ab * 16 : ab * 16 + 16, e * chans : (e + 1) * chans] = w_ref[tap : tap + 16, :]
    y = dot(wt_ref[...], xp_ref[...], ((1,), (1,)))
    lane = iota((16, 128), 1)

    def part(a, b, p, q):
        at = (a * 3 + b) * 16
        g = p * 2 + q
        return y[at : at + 16, g * 128 : (g + 1) * 128]

    def frames(of):
        one = jnp.where(lane >= 32, pltpu.roll(of(1), 32, 1), 0.0)
        two = jnp.where(lane >= 64, pltpu.roll(of(0), 64, 1), 0.0)
        return of(2) + one + two

    for q in range(2):
        own0 = frames(lambda a: part(a, 1, 0, q) + part(a, 2, 1, q))
        own1 = frames(lambda a: part(a, 0, 0, q) + part(a, 1, 1, q))
        down = frames(lambda a: part(a, 0, 1, q))
        up = frames(lambda a: part(a, 2, 0, q))
        out_ref[q * 16 : q * 16 + 16, :] = own0
        out_ref[32 + q * 16 : 48 + q * 16, :] = own1
        out_ref[64 + q * 16 : 80 + q * 16, :] = down
        out_ref[96 + q * 16 : 112 + q * 16, :] = up
    r2, c2 = iota((256, 256), 0), iota((256, 256), 1)
    spread = ((r2 // 64) == (c2 // 32) % 4) & (r2 % 64 == 2 * (c2 % 32) + c2 // 128)
    spread = jnp.where(spread, 1.0, 0.0)
    noise = jnp.concatenate(
        [jnp.concatenate([noise_ref[f, p] for f in range(4)], axis=1) for p in range(2)], axis=0
    )
    moved = dot(noise, spread, precision=HIGH)
    for p in range(2):
        for q in range(2):
            at = 128 + (p * 2 + q) * 16
            out_ref[at : at + 16, :] = moved[p * 16 : p * 16 + 16, q * 128 : (q + 1) * 128]


def gram_kernel(flow_ref, embed_hbm, time_hbm, after_ref, out_ref, embed_ref, time_ref, sems):
    copies = [
        pltpu.make_async_copy(time_hbm, time_ref, sems.at[0]),
        pltpu.make_async_copy(embed_hbm, embed_ref, sems.at[1]),
    ]
    for copy in copies:
        copy.start()
    start = flow_ref[0, 0].astype(F32) / TGRID
    finish = flow_ref[0, 1].astype(F32) / TGRID
    freqs = frequencies()
    angle = freqs * jnp.where(iota((8, 128), 1) < QUARTER, finish, finish - start)
    sines, cosines = jnp.sin(angle), jnp.cos(angle)
    row = iota((8, 128), 0)
    first = jnp.where(row == 0, sines, jnp.where(row == 1, freqs * cosines, 0.0))
    second = jnp.where(row == 0, cosines, jnp.where(row == 1, -freqs * sines, 0.0))
    q = QUARTER
    feats = jnp.concatenate([first[:, :q], second[:, :q], first[:, q:], second[:, q:]], axis=1)
    feat_hi, feat_lo = split(feats)
    feat_mid = (feats - feat_hi.astype(F32) - feat_lo.astype(F32)).astype(BF)
    feats = jnp.concatenate([feat_hi, feat_lo, feat_mid, jnp.zeros_like(feat_hi)], axis=0)
    for copy in copies:
        copy.wait()
    tau = dot(feats, time_ref[...])
    tau = tau[0:8] + tau[8:16] + tau[16:24]
    embed = embed_ref[...]
    out_ref[0:64, 0:64] = dot(embed, embed, ((1,), (1,)))
    tau_hi, tau_lo = split(tau)
    tau_mid = (tau - tau_hi.astype(F32) - tau_lo.astype(F32)).astype(BF)
    taus = jnp.concatenate([tau_hi, tau_lo, tau_mid, jnp.zeros_like(tau_hi)], axis=0)
    cross = dot(embed, taus, ((1,), (1,)))
    out_ref[0:64, 64:128] = jnp.concatenate(
        [cross[:, 0:8] + cross[:, 8:16] + cross[:, 16:24], jnp.zeros((64, 56), F32)], axis=1
    )
    out_ref[64:72, :] = jnp.sum(tau * tau[0:1], axis=1, keepdims=True) + jnp.zeros((8, 128), F32)


def feature_kernel(flow_ref, *refs):
    arrived = refs[:8]
    gram_ref, _, aq_ref, s_ref, d_ref, v_ref, slots, sems = refs[8:]
    copies = [pltpu.make_async_copy(arrived[k], slots.at[k], sems.at[k]) for k in range(8)]
    for copy in copies:
        copy.start()
    for copy in copies:
        copy.wait()
    here = lax.axis_index("seq")
    flow_t = flow_ref[0, 1].astype(F32) / TGRID
    patches, tangents = [], []
    for k in range(8):
        owner = lax.rem(here - k + 8, 8)
        before = slots[(k + 1) % 8, 64:96, :]
        after = slots[(k + 7) % 8, 96:128, :]
        halo = jnp.concatenate(
            [jnp.where(owner > 0, before, 0.0), jnp.where(owner < 7, after, 0.0)], axis=0
        )
        latent = slots[k, 0:64, :] + halo
        noise = slots[k, 128:192, :]
        patches.append((1.0 - flow_t) * latent + flow_t * noise)
        tangents.append(noise - latent)
    p = jnp.concatenate(patches, axis=1)
    dp = jnp.concatenate(tangents, axis=1)
    gp = dot(gram_ref[0:64, 0:64], p, precision=HIGH)
    e_tau, e_dtau = gram_ref[0:64, 64:65], gram_ref[0:64, 65:66]
    mean_sq = jnp.sum(p * (gp + 2.0 * e_tau), axis=0, keepdims=True) + gram_ref[64:65, 0:1]
    mean_sq = jnp.maximum(mean_sq * (1.0 / D), 0.0)
    mixed = jnp.sum(gp * dp + p * e_dtau + dp * e_tau, axis=0, keepdims=True) + gram_ref[65:66, 0:1]
    s = lax.rsqrt(mean_sq + EPSILON)
    c = -(s * s * s) * (mixed * (1.0 / D))
    a = p * s
    da = dp * s + p * c
    up = lambda x: x.astype(BF).astype(F32)
    a_hi, da_hi = up(a), up(da)
    a_lo, da_lo = a - a_hi, da - da_hi
    s_hi, c_hi = up(s), up(c)
    s_lo, c_lo = s - s_hi, c - c_hi
    tokens = p.shape[1]
    r = iota((8, tokens), 0)

    def coefs(high, low, kind):
        if kind == 0:
            return jnp.where((r % 4 == 0) | (r % 4 == 3), high, jnp.where(r % 4 == 1, low, 0.0))
        return jnp.where(r % 4 == 2, low, high)

    def misc(kind):
        plain = jnp.where(r < 4, coefs(s_hi, s_lo, kind), 0.0)
        tangent = jnp.where(r < 4, coefs(c_hi, c_lo, kind), coefs(s_hi, s_lo, kind))
        return plain, tangent

    zeros = lambda n: jnp.zeros((n, tokens), F32)
    cat = lambda xs: jnp.concatenate(xs, axis=0)
    m_s, m_d = misc(1)
    v_s, v_d = misc(0)
    s_ref[...] = cat([a_hi, a_hi, a_lo, m_s, zeros(56)]).astype(BF)
    d_ref[...] = cat([a_hi, da_hi, a_hi, m_s, zeros(8), m_d, zeros(40)]).astype(BF)
    v_ref[...] = cat([a_hi, a_hi, da_hi, v_s, v_d, v_s, v_d, zeros(32)]).astype(BF)
    own = lambda x: x[:, :128]
    z = jnp.zeros((120, 128), F32)
    aq_ref[0:128, :] = cat([own(a_hi), own(a_lo), own(v_s), z]).T.astype(BF)
    aq_ref[128:256, :] = cat([own(da_hi), own(da_lo), own(v_d), z]).T.astype(BF)


def attention_kernel(n_ref, aq_ref, as_ref, ad_ref, av_ref, out_ref, dout_ref, s_ref, d_ref, et_ref, l_ref):
    n = n_ref[0]
    m, misc = n[:64], n[64:80]
    width = n.shape[1] // 2
    heads = width // HD
    rows = heads * 128
    zero = lambda r, c=HD: jnp.zeros((r, c), BF)
    lane = iota((128, 256), 1)
    low_s = ((lane >= 64) & (lane < 128)) | (lane == 193) | (lane == 197)
    low_d = ((lane >= 128) & (lane < 192)) | (lane == 193) | (lane == 209) | (lane == 213)
    from_q = ((lane >= 64) & (lane < 128)) | (lane >= 200)
    lane = iota((256, 256), 1)
    low_r = ((lane >= 64) & (lane < 128)) | (lane >= 208)
    xs, xd = [], []
    narrow = iota((80, HD), 1)
    for h in range(heads):
        b = n[:, h * HD : (h + 1) * HD].astype(F32)
        twice = jnp.where(narrow < 64, b, pltpu.roll(b, 64, 1))
        again = jnp.where(narrow < 80, b, pltpu.roll(b, 16, 1))
        b = jnp.concatenate([twice, again], axis=1).astype(BF)
        b = jnp.concatenate([b[:64], b[:64], b[64:], jnp.zeros((112, 256), BF)], axis=0)
        absorbed = dot(aq_ref[...], b) * (LOG2E * HD ** -0.5)
        hi = absorbed.astype(BF).astype(F32)
        lo = absorbed - hi
        xs.append(jnp.where(low_s, lo[:128], hi[:128]).astype(BF))
        low = jnp.where(from_q, lo[:128], lo[128:])
        high = jnp.where(from_q, hi[:128], hi[128:])
        xd.append(jnp.where(low_d, low, high).astype(BF))
    s_ref[...] = dot(jnp.concatenate(xs, axis=0), as_ref[...])
    d_ref[...] = dot(jnp.concatenate(xd, axis=0), ad_ref[...])
    for i in range(rows // 16):
        r = slice(i * 16, (i + 1) * 16)
        s = s_ref[r]
        e = jnp.exp2(s - jnp.max(s, axis=1, keepdims=True))
        d = d_ref[r]
        inv = 1.0 / jnp.sum(e, axis=1, keepdims=True)
        mean = jnp.sum(e * d, axis=1, keepdims=True) * inv
        et_ref[r] = e.astype(BF)
        et_ref[rows + i * 16 : rows + (i + 1) * 16] = (e * (d - mean)).astype(BF)
        l_ref[r] = jnp.broadcast_to(inv, (16, 128))
    mixes = dot(et_ref[...], av_ref[...], ((1,), (1,)))
    for h in range(heads):
        cols = slice(width + h * HD, width + (h + 1) * HD)
        mv, miscv = m[:, cols], misc[:, cols]
        inv = l_ref[h * 128 : (h + 1) * 128, 0:1]
        mix = mixes[h * 128 : (h + 1) * 128] * inv
        mix_t = mixes[rows + h * 128 : rows + (h + 1) * 128] * (inv * LN2)
        nx = jnp.concatenate([mv, mv, zero(64), miscv, miscv, zero(32)], axis=0)
        late = jnp.concatenate([zero(8), miscv[:8]], axis=0)
        ny = jnp.concatenate([zero(128), mv, late, late, zero(32)], axis=0)
        both = jnp.concatenate([mix, mix_t], axis=0)
        hi = both.astype(BF).astype(F32)
        both = jnp.where(low_r, both - hi, hi).astype(BF)
        z = dot(both, jnp.concatenate([nx, ny], axis=1))
        out_ref[:, h * HD : (h + 1) * HD] = z[:128, :HD].astype(BF)
        dout_ref[:, h * HD : (h + 1) * HD] = (z[128:, :HD] + z[:128, HD:]).astype(BF)


def local(clip_features, enc_weight, noise_field, flow_times, embed_weight, time_weight, norm_gain, qkv_weight):
    clips = lax.axis_size("clip")
    peers = lax.axis_size("seq")
    depth = qkv_weight.shape[0]
    width = qkv_weight.shape[2]
    weight = qkv_weight.transpose(1, 0, 2)
    gain = norm_gain[None]
    shape = jax.ShapeDtypeStruct
    rows = 8 * clips
    heads = width // HD
    tokens = 128 * peers
    window = depth + 64

    partial = pl.pallas_call(
        fold_kernel,
        grid=(1,),
        out_shape=shape((rows, 3 * width + 128), BF),
        in_specs=[SMEM, HBM, HBM, HBM],
        out_specs=whole((rows, 3 * width + 128)),
        scratch_shapes=[
            pltpu.VMEM((64, window), BF),
            pltpu.VMEM((1, window), F32),
            pltpu.VMEM((3, depth, width), BF),
            pltpu.SemaphoreType.DMA((5,)),
        ],
        compiler_params=params(),
        name="fold",
    )(flow_times, embed_weight, gain, weight)
    got = lax.all_to_all(partial.reshape(clips, 8, -1), "clip", 0, 0, tiled=True).reshape(rows, -1)

    conv = pl.pallas_call(
        conv_kernel,
        grid=(1,),
        out_shape=shape((192, 128), F32),
        in_specs=[HBM, HBM, HBM, ANY],
        out_specs=whole((192, 128)),
        scratch_shapes=[
            pltpu.VMEM((512, 3 * 384), BF),
            pltpu.VMEM((144, 3 * 384), BF),
            pltpu.VMEM((4, 128, 384), BF),
            pltpu.VMEM((432, 384), BF),
            pltpu.VMEM((4, 2, 16, 64), F32),
            pltpu.SemaphoreType.DMA((3,)),
        ],
        compiler_params=params(),
        name="conv",
    )(
        clip_features.reshape(4, 128, 384),
        enc_weight.transpose(0, 1, 2, 4, 3).reshape(432, 384),
        noise_field[0].transpose(0, 1, 3, 2),
        partial,
    )

    def shift(value, k):
        return lax.ppermute(value, "seq", [(i, (i + k) % peers) for i in range(peers)])

    slots = [shift(conv, k) for k in (1, 2, 3)]
    got, *slots = lax.optimization_barrier((got, *slots))

    second = pl.pallas_call(
        time_kernel,
        grid=(1,),
        out_shape=shape((rows, 3 * width), BF),
        in_specs=[ANY, HBM, HBM, HBM],
        out_specs=whole((rows, 3 * width)),
        scratch_shapes=[
            pltpu.VMEM((rows, 3 * width + 128), BF),
            pltpu.VMEM((TFEAT, window), BF),
            pltpu.VMEM((1, window), F32),
            pltpu.VMEM((3, depth, width), BF),
            pltpu.SemaphoreType.DMA((6,)),
        ],
        compiler_params=params(),
        name="time_rows",
    )(got, time_weight, gain, weight)
    second, conv = lax.optimization_barrier((second, conv))
    got = lax.all_to_all(second.reshape(clips, 8, -1), "clip", 0, 0, tiled=True).reshape(rows, -1)

    slots = [conv] + slots + [shift(conv, k) for k in range(4, peers)]
    gram = pl.pallas_call(
        gram_kernel,
        grid=(1,),
        out_shape=shape((72, 128), F32),
        in_specs=[SMEM, HBM, HBM, ANY],
        out_specs=whole((72, 128)),
        scratch_shapes=[
            pltpu.VMEM(embed_weight.shape, BF),
            pltpu.VMEM(time_weight.shape, BF),
            pltpu.SemaphoreType.DMA((2,)),
        ],
        compiler_params=params(),
        name="gram",
    )(flow_times, embed_weight, time_weight, second)
    got, gram, *slots = lax.optimization_barrier((got, gram, *slots))

    folded = pl.pallas_call(
        head_rows_kernel,
        grid=(1,),
        out_shape=shape((peers, 80, 2 * width), BF),
        in_specs=[whole((rows, 3 * width))],
        out_specs=whole((peers, 80, 2 * width)),
        compiler_params=params(),
        name="head_rows",
    )(got)
    every = lax.all_to_all(folded, "seq", 0, 0, tiled=True)

    forms = [(256, 256)] + [(256, tokens)] * 3
    aq, a_s, a_d, a_v = pl.pallas_call(
        feature_kernel,
        grid=(1,),
        out_shape=[shape(f, BF) for f in forms],
        in_specs=[SMEM] + [ANY] * 8 + [whole((72, 128)), ANY],
        out_specs=[whole(f) for f in forms],
        scratch_shapes=[pltpu.VMEM((8, 192, 128), F32), pltpu.SemaphoreType.DMA((8,))],
        compiler_params=params(),
        name="features",
    )(flow_times, *slots, gram, folded)

    out, dout = pl.pallas_call(
        attention_kernel,
        grid=(peers,),
        out_shape=[shape((128, peers * width), BF)] * 2,
        in_specs=[pl.BlockSpec((1, 80, 2 * width), lambda i: (i, 0, 0))] + [whole(f) for f in forms],
        out_specs=[pl.BlockSpec((128, width), lambda i: (0, i))] * 2,
        scratch_shapes=[
            pltpu.VMEM((heads * 128, tokens), F32),
            pltpu.VMEM((heads * 128, tokens), F32),
            pltpu.VMEM((2 * heads * 128, tokens), BF),
            pltpu.VMEM((heads * 128, 128), F32),
        ],
        compiler_params=params(),
        name="attention",
    )(every, aq, a_s, a_d, a_v)
    return (out[None], dout[None])


def solution(mesh):
    placed = (
        P("clip", None, "seq", None, None),
        P(),
        P("clip", None, "seq", None, None),
        P("clip", None),
        P(),
        P(),
        P(),
        P("clip", None, "seq"),
    )
    return jax.shard_map(
        local,
        mesh=mesh,
        in_specs=placed,
        out_specs=(P("clip", "seq", None), P("clip", "seq", None)),
        check_vma=False,
    )
```

```python
import jax
import jax.numpy as jnp
import numpy as np
from jax import lax
from jax.experimental import pallas as pl
from jax.experimental.pallas import tpu as pltpu
from jax.sharding import PartitionSpec as P

D = 5120
HD = 128
TFEAT = 256
TGRID = 1000
EPSILON = 1e-06
QUARTER = TFEAT // 4
F32 = jnp.float32
BF = jnp.bfloat16
HIGH = lax.Precision.HIGHEST
LOG2E = 1.4426950408889634
LN2 = 0.6931471805599453
VMEM = pl.BlockSpec(memory_space=pltpu.VMEM)
SMEM = pl.BlockSpec(memory_space=pltpu.SMEM)
ANY = pl.BlockSpec(memory_space=pl.ANY)
HBM = pl.BlockSpec(memory_space=pltpu.HBM)


def whole(shape):
    return pl.BlockSpec(shape, lambda i: (0,) * len(shape))


def params(limit=63):
    return pltpu.CompilerParams(vmem_limit_bytes=limit * 1024 * 1024)


def dot(a, b, dims=((1,), (0,)), precision=None):
    return lax.dot_general(a, b, (dims, ((), ())), preferred_element_type=F32, precision=precision)


def split(x):
    hi = x.astype(BF)
    return hi, (x - hi.astype(F32)).astype(BF)


def iota(shape, axis):
    return lax.broadcasted_iota(jnp.int32, shape, axis)


def fold_kernel(flow_ref, embed_ref, gain_ref, weight_ref, out_ref, e_ref, g_ref, w_ref, sems):
    rows = out_ref.shape[0]
    _, depth, width = weight_ref.shape
    window = e_ref.shape[1]
    at_clip = lax.axis_index("clip")
    odd = at_clip % 2
    base = pl.multiple_of(at_clip * depth - odd * 64, 128)
    copies = [
        pltpu.make_async_copy(embed_ref.at[:, pl.ds(base, window)], e_ref, sems.at[0]),
        pltpu.make_async_copy(gain_ref.at[:, pl.ds(base, window)], g_ref, sems.at[1]),
    ] + [pltpu.make_async_copy(weight_ref.at[i], w_ref.at[i], sems.at[2 + i]) for i in range(3)]
    for copy in copies:
        copy.start()
    lane = iota((rows, 128), 1)
    start, finish = flow_ref[0, 0], flow_ref[0, 1]
    coded = jnp.where(
        lane == 0,
        start // 256,
        jnp.where(lane == 1, start % 256, jnp.where(lane == 2, finish // 256, finish % 256)),
    )
    out_ref[:, 3 * width :] = coded.astype(F32).astype(BF)
    row, col = iota((rows, 64), 0), iota((rows, 64), 1)
    twice = jnp.where(col == (row // 8) * 4 + row % 4, 1.0, 0.0).astype(BF)
    copies[0].wait()
    copies[1].wait()
    scaled = dot(twice, e_ref[...]) * g_ref[...]
    scaled = jnp.where(odd == 1, scaled[:, 64 : 64 + depth], scaled[:, :depth])
    scaled_hi, scaled_lo = split(scaled)
    first = (iota((rows, 1), 0) // 4) % 2 == 0
    for i in range(3):
        copies[2 + i].wait()
        w = w_ref[i]
        total = dot(scaled_hi, w) + dot(scaled_lo, w)
        hi = total.astype(BF).astype(F32)
        out_ref[:, i * width : (i + 1) * width] = jnp.where(first, hi, total - hi).astype(BF)


def frequencies():
    k = iota((1, 128), 1) % QUARTER
    return 8.0 * jnp.exp(k.astype(F32) * np.float32(-np.log(100.0) / QUARTER))


def time_kernel(got_ref, time_ref, gain_ref, weight_ref, out_ref, r_ref, t_ref, g_ref, w_ref, sems):
    rows = out_ref.shape[0]
    groups = rows // 8
    _, depth, width = weight_ref.shape
    window = t_ref.shape[1]
    at_clip = lax.axis_index("clip")
    odd = at_clip % 2
    base = pl.multiple_of(at_clip * depth - odd * 64, 128)
    copies = [
        pltpu.make_async_copy(got_ref, r_ref, sems.at[0]),
        pltpu.make_async_copy(gain_ref.at[:, pl.ds(base, window)], g_ref, sems.at[1]),
        pltpu.make_async_copy(time_ref.at[:, pl.ds(base, window)], t_ref, sems.at[2]),
    ] + [pltpu.make_async_copy(weight_ref.at[i], w_ref.at[i], sems.at[3 + i]) for i in range(3)]
    for copy in copies:
        copy.start()
    freqs = frequencies()
    copies[0].wait()
    codes = r_ref[:, 3 * width :].astype(F32)
    start = (codes[:, 0:1] * 256.0 + codes[:, 1:2]) / TGRID
    finish = (codes[:, 2:3] * 256.0 + codes[:, 3:4]) / TGRID
    half = iota((rows, 128), 1) < QUARTER
    angle = freqs * jnp.where(half, finish, finish - start)
    sines, cosines = jnp.sin(angle), jnp.cos(angle)
    place = iota((rows, 1), 0) % 8
    is_value = (place == 4) | (place == 5)
    is_tangent = place >= 6
    first = jnp.where(is_value, sines, jnp.where(is_tangent, freqs * cosines, 0.0))
    second = jnp.where(is_value, cosines, jnp.where(is_tangent, -freqs * sines, 0.0))
    first_hi, first_lo = split(first)
    second_hi, second_lo = split(second)
    copies[1].wait()
    copies[2].wait()
    q = QUARTER
    t_first = jnp.concatenate([t_ref[0:q], t_ref[2 * q : 3 * q]], axis=0)
    t_second = jnp.concatenate([t_ref[q : 2 * q], t_ref[3 * q : 4 * q]], axis=0)
    tau = dot(first_hi, t_first) + dot(first_lo, t_first) + dot(second_hi, t_second) + dot(second_lo, t_second)
    tau = tau * g_ref[...]
    tau = jnp.where(odd == 1, tau[:, 64 : 64 + depth], tau[:, :depth])
    tau_hi, tau_lo = split(tau)
    keep_hi = place % 2 == 0
    for i in range(3):
        cols = slice(i * width, (i + 1) * width)
        summed = r_ref[:, cols].astype(F32).reshape(groups, 8, width).sum(axis=0)
        summed = summed + jnp.concatenate([summed[4:], summed[:4]], axis=0)
        copies[3 + i].wait()
        w = w_ref[i]
        part = dot(tau_hi, w) + dot(tau_lo, w)
        hi = part.astype(BF).astype(F32)
        part = jnp.where(keep_hi, hi, part - hi)
        mine = jnp.concatenate([summed] * groups, axis=0)
        out_ref[:, cols] = jnp.where(place < 4, mine, part).astype(BF)


def head_rows_kernel(got_ref, feat_ref, out_ref):
    rows = got_ref.shape[0]
    heads = 3
    row, col = iota((128, rows), 0), iota((128, rows), 1)
    patch = (row < 64) & (col == (row // 4) * 8 + row % 4)
    place = col % 8
    value = (row >= 64) & (row < 68) & ((place == 4) | (place == 5))
    tangent = (row >= 68) & (row < 72) & (place >= 6)
    pick = jnp.where(patch | value | tangent, 1.0, 0.0).astype(BF)
    total = dot(pick, got_ref[...])
    width = total.shape[1] // 3
    low_row = lambda r: (r == 67) | (r == 71)
    r, l = iota((80, HD), 0), iota((80, HD), 1)
    products, values = [], []
    for h in range(heads):
        part = lambda i: total[:, i * width + h * HD : i * width + (h + 1) * HD]
        q_hi, q_lo = split(part(0)[:80])
        k_hi, k_lo = split(part(1))
        nt = ((1,), (1,))
        product = dot(q_hi, k_hi, nt) + dot(q_lo, k_hi, nt) + dot(q_hi, k_lo, nt)
        hi = product.astype(BF).astype(F32)
        lo = product - hi
        product = jnp.where(low_row(l), jnp.where(r < 64, lo, 0.0), jnp.where(low_row(r), lo, hi))
        products.append(product)
        v = part(2)[:80]
        v_hi = v.astype(BF).astype(F32)
        values.append(jnp.where(low_row(r), v - v_hi, v_hi).astype(BF))
    one, two, three = products
    first = jnp.where(l < 64, one, pltpu.roll(two, 64, 1))
    second = jnp.where(
        l < 64,
        three,
        jnp.where(
            l < 72,
            one,
            jnp.where(l < 80, pltpu.roll(two, 8, 1), jnp.where(l < 88, pltpu.roll(three, 16, 1), 0.0)),
        ),
    )
    blocks = [first.astype(BF), second.astype(BF)] + values
    for i in range(out_ref.shape[0]):
        for b, block in enumerate(blocks):
            out_ref[i, b * 80 : (b + 1) * 80, :] = block
        out_ref[i, 400:576, :] = feat_ref[...]


def conv_kernel(x_hbm, w_hbm, noise_hbm, after_ref, out_ref, down_ref, up_ref, xp_ref, wt_ref, x_ref, w_ref, noise_ref, sems):
    copies = [
        pltpu.make_async_copy(x_hbm, x_ref, sems.at[0]),
        pltpu.make_async_copy(w_hbm, w_ref, sems.at[1]),
        pltpu.make_async_copy(noise_hbm, noise_ref, sems.at[2]),
    ]
    for copy in copies:
        copy.start()
    for copy in copies:
        copy.wait()
    chans = x_ref.shape[2]
    row, col = iota((128, 128), 0), iota((128, 128), 1)
    row_w = 2 * (row % 32) + (row // 32) % 2
    same = (row // 64) == (col // 64)
    for e in range(3):
        perm = jnp.where(same & (col % 64 == row_w + (e - 1)), 1.0, 0.0).astype(BF)
        for f in range(4):
            moved = dot(perm, x_ref[f]).astype(BF)
            for g in range(4):
                xp_ref[g * 128 + f * 32 : g * 128 + f * 32 + 32, e * chans : (e + 1) * chans] = moved[
                    g * 32 : g * 32 + 32
                ]
        for ab in range(9):
            tap = (ab * 3 + e) * 16
            wt_ref[ab * 16 : ab * 16 + 16, e * chans : (e + 1) * chans] = w_ref[tap : tap + 16, :]
    y = dot(wt_ref[...], xp_ref[...], ((1,), (1,)))
    lane = iota((16, 128), 1)

    def part(a, b, p, q):
        at = (a * 3 + b) * 16
        g = p * 2 + q
        return y[at : at + 16, g * 128 : (g + 1) * 128]

    def frames(of):
        one = jnp.where(lane >= 32, pltpu.roll(of(1), 32, 1), 0.0)
        two = jnp.where(lane >= 64, pltpu.roll(of(0), 64, 1), 0.0)
        return of(2) + one + two

    for q in range(2):
        own0 = frames(lambda a: part(a, 1, 0, q) + part(a, 2, 1, q))
        own1 = frames(lambda a: part(a, 0, 0, q) + part(a, 1, 1, q))
        down = frames(lambda a: part(a, 0, 1, q))
        up = frames(lambda a: part(a, 2, 0, q))
        out_ref[q * 16 : q * 16 + 16, :] = own0
        out_ref[32 + q * 16 : 48 + q * 16, :] = own1
        down_ref[q * 16 : q * 16 + 16, :] = down
        up_ref[q * 16 : q * 16 + 16, :] = up
    r2, c2 = iota((256, 256), 0), iota((256, 256), 1)
    spread = ((r2 // 64) == (c2 // 32) % 4) & (r2 % 64 == 2 * (c2 % 32) + c2 // 128)
    spread = jnp.where(spread, 1.0, 0.0)
    noise = jnp.concatenate(
        [jnp.concatenate([noise_ref[f, p] for f in range(4)], axis=1) for p in range(2)], axis=0
    )
    moved = dot(noise, spread, precision=HIGH)
    for p in range(2):
        for q in range(2):
            at = 64 + (p * 2 + q) * 16
            out_ref[at : at + 16, :] = moved[p * 16 : p * 16 + 16, q * 128 : (q + 1) * 128]


def feature_kernel(
    flow_ref, embed_hbm, time_hbm, base_ref, above_ref, below_ref, after_ref, feat_ref, aq_ref, embed_ref, time_ref, sems
):
    copies = [
        pltpu.make_async_copy(time_hbm, time_ref, sems.at[0]),
        pltpu.make_async_copy(embed_hbm, embed_ref, sems.at[1]),
    ]
    for copy in copies:
        copy.start()
    start = flow_ref[0, 0].astype(F32) / TGRID
    finish = flow_ref[0, 1].astype(F32) / TGRID
    freqs = frequencies()
    angle = freqs * jnp.where(iota((8, 128), 1) < QUARTER, finish, finish - start)
    sines, cosines = jnp.sin(angle), jnp.cos(angle)
    row = iota((8, 128), 0)
    first = jnp.where(row == 0, sines, jnp.where(row == 1, freqs * cosines, 0.0))
    second = jnp.where(row == 0, cosines, jnp.where(row == 1, -freqs * sines, 0.0))
    q = QUARTER
    feats = jnp.concatenate([first[:, :q], second[:, :q], first[:, q:], second[:, q:]], axis=1)

    def three(x):
        hi, mid = split(x)
        low = (x - hi.astype(F32) - mid.astype(F32)).astype(BF)
        return jnp.concatenate([hi, mid, low, jnp.zeros_like(hi)], axis=0)

    latent = base_ref[0:64, :] + jnp.concatenate([above_ref[...], below_ref[...]], axis=0)
    noise = base_ref[64:128, :]
    p = (1.0 - finish) * latent + finish * noise
    dp = noise - latent
    for copy in copies:
        copy.wait()
    tau = dot(three(feats), time_ref[...])
    tau = tau[0:8] + tau[8:16] + tau[16:24]
    embed = embed_ref[...]
    gram = dot(embed, embed, ((1,), (1,)))
    cross = dot(embed, three(tau), ((1,), (1,)))
    cross = cross[:, 0:8] + cross[:, 8:16] + cross[:, 16:24]
    square = jnp.sum(tau * tau[0:1], axis=1, keepdims=True)
    gp = dot(gram, p, precision=HIGH)
    e_tau, e_dtau = cross[:, 0:1], cross[:, 1:2]
    mean_sq = jnp.sum(p * (gp + 2.0 * e_tau), axis=0, keepdims=True) + square[0:1]
    mean_sq = jnp.maximum(mean_sq * (1.0 / D), 0.0)
    mixed = jnp.sum(gp * dp + p * e_dtau + dp * e_tau, axis=0, keepdims=True) + square[1:2]
    s = lax.rsqrt(mean_sq + EPSILON)
    c = -(s * s * s) * (mixed * (1.0 / D))
    a = p * s
    da = dp * s + p * c
    up = lambda x: x.astype(BF).astype(F32)
    a_hi, da_hi = up(a), up(da)
    s_hi, c_hi = up(s), up(c)
    s_lo, c_lo = s - s_hi, c - c_hi
    r = iota((8, p.shape[1]), 0)

    def coefs(high, low, kind):
        if kind == 0:
            return jnp.where((r % 4 == 0) | (r % 4 == 3), high, jnp.where(r % 4 == 1, low, 0.0))
        return jnp.where(r % 4 == 2, low, high)

    def misc(kind):
        plain = jnp.where(r < 4, coefs(s_hi, s_lo, kind), 0.0)
        tangent = jnp.where(r < 4, coefs(c_hi, c_lo, kind), coefs(s_hi, s_lo, kind))
        return plain, tangent

    cat = lambda xs: jnp.concatenate(xs, axis=0)
    zero = jnp.zeros((8, p.shape[1]), F32)
    m_s, m_d = misc(1)
    v_s, v_d = misc(0)
    feat_ref[...] = cat([a_hi, da_hi, m_s, zero, m_d, zero, v_s, v_d]).astype(BF)
    z = jnp.zeros((120, 128), F32)
    aq_ref[0:128, :] = cat([a_hi, a - a_hi, v_s, z]).T.astype(BF)
    aq_ref[128:256, :] = cat([da_hi, da - da_hi, v_d, z]).T.astype(BF)


def attention_kernel(
    n_ref, every_ref, aq_ref, out_ref, dout_ref, f_ref, as_ref, ad_ref, av_ref, s_ref, d_ref, et_ref, l_ref, sems
):
    peers = f_ref.shape[0]

    @pl.when(pl.program_id(0) == 0)
    def _():
        copies = [
            pltpu.make_async_copy(every_ref.at[i, 400:576], f_ref.at[i], sems.at[i]) for i in range(peers)
        ]
        for copy in copies:
            copy.start()
        for i, copy in enumerate(copies):
            copy.wait()
            cols = slice(i * 128, (i + 1) * 128)
            a, da = f_ref[i, 0:64], f_ref[i, 64:128]
            as_ref[:, cols] = jnp.concatenate(
                [a, a, jnp.zeros((64, 128), BF), f_ref[i, 128:144], jnp.zeros((48, 128), BF)], axis=0
            )
            ad_ref[:, cols] = jnp.concatenate([a, da, a, f_ref[i, 128:160], jnp.zeros((32, 128), BF)], axis=0)
            av_ref[:, cols] = jnp.concatenate(
                [a, a, da, f_ref[i, 160:176], f_ref[i, 160:176], jnp.zeros((32, 128), BF)], axis=0
            )

    heads = 3
    rows = heads * 128
    zero = lambda r, c=HD: jnp.zeros((r, c), BF)
    lane = iota((128, 256), 1)
    low_s = ((lane >= 64) & (lane < 128)) | (lane == 193) | (lane == 197)
    low_d = ((lane >= 128) & (lane < 192)) | (lane == 193) | (lane == 209) | (lane == 213)
    from_q = ((lane >= 64) & (lane < 128)) | (lane >= 200)
    lane = iota((256, 256), 1)
    low_r = ((lane >= 64) & (lane < 128)) | (lane >= 208)
    xs, xd = [], []
    l = iota((80, HD), 1)
    first, second = n_ref[0, 0:80].astype(F32), n_ref[0, 80:160].astype(F32)
    for h in range(heads):
        block = (first, pltpu.roll(first, 64, 1), second)[h]
        swapped = (pltpu.roll(first, 64, 1), first, pltpu.roll(second, 64, 1))[h]
        again = jnp.where(
            l < 64,
            block,
            jnp.where(
                l < 72,
                pltpu.roll(second, (HD - 8 * h) % HD, 1) if h else second,
                jnp.where((l >= 80) & (l < 88), pltpu.roll(second, 16 - 8 * h, 1) if h < 2 else second, 0.0),
            ),
        )
        b = jnp.concatenate([jnp.where(l < 64, block, swapped), again], axis=1).astype(BF)
        b = jnp.concatenate([b[:64], b[:64], b[64:], jnp.zeros((112, 256), BF)], axis=0)
        absorbed = dot(aq_ref[...], b) * (LOG2E * HD ** -0.5)
        hi = absorbed.astype(BF).astype(F32)
        lo = absorbed - hi
        xs.append(jnp.where(low_s, lo[:128], hi[:128]).astype(BF))
        low = jnp.where(from_q, lo[:128], lo[128:])
        high = jnp.where(from_q, hi[:128], hi[128:])
        xd.append(jnp.where(low_d, low, high).astype(BF))
    s_ref[...] = dot(jnp.concatenate(xs, axis=0), as_ref[...])
    d_ref[...] = dot(jnp.concatenate(xd, axis=0), ad_ref[...])
    for i in range(rows // 16):
        r = slice(i * 16, (i + 1) * 16)
        s = s_ref[r]
        e = jnp.exp2(s - jnp.max(s, axis=1, keepdims=True))
        d = d_ref[r]
        inv = 1.0 / jnp.sum(e, axis=1, keepdims=True)
        mean = jnp.sum(e * d, axis=1, keepdims=True) * inv
        et_ref[r] = e.astype(BF)
        et_ref[rows + i * 16 : rows + (i + 1) * 16] = (e * (d - mean)).astype(BF)
        l_ref[r] = jnp.broadcast_to(inv, (16, 128))
    mixes = dot(et_ref[...], av_ref[...], ((1,), (1,)))
    for h in range(heads):
        at = 160 + h * 80
        mv, miscv = n_ref[0, at : at + 64], n_ref[0, at + 64 : at + 80]
        inv = l_ref[h * 128 : (h + 1) * 128, 0:1]
        mix = mixes[h * 128 : (h + 1) * 128] * inv
        mix_t = mixes[rows + h * 128 : rows + (h + 1) * 128] * (inv * LN2)
        nx = jnp.concatenate([mv, mv, zero(64), miscv, miscv, zero(32)], axis=0)
        late = jnp.concatenate([zero(8), miscv[:8]], axis=0)
        ny = jnp.concatenate([zero(128), mv, late, late, zero(32)], axis=0)
        both = jnp.concatenate([mix, mix_t], axis=0)
        hi = both.astype(BF).astype(F32)
        both = jnp.where(low_r, both - hi, hi).astype(BF)
        z = dot(both, jnp.concatenate([nx, ny], axis=1))
        out_ref[:, h * HD : (h + 1) * HD] = z[:128, :HD].astype(BF)
        dout_ref[:, h * HD : (h + 1) * HD] = (z[128:, :HD] + z[:128, HD:]).astype(BF)


def local(clip_features, enc_weight, noise_field, flow_times, embed_weight, time_weight, norm_gain, qkv_weight):
    clips = lax.axis_size("clip")
    peers = lax.axis_size("seq")
    depth = qkv_weight.shape[0]
    width = qkv_weight.shape[2]
    weight = qkv_weight.transpose(1, 0, 2)
    gain = norm_gain[None]
    shape = jax.ShapeDtypeStruct
    rows = 8 * clips
    heads = width // HD
    tokens = 128 * peers
    window = depth + 64

    partial = pl.pallas_call(
        fold_kernel,
        grid=(1,),
        out_shape=shape((rows, 3 * width + 128), BF),
        in_specs=[SMEM, HBM, HBM, HBM],
        out_specs=whole((rows, 3 * width + 128)),
        scratch_shapes=[
            pltpu.VMEM((64, window), BF),
            pltpu.VMEM((1, window), F32),
            pltpu.VMEM((3, depth, width), BF),
            pltpu.SemaphoreType.DMA((5,)),
        ],
        compiler_params=params(),
        name="fold",
    )(flow_times, embed_weight, gain, weight)
    got = lax.all_to_all(partial.reshape(clips, 8, -1), "clip", 0, 0, tiled=True).reshape(rows, -1)

    base, down, up = pl.pallas_call(
        conv_kernel,
        grid=(1,),
        out_shape=[shape((128, 128), F32), shape((32, 128), F32), shape((32, 128), F32)],
        in_specs=[HBM, HBM, HBM, ANY],
        out_specs=[whole((128, 128)), whole((32, 128)), whole((32, 128))],
        scratch_shapes=[
            pltpu.VMEM((512, 3 * 384), BF),
            pltpu.VMEM((144, 3 * 384), BF),
            pltpu.VMEM((4, 128, 384), BF),
            pltpu.VMEM((432, 384), BF),
            pltpu.VMEM((4, 2, 16, 64), F32),
            pltpu.SemaphoreType.DMA((3,)),
        ],
        compiler_params=params(),
        name="conv",
    )(
        clip_features.reshape(4, 128, 384),
        enc_weight.transpose(0, 1, 2, 4, 3).reshape(432, 384),
        noise_field[0].transpose(0, 1, 3, 2),
        partial,
    )
    above = lax.ppermute(down, "seq", [(i, i + 1) for i in range(peers - 1)])
    below = lax.ppermute(up, "seq", [(i + 1, i) for i in range(peers - 1)])
    got, base = lax.optimization_barrier((got, base))

    second = pl.pallas_call(
        time_kernel,
        grid=(1,),
        out_shape=shape((rows, 3 * width), BF),
        in_specs=[ANY, HBM, HBM, HBM],
        out_specs=whole((rows, 3 * width)),
        scratch_shapes=[
            pltpu.VMEM((rows, 3 * width + 128), BF),
            pltpu.VMEM((TFEAT, window), BF),
            pltpu.VMEM((1, window), F32),
            pltpu.VMEM((3, depth, width), BF),
            pltpu.SemaphoreType.DMA((6,)),
        ],
        compiler_params=params(),
        name="time_rows",
    )(got, time_weight, gain, weight)
    got = lax.all_to_all(second.reshape(clips, 8, -1), "clip", 0, 0, tiled=True).reshape(rows, -1)

    feat, aq = pl.pallas_call(
        feature_kernel,
        grid=(1,),
        out_shape=[shape((176, 128), BF), shape((256, 256), BF)],
        in_specs=[SMEM, HBM, HBM, whole((128, 128)), whole((32, 128)), whole((32, 128)), ANY],
        out_specs=[whole((176, 128)), whole((256, 256))],
        scratch_shapes=[
            pltpu.VMEM(embed_weight.shape, BF),
            pltpu.VMEM(time_weight.shape, BF),
            pltpu.SemaphoreType.DMA((2,)),
        ],
        compiler_params=params(),
        name="features",
    )(flow_times, embed_weight, time_weight, base, above, below, second)
    got, feat = lax.optimization_barrier((got, feat))

    folded = pl.pallas_call(
        head_rows_kernel,
        grid=(1,),
        out_shape=shape((peers, 576, 128), BF),
        in_specs=[whole((rows, 3 * width)), whole((176, 128))],
        out_specs=whole((peers, 576, 128)),
        compiler_params=params(),
        name="head_rows",
    )(got, feat)
    every = lax.all_to_all(folded, "seq", 0, 0, tiled=True)

    out, dout = pl.pallas_call(
        attention_kernel,
        grid=(peers,),
        out_shape=[shape((128, peers * width), BF)] * 2,
        in_specs=[pl.BlockSpec((1, 400, 128), lambda i: (i, 0, 0)), ANY, whole((256, 256))],
        out_specs=[pl.BlockSpec((128, width), lambda i: (0, i))] * 2,
        scratch_shapes=[
            pltpu.VMEM((peers, 176, 128), BF),
            pltpu.VMEM((256, tokens), BF),
            pltpu.VMEM((256, tokens), BF),
            pltpu.VMEM((256, tokens), BF),
            pltpu.VMEM((heads * 128, tokens), F32),
            pltpu.VMEM((heads * 128, tokens), F32),
            pltpu.VMEM((2 * heads * 128, tokens), BF),
            pltpu.VMEM((heads * 128, 128), F32),
            pltpu.SemaphoreType.DMA((peers,)),
        ],
        compiler_params=params(),
        name="attention",
    )(every, every, aq)
    return (out[None], dout[None])


def solution(mesh):
    placed = (
        P("clip", None, "seq", None, None),
        P(),
        P("clip", None, "seq", None, None),
        P("clip", None),
        P(),
        P(),
        P(),
        P("clip", None, "seq"),
    )
    return jax.shard_map(
        local,
        mesh=mesh,
        in_specs=placed,
        out_specs=(P("clip", "seq", None), P("clip", "seq", None)),
        check_vma=False,
    )
```

```python
import jax
import jax.numpy as jnp
import numpy as np
from jax import lax
from jax.experimental import pallas as pl
from jax.experimental.pallas import tpu as pltpu
from jax.sharding import PartitionSpec as P

D = 5120
HD = 128
TFEAT = 256
TGRID = 1000
EPSILON = 1e-06
QUARTER = TFEAT // 4
F32 = jnp.float32
BF = jnp.bfloat16
HIGH = lax.Precision.HIGHEST
LOG2E = 1.4426950408889634
LN2 = 0.6931471805599453
VMEM = pl.BlockSpec(memory_space=pltpu.VMEM)
SMEM = pl.BlockSpec(memory_space=pltpu.SMEM)
ANY = pl.BlockSpec(memory_space=pl.ANY)
HBM = pl.BlockSpec(memory_space=pltpu.HBM)


def whole(shape):
    return pl.BlockSpec(shape, lambda i: (0,) * len(shape))


def params(limit=63):
    return pltpu.CompilerParams(vmem_limit_bytes=limit * 1024 * 1024)


def dot(a, b, dims=((1,), (0,)), precision=None):
    return lax.dot_general(a, b, (dims, ((), ())), preferred_element_type=F32, precision=precision)


def split(x):
    hi = x.astype(BF)
    return hi, (x - hi.astype(F32)).astype(BF)


def iota(shape, axis):
    return lax.broadcasted_iota(jnp.int32, shape, axis)


def fold_kernel(flow_ref, embed_ref, gain_ref, weight_ref, out_ref, e_ref, g_ref, w_ref, sems):
    rows = out_ref.shape[0]
    _, depth, width = weight_ref.shape
    window = e_ref.shape[1]
    at_clip = lax.axis_index("clip")
    odd = at_clip % 2
    base = pl.multiple_of(at_clip * depth - odd * 64, 128)
    copies = [
        pltpu.make_async_copy(embed_ref.at[:, pl.ds(base, window)], e_ref, sems.at[0]),
        pltpu.make_async_copy(gain_ref.at[:, pl.ds(base, window)], g_ref, sems.at[1]),
    ] + [pltpu.make_async_copy(weight_ref.at[i], w_ref.at[i], sems.at[2 + i]) for i in range(3)]
    for copy in copies:
        copy.start()
    lane = iota((rows, 128), 1)
    start, finish = flow_ref[0, 0], flow_ref[0, 1]
    coded = jnp.where(
        lane == 0,
        start // 256,
        jnp.where(lane == 1, start % 256, jnp.where(lane == 2, finish // 256, finish % 256)),
    )
    row, col = iota((rows, 64), 0), iota((rows, 64), 1)
    twice = jnp.where(col == (row // 8) * 4 + row % 4, 1.0, 0.0).astype(BF)
    copies[0].wait()
    copies[1].wait()
    scaled = dot(twice, e_ref[...]) * g_ref[...]
    scaled = jnp.where(odd == 1, scaled[:, 64 : 64 + depth], scaled[:, :depth])
    scaled_hi, scaled_lo = split(scaled)
    first = (iota((rows, 1), 0) // 4) % 2 == 0
    totals = []
    for i in range(3):
        copies[2 + i].wait()
        totals.append(dot(scaled_hi, w_ref[i]) + dot(scaled_lo, w_ref[i]))
    total = jnp.concatenate(totals + [coded.astype(F32)], axis=1)
    half = out_ref.shape[1]
    out_ref[...] = jnp.where(first, total[:, :half], total[:, half:]).astype(BF)


def frequencies():
    k = iota((1, 128), 1) % QUARTER
    return 8.0 * jnp.exp(k.astype(F32) * np.float32(-np.log(100.0) / QUARTER))


def time_kernel(got_ref, time_ref, gain_ref, weight_ref, out_ref, r_ref, t_ref, g_ref, w_ref, sems):
    rows = out_ref.shape[0]
    groups = rows // 8
    _, depth, width = weight_ref.shape
    window = t_ref.shape[1]
    at_clip = lax.axis_index("clip")
    odd = at_clip % 2
    base = pl.multiple_of(at_clip * depth - odd * 64, 128)
    copies = [
        pltpu.make_async_copy(got_ref, r_ref, sems.at[0]),
        pltpu.make_async_copy(gain_ref.at[:, pl.ds(base, window)], g_ref, sems.at[1]),
        pltpu.make_async_copy(time_ref.at[:, pl.ds(base, window)], t_ref, sems.at[2]),
    ] + [pltpu.make_async_copy(weight_ref.at[i], w_ref.at[i], sems.at[3 + i]) for i in range(3)]
    for copy in copies:
        copy.start()
    freqs = frequencies()
    half_width = r_ref.shape[1]
    copies[0].wait()
    codes = r_ref[:, 3 * width - half_width :].astype(F32)
    start = (codes[:, 0:1] * 256.0 + codes[:, 1:2]) / TGRID
    finish = (codes[:, 2:3] * 256.0 + codes[:, 3:4]) / TGRID
    half = iota((rows, 128), 1) < QUARTER
    angle = freqs * jnp.where(half, finish, finish - start)
    sines, cosines = jnp.sin(angle), jnp.cos(angle)
    place = iota((rows, 1), 0) % 8
    is_value = (place == 4) | (place == 5)
    is_tangent = place >= 6
    first = jnp.where(is_value, sines, jnp.where(is_tangent, freqs * cosines, 0.0))
    second = jnp.where(is_value, cosines, jnp.where(is_tangent, -freqs * sines, 0.0))
    first_hi, first_lo = split(first)
    second_hi, second_lo = split(second)
    copies[1].wait()
    copies[2].wait()
    q = QUARTER
    t_first = jnp.concatenate([t_ref[0:q], t_ref[2 * q : 3 * q]], axis=0)
    t_second = jnp.concatenate([t_ref[q : 2 * q], t_ref[3 * q : 4 * q]], axis=0)
    tau = dot(first_hi, t_first) + dot(first_lo, t_first) + dot(second_hi, t_second) + dot(second_lo, t_second)
    tau = tau * g_ref[...]
    tau = jnp.where(odd == 1, tau[:, 64 : 64 + depth], tau[:, :depth])
    tau_hi, tau_lo = split(tau)
    keep_hi = place % 2 == 0
    summed = r_ref[...].astype(F32).reshape(groups, 8, half_width).sum(axis=0)
    turned = jnp.concatenate([summed[4:], summed[:4]], axis=0)
    summed = jnp.concatenate([summed, turned], axis=1)
    for i in range(3):
        cols = slice(i * width, (i + 1) * width)
        copies[3 + i].wait()
        w = w_ref[i]
        part = dot(tau_hi, w) + dot(tau_lo, w)
        hi = part.astype(BF).astype(F32)
        part = jnp.where(keep_hi, hi, part - hi)
        mine = jnp.concatenate([summed[:, cols]] * groups, axis=0)
        out_ref[:, cols] = jnp.where(place < 4, mine, part).astype(BF)


def head_rows_kernel(got_ref, feat_ref, out_ref):
    rows = got_ref.shape[0]
    heads = 3
    row, col = iota((128, rows), 0), iota((128, rows), 1)
    patch = (row < 64) & (col == (row // 4) * 8 + row % 4)
    place = col % 8
    value = (row >= 64) & (row < 68) & ((place == 4) | (place == 5))
    tangent = (row >= 68) & (row < 72) & (place >= 6)
    pick = jnp.where(patch | value | tangent, 1.0, 0.0).astype(BF)
    total = dot(pick, got_ref[...])
    width = total.shape[1] // 3
    low_row = lambda r: (r == 67) | (r == 71)
    r, l = iota((80, HD), 0), iota((80, HD), 1)
    products, values = [], []
    for h in range(heads):
        part = lambda i: total[:, i * width + h * HD : i * width + (h + 1) * HD]
        q_hi, q_lo = split(part(0)[:80])
        k_hi, k_lo = split(part(1))
        nt = ((1,), (1,))
        product = dot(q_hi, k_hi, nt) + dot(q_lo, k_hi, nt) + dot(q_hi, k_lo, nt)
        hi = product.astype(BF).astype(F32)
        lo = product - hi
        product = jnp.where(low_row(l), jnp.where(r < 64, lo, 0.0), jnp.where(low_row(r), lo, hi))
        products.append(product)
        v = part(2)[:80]
        v_hi = v.astype(BF).astype(F32)
        values.append(jnp.where(low_row(r), v - v_hi, v_hi))
    one, two, three = products
    first = jnp.where(l < 64, one, pltpu.roll(two, 64, 1))
    second = jnp.where(
        l < 64,
        three,
        jnp.where(
            l < 72,
            one,
            jnp.where(l < 80, pltpu.roll(two, 8, 1), jnp.where(l < 88, pltpu.roll(three, 16, 1), 0.0)),
        ),
    )
    blocks = [first, second] + values
    times = jnp.concatenate([b[64:72] for b in blocks] + [jnp.zeros((8, HD), F32)], axis=0).astype(BF)
    for i in range(out_ref.shape[0]):
        for b, block in enumerate(blocks):
            out_ref[i, b * 64 : (b + 1) * 64, :] = block[:64].astype(BF)
        out_ref[i, 320:368, :] = times
        out_ref[i, 368:512, :] = feat_ref[...]


def conv_kernel(x_hbm, w_hbm, noise_hbm, after_ref, out_ref, down_ref, up_ref, xp_ref, wt_ref, x_ref, w_ref, noise_ref, sems):
    copies = [
        pltpu.make_async_copy(x_hbm, x_ref, sems.at[0]),
        pltpu.make_async_copy(w_hbm, w_ref, sems.at[1]),
        pltpu.make_async_copy(noise_hbm, noise_ref, sems.at[2]),
    ]
    for copy in copies:
        copy.start()
    for copy in copies:
        copy.wait()
    chans = x_ref.shape[2]
    row, col = iota((128, 128), 0), iota((128, 128), 1)
    row_w = 2 * (row % 32) + (row // 32) % 2
    same = (row // 64) == (col // 64)
    for e in range(3):
        perm = jnp.where(same & (col % 64 == row_w + (e - 1)), 1.0, 0.0).astype(BF)
        for f in range(4):
            moved = dot(perm, x_ref[f]).astype(BF)
            for g in range(4):
                xp_ref[g * 128 + f * 32 : g * 128 + f * 32 + 32, e * chans : (e + 1) * chans] = moved[
                    g * 32 : g * 32 + 32
                ]
        for ab in range(9):
            tap = (ab * 3 + e) * 16
            wt_ref[ab * 16 : ab * 16 + 16, e * chans : (e + 1) * chans] = w_ref[tap : tap + 16, :]
    y = dot(wt_ref[...], xp_ref[...], ((1,), (1,)))
    lane = iota((16, 128), 1)

    def part(a, b, p, q):
        at = (a * 3 + b) * 16
        g = p * 2 + q
        return y[at : at + 16, g * 128 : (g + 1) * 128]

    def frames(of):
        one = jnp.where(lane >= 32, pltpu.roll(of(1), 32, 1), 0.0)
        two = jnp.where(lane >= 64, pltpu.roll(of(0), 64, 1), 0.0)
        return of(2) + one + two

    for q in range(2):
        own0 = frames(lambda a: part(a, 1, 0, q) + part(a, 2, 1, q))
        own1 = frames(lambda a: part(a, 0, 0, q) + part(a, 1, 1, q))
        down = frames(lambda a: part(a, 0, 1, q))
        up = frames(lambda a: part(a, 2, 0, q))
        out_ref[q * 16 : q * 16 + 16, :] = own0
        out_ref[32 + q * 16 : 48 + q * 16, :] = own1
        down_ref[q * 16 : q * 16 + 16, :] = down
        up_ref[q * 16 : q * 16 + 16, :] = up
    r2, c2 = iota((256, 256), 0), iota((256, 256), 1)
    spread = ((r2 // 64) == (c2 // 32) % 4) & (r2 % 64 == 2 * (c2 % 32) + c2 // 128)
    spread = jnp.where(spread, 1.0, 0.0)
    noise = jnp.concatenate(
        [jnp.concatenate([noise_ref[f, p] for f in range(4)], axis=1) for p in range(2)], axis=0
    )
    moved = dot(noise, spread, precision=HIGH)
    for p in range(2):
        for q in range(2):
            at = 64 + (p * 2 + q) * 16
            out_ref[at : at + 16, :] = moved[p * 16 : p * 16 + 16, q * 128 : (q + 1) * 128]


def time_coefs(s_hi, s_lo, c_hi, c_lo, kind):
    r = iota((8, s_hi.shape[1]), 0)

    def coefs(high, low):
        if kind == 0:
            return jnp.where((r % 4 == 0) | (r % 4 == 3), high, jnp.where(r % 4 == 1, low, 0.0))
        return jnp.where(r % 4 == 2, low, high)

    plain = jnp.where(r < 4, coefs(s_hi, s_lo), 0.0)
    tangent = jnp.where(r < 4, coefs(c_hi, c_lo), coefs(s_hi, s_lo))
    return plain, tangent


def feature_kernel(
    flow_ref, embed_hbm, time_hbm, base_ref, above_ref, below_ref, after_ref, feat_ref, aq_ref, embed_ref, time_ref, sems
):
    copies = [
        pltpu.make_async_copy(time_hbm, time_ref, sems.at[0]),
        pltpu.make_async_copy(embed_hbm, embed_ref, sems.at[1]),
    ]
    for copy in copies:
        copy.start()
    start = flow_ref[0, 0].astype(F32) / TGRID
    finish = flow_ref[0, 1].astype(F32) / TGRID
    freqs = frequencies()
    angle = freqs * jnp.where(iota((8, 128), 1) < QUARTER, finish, finish - start)
    sines, cosines = jnp.sin(angle), jnp.cos(angle)
    row = iota((8, 128), 0)
    first = jnp.where(row == 0, sines, jnp.where(row == 1, freqs * cosines, 0.0))
    second = jnp.where(row == 0, cosines, jnp.where(row == 1, -freqs * sines, 0.0))
    q = QUARTER
    feats = jnp.concatenate([first[:, :q], second[:, :q], first[:, q:], second[:, q:]], axis=1)

    def three(x):
        hi, mid = split(x)
        low = (x - hi.astype(F32) - mid.astype(F32)).astype(BF)
        return jnp.concatenate([hi, mid, low, jnp.zeros_like(hi)], axis=0)

    latent = base_ref[0:64, :] + jnp.concatenate([above_ref[...], below_ref[...]], axis=0)
    noise = base_ref[64:128, :]
    p = (1.0 - finish) * latent + finish * noise
    dp = noise - latent
    for copy in copies:
        copy.wait()
    tau = dot(three(feats), time_ref[...])
    tau = tau[0:8] + tau[8:16] + tau[16:24]
    embed = embed_ref[...]
    gram = dot(embed, embed, ((1,), (1,)))
    cross = dot(embed, three(tau), ((1,), (1,)))
    cross = cross[:, 0:8] + cross[:, 8:16] + cross[:, 16:24]
    square = jnp.sum(tau * tau[0:1], axis=1, keepdims=True)
    gp = dot(gram, p, precision=HIGH)
    e_tau, e_dtau = cross[:, 0:1], cross[:, 1:2]
    mean_sq = jnp.sum(p * (gp + 2.0 * e_tau), axis=0, keepdims=True) + square[0:1]
    mean_sq = jnp.maximum(mean_sq * (1.0 / D), 0.0)
    mixed = jnp.sum(gp * dp + p * e_dtau + dp * e_tau, axis=0, keepdims=True) + square[1:2]
    s = lax.rsqrt(mean_sq + EPSILON)
    c = -(s * s * s) * (mixed * (1.0 / D))
    a = p * s
    da = dp * s + p * c
    up = lambda x: x.astype(BF).astype(F32)
    a_hi, da_hi = up(a), up(da)
    s_hi, c_hi = up(s), up(c)
    s_lo, c_lo = s - s_hi, c - c_hi
    r = iota((8, p.shape[1]), 0)

    cat = lambda xs: jnp.concatenate(xs, axis=0)
    zero = jnp.zeros((8, p.shape[1]), F32)
    v_s, v_d = time_coefs(s_hi, s_lo, c_hi, c_lo, 0)
    scales = jnp.where(r == 0, s_hi, jnp.where(r == 1, s_lo, jnp.where(r == 2, c_hi, jnp.where(r == 3, c_lo, 0.0))))
    feat_ref[...] = cat([a_hi, da_hi, scales, zero]).astype(BF)
    z = jnp.zeros((120, 128), F32)
    aq_ref[0:128, :] = cat([a_hi, a - a_hi, v_s, z]).T.astype(BF)
    aq_ref[128:256, :] = cat([da_hi, da - da_hi, v_d, z]).T.astype(BF)


def attention_kernel(n_ref, aq_ref, out_ref, dout_ref, as_ref, ad_ref, av_ref, *scratch):
    peers = n_ref.shape[0]
    heads = 3
    rows = heads * 128
    chunk = 16
    zero = lambda r, c=HD: jnp.zeros((r, c), BF)
    cat = lambda xs, axis=0: jnp.concatenate(xs, axis=axis)
    for i in range(peers):
        cols = slice(i * 128, (i + 1) * 128)
        a, da = n_ref[i, 368:432], n_ref[i, 432:496]
        scales = n_ref[i, 496:512].astype(F32)
        scales = [scales[k : k + 1] for k in range(4)]
        blank = jnp.zeros((8, 128), F32)
        m_s, m_d = time_coefs(*scales, 1)
        v_s, v_d = time_coefs(*scales, 0)
        m_s, m_d = cat([m_s, blank]).astype(BF), cat([m_d, blank]).astype(BF)
        v = cat([v_s, v_d]).astype(BF)
        as_ref[:, cols] = cat([a, a, zero(64), m_s, zero(48)])
        ad_ref[:, cols] = cat([a, da, a, m_s, m_d, zero(32)])
        av_ref[:, cols] = cat([a, a, da, v, v, zero(32)])

    lane = iota((128, 256), 1)
    low_s = ((lane >= 64) & (lane < 128)) | (lane == 193) | (lane == 197)
    low_d = ((lane >= 128) & (lane < 192)) | (lane == 193) | (lane == 209) | (lane == 213)
    from_q = ((lane >= 64) & (lane < 128)) | (lane >= 200)
    lane = iota((256, 256), 1)
    low_r = ((lane >= 64) & (lane < 128)) | (lane >= 208)
    l = iota((72, HD), 1)

    def times(g, block):
        return n_ref[g, 320:368].astype(F32)[8 * block : 8 * block + 8]

    def scores(g):
        s_ref, d_ref = scratch[4 * (g % 2) : 4 * (g % 2) + 2]
        made = {}

        def absorb(h):
            first = cat([n_ref[g, 0:64].astype(F32), times(g, 0)])
            second = cat([n_ref[g, 64:128].astype(F32), times(g, 1)])
            block = (first, pltpu.roll(first, 64, 1), second)[h]
            swapped = (pltpu.roll(first, 64, 1), first, pltpu.roll(second, 64, 1))[h]
            early = pltpu.roll(second, HD - 8 * h, 1) if h else second
            late = pltpu.roll(second, 16 - 8 * h, 1) if h < 2 else second
            again = jnp.where(
                l < 64, block, jnp.where(l < 72, early, jnp.where((l >= 80) & (l < 88), late, 0.0))
            )
            b = cat([jnp.where(l < 64, block, swapped), again], 1)
            b = cat([b, jnp.zeros((8, 256), F32)]).astype(BF)
            b = cat([b[:64], b[:64], b[64:], zero(112, 256)])
            absorbed = dot(aq_ref[...], b) * (LOG2E * HD ** -0.5)
            hi = absorbed.astype(BF).astype(F32)
            lo = absorbed - hi
            x = jnp.where(low_s, lo[:128], hi[:128]).astype(BF)
            low = jnp.where(from_q, lo[:128], lo[128:])
            high = jnp.where(from_q, hi[:128], hi[128:])
            made[h] = (x, jnp.where(low_d, low, high).astype(BF))

        def score(j, which):
            cols = slice(j * 256, (j + 1) * 256)
            x = cat([made[h][which] for h in range(heads)])
            if which == 0:
                s_ref[:, cols] = dot(x, as_ref[:, cols])
            else:
                d_ref[:, cols] = dot(x, ad_ref[:, cols])

        parts = [lambda h=h: absorb(h) for h in range(heads)]
        tiles = as_ref.shape[1] // 256
        return parts + [lambda j=j, w=w: score(j, w) for w in (0, 1) for j in range(tiles)]

    def softmax(g):
        s_ref, d_ref, et_ref, l_ref = scratch[4 * (g % 2) : 4 * (g % 2) + 4]

        def step(i):
            r = slice(i * chunk, (i + 1) * chunk)
            s = s_ref[r]
            e = jnp.exp2(s - jnp.max(s, axis=1, keepdims=True))
            d = d_ref[r]
            inv = 1.0 / jnp.sum(e, axis=1, keepdims=True)
            mean = jnp.sum(e * d, axis=1, keepdims=True) * inv
            et_ref[r] = e.astype(BF)
            et_ref[rows + i * chunk : rows + (i + 1) * chunk] = (e * (d - mean)).astype(BF)
            l_ref[r] = jnp.broadcast_to(inv, (chunk, 128))

        return [lambda i=i: step(i) for i in range(rows // chunk)]

    def outputs(g):
        et_ref, l_ref = scratch[4 * (g % 2) + 2 : 4 * (g % 2) + 4]
        made = {}

        def mixing():
            made[0] = dot(et_ref[...], av_ref[...], ((1,), (1,)))

        def output(h):
            mixes = made[0]
            at = 128 + h * 64
            mv = n_ref[g, at : at + 64]
            t = times(g, 2 + h)
            blank = jnp.zeros((8, HD), F32)
            early, late = cat([t, blank]).astype(BF), cat([blank, t]).astype(BF)
            inv = l_ref[h * 128 : (h + 1) * 128, 0:1]
            mix = mixes[h * 128 : (h + 1) * 128] * inv
            mix_t = mixes[rows + h * 128 : rows + (h + 1) * 128] * (inv * LN2)
            nx = cat([mv, mv, zero(64), early, early, zero(32)])
            ny = cat([zero(128), mv, late, late, zero(32)])
            both = cat([mix, mix_t])
            hi = both.astype(BF).astype(F32)
            both = jnp.where(low_r, both - hi, hi).astype(BF)
            z = dot(both, cat([nx, ny], 1))
            cols = slice((g * heads + h) * HD, (g * heads + h + 1) * HD)
            out_ref[:, cols] = z[:128, :HD].astype(BF)
            dout_ref[:, cols] = (z[128:, :HD] + z[:128, HD:]).astype(BF)

        return [mixing] + [lambda h=h: output(h) for h in range(heads)]

    for part in scores(0):
        part()
    for g in range(peers):
        matmuls = (outputs(g - 1) if g > 0 else []) + (scores(g + 1) if g + 1 < peers else [])
        steps = softmax(g)
        done = 0
        for i, step in enumerate(steps):
            while done < len(matmuls) and done * len(steps) <= i * len(matmuls):
                matmuls[done]()
                done += 1
            step()
        for part in matmuls[done:]:
            part()
    for part in outputs(peers - 1):
        part()


def local(clip_features, enc_weight, noise_field, flow_times, embed_weight, time_weight, norm_gain, qkv_weight):
    clips = lax.axis_size("clip")
    peers = lax.axis_size("seq")
    depth = qkv_weight.shape[0]
    width = qkv_weight.shape[2]
    weight = qkv_weight.transpose(1, 0, 2)
    gain = norm_gain[None]
    shape = jax.ShapeDtypeStruct
    rows = 8 * clips
    heads = width // HD
    tokens = 128 * peers
    window = depth + 64
    half = (3 * width + 128) // 2

    partial = pl.pallas_call(
        fold_kernel,
        grid=(1,),
        out_shape=shape((rows, half), BF),
        in_specs=[SMEM, HBM, HBM, HBM],
        out_specs=whole((rows, half)),
        scratch_shapes=[
            pltpu.VMEM((64, window), BF),
            pltpu.VMEM((1, window), F32),
            pltpu.VMEM((3, depth, width), BF),
            pltpu.SemaphoreType.DMA((5,)),
        ],
        compiler_params=params(),
        name="fold",
    )(flow_times, embed_weight, gain, weight)
    got = lax.all_to_all(partial.reshape(clips, 8, -1), "clip", 0, 0, tiled=True).reshape(rows, -1)

    base, down, up = pl.pallas_call(
        conv_kernel,
        grid=(1,),
        out_shape=[shape((128, 128), F32), shape((32, 128), F32), shape((32, 128), F32)],
        in_specs=[HBM, HBM, HBM, ANY],
        out_specs=[whole((128, 128)), whole((32, 128)), whole((32, 128))],
        scratch_shapes=[
            pltpu.VMEM((512, 3 * 384), BF),
            pltpu.VMEM((144, 3 * 384), BF),
            pltpu.VMEM((4, 128, 384), BF),
            pltpu.VMEM((432, 384), BF),
            pltpu.VMEM((4, 2, 16, 64), F32),
            pltpu.SemaphoreType.DMA((3,)),
        ],
        compiler_params=params(),
        name="conv",
    )(
        clip_features.reshape(4, 128, 384),
        enc_weight.transpose(0, 1, 2, 4, 3).reshape(432, 384),
        noise_field[0].transpose(0, 1, 3, 2),
        partial,
    )
    above = lax.ppermute(down, "seq", [(i, i + 1) for i in range(peers - 1)])
    below = lax.ppermute(up, "seq", [(i + 1, i) for i in range(peers - 1)])
    got, base, above, below = lax.optimization_barrier((got, base, above, below))

    second = pl.pallas_call(
        time_kernel,
        grid=(1,),
        out_shape=shape((rows, 3 * width), BF),
        in_specs=[ANY, HBM, HBM, HBM],
        out_specs=whole((rows, 3 * width)),
        scratch_shapes=[
            pltpu.VMEM((rows, half), BF),
            pltpu.VMEM((TFEAT, window), BF),
            pltpu.VMEM((1, window), F32),
            pltpu.VMEM((3, depth, width), BF),
            pltpu.SemaphoreType.DMA((6,)),
        ],
        compiler_params=params(),
        name="time_rows",
    )(got, time_weight, gain, weight)
    got = lax.all_to_all(second.reshape(clips, 8, -1), "clip", 0, 0, tiled=True).reshape(rows, -1)

    feat, aq = pl.pallas_call(
        feature_kernel,
        grid=(1,),
        out_shape=[shape((144, 128), BF), shape((256, 256), BF)],
        in_specs=[SMEM, HBM, HBM, whole((128, 128)), whole((32, 128)), whole((32, 128)), ANY],
        out_specs=[whole((144, 128)), whole((256, 256))],
        scratch_shapes=[
            pltpu.VMEM(embed_weight.shape, BF),
            pltpu.VMEM(time_weight.shape, BF),
            pltpu.SemaphoreType.DMA((2,)),
        ],
        compiler_params=params(),
        name="features",
    )(flow_times, embed_weight, time_weight, base, above, below, second)
    got, feat = lax.optimization_barrier((got, feat))

    folded = pl.pallas_call(
        head_rows_kernel,
        grid=(1,),
        out_shape=shape((peers, 512, 128), BF),
        in_specs=[whole((rows, 3 * width)), whole((144, 128))],
        out_specs=whole((peers, 512, 128)),
        compiler_params=params(),
        name="head_rows",
    )(got, feat)
    every = lax.all_to_all(folded, "seq", 0, 0, tiled=True)

    out, dout = pl.pallas_call(
        attention_kernel,
        grid=(1,),
        out_shape=[shape((128, peers * width), BF)] * 2,
        in_specs=[whole((peers, 512, 128)), whole((256, 256))],
        out_specs=[whole((128, peers * width))] * 2,
        scratch_shapes=[pltpu.VMEM((256, tokens), BF)] * 3
        + [
            pltpu.VMEM((heads * 128, tokens), F32),
            pltpu.VMEM((heads * 128, tokens), F32),
            pltpu.VMEM((2 * heads * 128, tokens), BF),
            pltpu.VMEM((heads * 128, 128), F32),
        ]
        * 2,
        compiler_params=params(),
        name="attention",
    )(every, aq)
    return (out[None], dout[None])


def solution(mesh):
    placed = (
        P("clip", None, "seq", None, None),
        P(),
        P("clip", None, "seq", None, None),
        P("clip", None),
        P(),
        P(),
        P(),
        P("clip", None, "seq"),
    )
    return jax.shard_map(
        local,
        mesh=mesh,
        in_specs=placed,
        out_specs=(P("clip", "seq", None), P("clip", "seq", None)),
        check_vma=False,
    )
```

```python
import jax
import jax.numpy as jnp
import numpy as np
from jax import lax
from jax.experimental import pallas as pl
from jax.experimental.pallas import tpu as pltpu
from jax.sharding import PartitionSpec as P

D = 5120
HD = 128
TFEAT = 256
TGRID = 1000
EPSILON = 1e-06
QUARTER = TFEAT // 4
F32 = jnp.float32
BF = jnp.bfloat16
HIGH = lax.Precision.HIGHEST
LOG2E = 1.4426950408889634
LN2 = 0.6931471805599453
VMEM = pl.BlockSpec(memory_space=pltpu.VMEM)
SMEM = pl.BlockSpec(memory_space=pltpu.SMEM)
ANY = pl.BlockSpec(memory_space=pl.ANY)
HBM = pl.BlockSpec(memory_space=pltpu.HBM)


def whole(shape):
    return pl.BlockSpec(shape, lambda i: (0,) * len(shape))


def params(limit=63):
    return pltpu.CompilerParams(vmem_limit_bytes=limit * 1024 * 1024)


def dot(a, b, dims=((1,), (0,)), precision=None):
    return lax.dot_general(a, b, (dims, ((), ())), preferred_element_type=F32, precision=precision)


def split(x):
    hi = x.astype(BF)
    return hi, (x - hi.astype(F32)).astype(BF)


def iota(shape, axis):
    return lax.broadcasted_iota(jnp.int32, shape, axis)


def fold_kernel(flow_ref, embed_ref, gain_ref, weight_ref, out_ref, e_ref, g_ref, w_ref, sems):
    rows = out_ref.shape[0]
    _, depth, width = weight_ref.shape
    window = e_ref.shape[1]
    at_clip = lax.axis_index("clip")
    odd = at_clip % 2
    base = pl.multiple_of(at_clip * depth - odd * 64, 128)
    copies = [
        pltpu.make_async_copy(embed_ref.at[:, pl.ds(base, window)], e_ref, sems.at[0]),
        pltpu.make_async_copy(gain_ref.at[:, pl.ds(base, window)], g_ref, sems.at[1]),
    ] + [pltpu.make_async_copy(weight_ref.at[i], w_ref.at[i], sems.at[2 + i]) for i in range(3)]
    for copy in copies:
        copy.start()
    lane = iota((rows, 128), 1)
    start, finish = flow_ref[0, 0], flow_ref[0, 1]
    coded = jnp.where(
        lane == 0,
        start // 256,
        jnp.where(lane == 1, start % 256, jnp.where(lane == 2, finish // 256, finish % 256)),
    )
    row, col = iota((rows, 64), 0), iota((rows, 64), 1)
    twice = jnp.where(col == (row // 8) * 4 + row % 4, 1.0, 0.0).astype(BF)
    copies[0].wait()
    copies[1].wait()
    scaled = dot(twice, e_ref[...]) * g_ref[...]
    scaled = jnp.where(odd == 1, scaled[:, 64 : 64 + depth], scaled[:, :depth])
    scaled_hi, scaled_lo = split(scaled)
    first = (iota((rows, 1), 0) // 4) % 2 == 0
    totals = []
    for i in range(3):
        copies[2 + i].wait()
        totals.append(dot(scaled_hi, w_ref[i]) + dot(scaled_lo, w_ref[i]))
    total = jnp.concatenate(totals + [coded.astype(F32)], axis=1)
    half = out_ref.shape[1]
    out_ref[...] = jnp.where(first, total[:, :half], total[:, half:]).astype(BF)


def frequencies():
    k = iota((1, 128), 1) % QUARTER
    return 8.0 * jnp.exp(k.astype(F32) * np.float32(-np.log(100.0) / QUARTER))


def time_kernel(got_ref, time_ref, gain_ref, weight_ref, out_ref, r_ref, t_ref, g_ref, w_ref, sems):
    rows = out_ref.shape[0]
    groups = rows // 8
    _, depth, width = weight_ref.shape
    window = t_ref.shape[1]
    at_clip = lax.axis_index("clip")
    odd = at_clip % 2
    base = pl.multiple_of(at_clip * depth - odd * 64, 128)
    copies = [
        pltpu.make_async_copy(got_ref, r_ref, sems.at[0]),
        pltpu.make_async_copy(gain_ref.at[:, pl.ds(base, window)], g_ref, sems.at[1]),
        pltpu.make_async_copy(time_ref.at[:, pl.ds(base, window)], t_ref, sems.at[2]),
    ] + [pltpu.make_async_copy(weight_ref.at[i], w_ref.at[i], sems.at[3 + i]) for i in range(3)]
    for copy in copies:
        copy.start()
    freqs = frequencies()
    half_width = r_ref.shape[1]
    copies[0].wait()
    codes = r_ref[:, 3 * width - half_width :].astype(F32)
    start = (codes[:, 0:1] * 256.0 + codes[:, 1:2]) / TGRID
    finish = (codes[:, 2:3] * 256.0 + codes[:, 3:4]) / TGRID
    half = iota((rows, 128), 1) < QUARTER
    angle = freqs * jnp.where(half, finish, finish - start)
    sines, cosines = jnp.sin(angle), jnp.cos(angle)
    place = iota((rows, 1), 0) % 8
    is_value = (place == 4) | (place == 5)
    is_tangent = place >= 6
    first = jnp.where(is_value, sines, jnp.where(is_tangent, freqs * cosines, 0.0))
    second = jnp.where(is_value, cosines, jnp.where(is_tangent, -freqs * sines, 0.0))
    first_hi, first_lo = split(first)
    second_hi, second_lo = split(second)
    copies[1].wait()
    copies[2].wait()
    q = QUARTER
    t_first = jnp.concatenate([t_ref[0:q], t_ref[2 * q : 3 * q]], axis=0)
    t_second = jnp.concatenate([t_ref[q : 2 * q], t_ref[3 * q : 4 * q]], axis=0)
    tau = dot(first_hi, t_first) + dot(first_lo, t_first) + dot(second_hi, t_second) + dot(second_lo, t_second)
    tau = tau * g_ref[...]
    tau = jnp.where(odd == 1, tau[:, 64 : 64 + depth], tau[:, :depth])
    tau_hi, tau_lo = split(tau)
    keep_hi = place % 2 == 0
    summed = r_ref[...].astype(F32).reshape(groups, 8, half_width).sum(axis=0)
    turned = jnp.concatenate([summed[4:], summed[:4]], axis=0)
    summed = jnp.concatenate([summed, turned], axis=1)
    for i in range(3):
        cols = slice(i * width, (i + 1) * width)
        copies[3 + i].wait()
        w = w_ref[i]
        part = dot(tau_hi, w) + dot(tau_lo, w)
        hi = part.astype(BF).astype(F32)
        part = jnp.where(keep_hi, hi, part - hi)
        mine = jnp.concatenate([summed[:, cols]] * groups, axis=0)
        out_ref[:, cols] = jnp.where(place < 4, mine, part).astype(BF)


def head_rows_kernel(got_ref, conv_ref, out_ref):
    rows = got_ref.shape[0]
    heads = 3
    row, col = iota((128, rows), 0), iota((128, rows), 1)
    patch = (row < 64) & (col == (row // 4) * 8 + row % 4)
    place = col % 8
    value = (row >= 64) & (row < 68) & ((place == 4) | (place == 5))
    tangent = (row >= 68) & (row < 72) & (place >= 6)
    pick = jnp.where(patch | value | tangent, 1.0, 0.0).astype(BF)
    total = dot(pick, got_ref[...])
    width = total.shape[1] // 3
    low_row = lambda r: (r == 67) | (r == 71)
    r, l = iota((80, HD), 0), iota((80, HD), 1)
    products, values = [], []
    for h in range(heads):
        part = lambda i: total[:, i * width + h * HD : i * width + (h + 1) * HD]
        q_hi, q_lo = split(part(0)[:80])
        k_hi, k_lo = split(part(1))
        nt = ((1,), (1,))
        product = dot(q_hi, k_hi, nt) + dot(q_lo, k_hi, nt) + dot(q_hi, k_lo, nt)
        hi = product.astype(BF).astype(F32)
        lo = product - hi
        product = jnp.where(low_row(l), jnp.where(r < 64, lo, 0.0), jnp.where(low_row(r), lo, hi))
        products.append(product)
        v = part(2)[:80]
        v_hi = v.astype(BF).astype(F32)
        values.append(jnp.where(low_row(r), v - v_hi, v_hi))
    one, two, three = products
    first = jnp.where(l < 64, one, pltpu.roll(two, 64, 1))
    second = jnp.where(
        l < 64,
        three,
        jnp.where(
            l < 72,
            one,
            jnp.where(l < 80, pltpu.roll(two, 8, 1), jnp.where(l < 88, pltpu.roll(three, 16, 1), 0.0)),
        ),
    )
    blocks = [first, second] + values
    times = jnp.concatenate([b[64:72] for b in blocks] + [jnp.zeros((8, HD), F32)], axis=0).astype(BF)
    for i in range(out_ref.shape[0]):
        for b, block in enumerate(blocks):
            out_ref[i, b * 64 : (b + 1) * 64, :] = block[:64].astype(BF)
        out_ref[i, 320:368, :] = times
        out_ref[i, 368:560, :] = conv_ref[...]


def conv_kernel(x_hbm, w_hbm, noise_hbm, after_ref, out_ref, xp_ref, wt_ref, x_ref, w_ref, noise_ref, sems):
    copies = [
        pltpu.make_async_copy(x_hbm, x_ref, sems.at[0]),
        pltpu.make_async_copy(w_hbm, w_ref, sems.at[1]),
        pltpu.make_async_copy(noise_hbm, noise_ref, sems.at[2]),
    ]
    for copy in copies:
        copy.start()
    for copy in copies:
        copy.wait()
    chans = x_ref.shape[2]
    row, col = iota((128, 128), 0), iota((128, 128), 1)
    row_w = 2 * (row % 32) + (row // 32) % 2
    same = (row // 64) == (col // 64)
    for e in range(3):
        perm = jnp.where(same & (col % 64 == row_w + (e - 1)), 1.0, 0.0).astype(BF)
        for f in range(4):
            moved = dot(perm, x_ref[f]).astype(BF)
            for g in range(4):
                xp_ref[g * 128 + f * 32 : g * 128 + f * 32 + 32, e * chans : (e + 1) * chans] = moved[
                    g * 32 : g * 32 + 32
                ]
        for ab in range(9):
            tap = (ab * 3 + e) * 16
            wt_ref[ab * 16 : ab * 16 + 16, e * chans : (e + 1) * chans] = w_ref[tap : tap + 16, :]
    y = dot(wt_ref[...], xp_ref[...], ((1,), (1,)))
    lane = iota((16, 128), 1)

    def part(a, b, p, q):
        at = (a * 3 + b) * 16
        g = p * 2 + q
        return y[at : at + 16, g * 128 : (g + 1) * 128]

    def frames(of):
        one = jnp.where(lane >= 32, pltpu.roll(of(1), 32, 1), 0.0)
        two = jnp.where(lane >= 64, pltpu.roll(of(0), 64, 1), 0.0)
        return of(2) + one + two

    for q in range(2):
        own0 = frames(lambda a: part(a, 1, 0, q) + part(a, 2, 1, q))
        own1 = frames(lambda a: part(a, 0, 0, q) + part(a, 1, 1, q))
        down = frames(lambda a: part(a, 0, 1, q))
        up = frames(lambda a: part(a, 2, 0, q))
        out_ref[q * 16 : q * 16 + 16, :] = own0.astype(BF)
        out_ref[32 + q * 16 : 48 + q * 16, :] = own1.astype(BF)
        out_ref[128 + q * 16 : 144 + q * 16, :] = down.astype(BF)
        out_ref[160 + q * 16 : 176 + q * 16, :] = up.astype(BF)
    r2, c2 = iota((256, 256), 0), iota((256, 256), 1)
    spread = ((r2 // 64) == (c2 // 32) % 4) & (r2 % 64 == 2 * (c2 % 32) + c2 // 128)
    spread = jnp.where(spread, 1.0, 0.0)
    noise = jnp.concatenate(
        [jnp.concatenate([noise_ref[f, p] for f in range(4)], axis=1) for p in range(2)], axis=0
    )
    moved = dot(noise, spread, precision=HIGH)
    for p in range(2):
        for q in range(2):
            at = 64 + (p * 2 + q) * 16
            out_ref[at : at + 16, :] = moved[p * 16 : p * 16 + 16, q * 128 : (q + 1) * 128].astype(BF)


def gram_kernel(flow_ref, embed_hbm, time_hbm, after_ref, out_ref, embed_ref, time_ref, sems):
    copies = [
        pltpu.make_async_copy(time_hbm, time_ref, sems.at[0]),
        pltpu.make_async_copy(embed_hbm, embed_ref, sems.at[1]),
    ]
    for copy in copies:
        copy.start()
    start = flow_ref[0, 0].astype(F32) / TGRID
    finish = flow_ref[0, 1].astype(F32) / TGRID
    freqs = frequencies()
    angle = freqs * jnp.where(iota((8, 128), 1) < QUARTER, finish, finish - start)
    sines, cosines = jnp.sin(angle), jnp.cos(angle)
    row = iota((8, 128), 0)
    first = jnp.where(row == 0, sines, jnp.where(row == 1, freqs * cosines, 0.0))
    second = jnp.where(row == 0, cosines, jnp.where(row == 1, -freqs * sines, 0.0))
    q = QUARTER
    feats = jnp.concatenate([first[:, :q], second[:, :q], first[:, q:], second[:, q:]], axis=1)
    feat_hi, feat_lo = split(feats)
    feat_mid = (feats - feat_hi.astype(F32) - feat_lo.astype(F32)).astype(BF)
    feats = jnp.concatenate([feat_hi, feat_lo, feat_mid, jnp.zeros_like(feat_hi)], axis=0)
    for copy in copies:
        copy.wait()
    tau = dot(feats, time_ref[...])
    tau = tau[0:8] + tau[8:16] + tau[16:24]
    embed = embed_ref[...]
    out_ref[0:64, 0:64] = dot(embed, embed, ((1,), (1,)))
    tau_hi, tau_lo = split(tau)
    tau_mid = (tau - tau_hi.astype(F32) - tau_lo.astype(F32)).astype(BF)
    taus = jnp.concatenate([tau_hi, tau_lo, tau_mid, jnp.zeros_like(tau_hi)], axis=0)
    cross = dot(embed, taus, ((1,), (1,)))
    out_ref[0:64, 64:128] = jnp.concatenate(
        [cross[:, 0:8] + cross[:, 8:16] + cross[:, 16:24], jnp.zeros((64, 56), F32)], axis=1
    )
    out_ref[64:72, :] = jnp.sum(tau * tau[0:1], axis=1, keepdims=True) + jnp.zeros((8, 128), F32)


def time_coefs(s_hi, s_lo, c_hi, c_lo, kind):
    r = iota((8, s_hi.shape[1]), 0)

    def coefs(high, low):
        if kind == 0:
            return jnp.where((r % 4 == 0) | (r % 4 == 3), high, jnp.where(r % 4 == 1, low, 0.0))
        return jnp.where(r % 4 == 2, low, high)

    plain = jnp.where(r < 4, coefs(s_hi, s_lo), 0.0)
    tangent = jnp.where(r < 4, coefs(c_hi, c_lo), coefs(s_hi, s_lo))
    return plain, tangent


def attention_kernel(flow_ref, n_ref, gram_ref, out_ref, dout_ref, keep_ref, aq_ref, as_ref, ad_ref, av_ref, *scratch):
    peers = n_ref.shape[0]
    tokens = peers * 128
    heads = 3
    rows = heads * 128
    chunk = 16
    zero = lambda r, c=HD: jnp.zeros((r, c), BF)
    cat = lambda xs, axis=0: jnp.concatenate(xs, axis=axis)
    up = lambda x: x.astype(BF).astype(F32)

    flow_t = flow_ref[0, 1].astype(F32) / TGRID
    patches, tangents = [], []
    none = jnp.zeros((32, 128), F32)
    for i in range(peers):
        above = n_ref[i - 1, 496:528].astype(F32) if i > 0 else none
        below = n_ref[i + 1, 528:560].astype(F32) if i + 1 < peers else none
        latent = n_ref[i, 368:432].astype(F32) + cat([above, below])
        noise = n_ref[i, 432:496].astype(F32)
        patches.append((1.0 - flow_t) * latent + flow_t * noise)
        tangents.append(noise - latent)
    p, dp = cat(patches, 1), cat(tangents, 1)
    gp = dot(gram_ref[0:64, 0:64], p, precision=HIGH)
    e_tau, e_dtau = gram_ref[0:64, 64:65], gram_ref[0:64, 65:66]
    mean_sq = jnp.sum(p * (gp + 2.0 * e_tau), axis=0, keepdims=True) + gram_ref[64:65, 0:1]
    mean_sq = jnp.maximum(mean_sq * (1.0 / D), 0.0)
    mixed = jnp.sum(gp * dp + p * e_dtau + dp * e_tau, axis=0, keepdims=True) + gram_ref[65:66, 0:1]
    s = lax.rsqrt(mean_sq + EPSILON)
    c = -(s * s * s) * (mixed * (1.0 / D))
    a = p * s
    da = dp * s + p * c
    a_hi, da_hi = up(a), up(da)
    s_hi, c_hi = up(s), up(c)
    coefs = (s_hi, s - s_hi, c_hi, c - c_hi)
    m_s, m_d = time_coefs(*coefs, 1)
    v_s, v_d = time_coefs(*coefs, 0)
    gap = lambda n: jnp.zeros((n, tokens), F32)
    as_ref[...] = cat([a_hi, a_hi, a - a_hi, m_s, gap(56)]).astype(BF)
    ad_ref[...] = cat([a_hi, da_hi, a_hi, m_s, gap(8), m_d, gap(40)]).astype(BF)
    av_ref[...] = cat([a_hi, a_hi, da_hi, v_s, v_d, v_s, v_d, gap(32)]).T.astype(BF)
    keep_ref[...] = cat([a, da, v_s, v_d])
    own = pl.multiple_of(lax.axis_index("seq") * 128, 128)
    mine = keep_ref[:, pl.ds(own, 128)]
    a, da = mine[0:64], mine[64:128]
    a_hi, da_hi = up(a), up(da)
    gap = jnp.zeros((120, 128), F32)
    aq_ref[0:128, :] = cat([a_hi, a - a_hi, mine[128:136], gap]).T.astype(BF)
    aq_ref[128:256, :] = cat([da_hi, da - da_hi, mine[136:144], gap]).T.astype(BF)

    lane = iota((128, 256), 1)
    low_s = ((lane >= 64) & (lane < 128)) | (lane == 193) | (lane == 197)
    low_d = ((lane >= 128) & (lane < 192)) | (lane == 193) | (lane == 209) | (lane == 213)
    from_q = ((lane >= 64) & (lane < 128)) | (lane >= 200)
    lane = iota((256, 256), 1)
    low_r = ((lane >= 64) & (lane < 128)) | (lane >= 208)
    l = iota((72, HD), 1)

    def times(g, block):
        return n_ref[g, 320:368].astype(F32)[8 * block : 8 * block + 8]

    def scores(g):
        s_ref, d_ref = scratch[4 * (g % 2) : 4 * (g % 2) + 2]
        made = {}

        def absorb(h):
            first = cat([n_ref[g, 0:64].astype(F32), times(g, 0)])
            second = cat([n_ref[g, 64:128].astype(F32), times(g, 1)])
            block = (first, pltpu.roll(first, 64, 1), second)[h]
            swapped = (pltpu.roll(first, 64, 1), first, pltpu.roll(second, 64, 1))[h]
            early = pltpu.roll(second, HD - 8 * h, 1) if h else second
            late = pltpu.roll(second, 16 - 8 * h, 1) if h < 2 else second
            again = jnp.where(
                l < 64, block, jnp.where(l < 72, early, jnp.where((l >= 80) & (l < 88), late, 0.0))
            )
            b = cat([jnp.where(l < 64, block, swapped), again], 1)
            b = cat([b, jnp.zeros((8, 256), F32)]).astype(BF)
            b = cat([b[:64], b[:64], b[64:], zero(112, 256)])
            absorbed = dot(aq_ref[...], b) * (LOG2E * HD ** -0.5)
            hi = absorbed.astype(BF).astype(F32)
            lo = absorbed - hi
            x = jnp.where(low_s, lo[:128], hi[:128]).astype(BF)
            low = jnp.where(from_q, lo[:128], lo[128:])
            high = jnp.where(from_q, hi[:128], hi[128:])
            made[h] = (x, jnp.where(low_d, low, high).astype(BF))

        def score(j, which):
            cols = slice(j * 256, (j + 1) * 256)
            x = cat([made[h][which] for h in range(heads)])
            if which == 0:
                s_ref[:, cols] = dot(x, as_ref[:, cols])
            else:
                d_ref[:, cols] = dot(x, ad_ref[:, cols])

        parts = [lambda h=h: absorb(h) for h in range(heads)]
        tiles = as_ref.shape[1] // 256
        return parts + [lambda j=j, w=w: score(j, w) for w in (0, 1) for j in range(tiles)]

    def softmax(g):
        s_ref, d_ref, et_ref, l_ref = scratch[4 * (g % 2) : 4 * (g % 2) + 4]

        def step(i):
            r = slice(i * chunk, (i + 1) * chunk)
            s = s_ref[r]
            e = jnp.exp2(s - jnp.max(s, axis=1, keepdims=True))
            d = d_ref[r]
            inv = 1.0 / jnp.sum(e, axis=1, keepdims=True)
            mean = jnp.sum(e * d, axis=1, keepdims=True) * inv
            et_ref[r] = e.astype(BF)
            et_ref[rows + i * chunk : rows + (i + 1) * chunk] = (e * (d - mean)).astype(BF)
            l_ref[r] = jnp.broadcast_to(inv, (chunk, 128))

        return [lambda i=i: step(i) for i in range(rows // chunk)]

    def outputs(g):
        et_ref, l_ref = scratch[4 * (g % 2) + 2 : 4 * (g % 2) + 4]
        made = {}

        def mixing():
            made[0] = cat([dot(et_ref[k * 128 : (k + 1) * 128], av_ref[...]) for k in range(2 * heads)])

        def output(h):
            mixes = made[0]
            at = 128 + h * 64
            mv = n_ref[g, at : at + 64]
            t = times(g, 2 + h)
            blank = jnp.zeros((8, HD), F32)
            early, late = cat([t, blank]).astype(BF), cat([blank, t]).astype(BF)
            inv = l_ref[h * 128 : (h + 1) * 128, 0:1]
            mix = mixes[h * 128 : (h + 1) * 128] * inv
            mix_t = mixes[rows + h * 128 : rows + (h + 1) * 128] * (inv * LN2)
            nx = cat([mv, mv, zero(64), early, early, zero(32)])
            ny = cat([zero(128), mv, late, late, zero(32)])
            both = cat([mix, mix_t])
            hi = both.astype(BF).astype(F32)
            both = jnp.where(low_r, both - hi, hi).astype(BF)
            z = dot(both, cat([nx, ny], 1))
            cols = slice((g * heads + h) * HD, (g * heads + h + 1) * HD)
            out_ref[:, cols] = z[:128, :HD].astype(BF)
            dout_ref[:, cols] = (z[128:, :HD] + z[:128, HD:]).astype(BF)

        return [mixing] + [lambda h=h: output(h) for h in range(heads)]

    for part in scores(0):
        part()
    for g in range(peers):
        matmuls = (outputs(g - 1) if g > 0 else []) + (scores(g + 1) if g + 1 < peers else [])
        steps = softmax(g)
        done = 0
        for i, step in enumerate(steps):
            while done < len(matmuls) and done * len(steps) <= i * len(matmuls):
                matmuls[done]()
                done += 1
            step()
        for part in matmuls[done:]:
            part()
    for part in outputs(peers - 1):
        part()


def local(clip_features, enc_weight, noise_field, flow_times, embed_weight, time_weight, norm_gain, qkv_weight):
    clips = lax.axis_size("clip")
    peers = lax.axis_size("seq")
    depth = qkv_weight.shape[0]
    width = qkv_weight.shape[2]
    weight = qkv_weight.transpose(1, 0, 2)
    gain = norm_gain[None]
    shape = jax.ShapeDtypeStruct
    rows = 8 * clips
    heads = width // HD
    tokens = 128 * peers
    window = depth + 64
    half = (3 * width + 128) // 2

    partial = pl.pallas_call(
        fold_kernel,
        grid=(1,),
        out_shape=shape((rows, half), BF),
        in_specs=[SMEM, HBM, HBM, HBM],
        out_specs=whole((rows, half)),
        scratch_shapes=[
            pltpu.VMEM((64, window), BF),
            pltpu.VMEM((1, window), F32),
            pltpu.VMEM((3, depth, width), BF),
            pltpu.SemaphoreType.DMA((5,)),
        ],
        compiler_params=params(),
        name="fold",
    )(flow_times, embed_weight, gain, weight)
    got = lax.all_to_all(partial.reshape(clips, 8, -1), "clip", 0, 0, tiled=True).reshape(rows, -1)

    conv = pl.pallas_call(
        conv_kernel,
        grid=(1,),
        out_shape=shape((192, 128), BF),
        in_specs=[HBM, HBM, HBM, ANY],
        out_specs=whole((192, 128)),
        scratch_shapes=[
            pltpu.VMEM((512, 3 * 384), BF),
            pltpu.VMEM((144, 3 * 384), BF),
            pltpu.VMEM((4, 128, 384), BF),
            pltpu.VMEM((432, 384), BF),
            pltpu.VMEM((4, 2, 16, 64), F32),
            pltpu.SemaphoreType.DMA((3,)),
        ],
        compiler_params=params(),
        name="conv",
    )(
        clip_features.reshape(4, 128, 384),
        enc_weight.transpose(0, 1, 2, 4, 3).reshape(432, 384),
        noise_field[0].transpose(0, 1, 3, 2),
        partial,
    )
    got, conv = lax.optimization_barrier((got, conv))

    second = pl.pallas_call(
        time_kernel,
        grid=(1,),
        out_shape=shape((rows, 3 * width), BF),
        in_specs=[ANY, HBM, HBM, HBM],
        out_specs=whole((rows, 3 * width)),
        scratch_shapes=[
            pltpu.VMEM((rows, half), BF),
            pltpu.VMEM((TFEAT, window), BF),
            pltpu.VMEM((1, window), F32),
            pltpu.VMEM((3, depth, width), BF),
            pltpu.SemaphoreType.DMA((6,)),
        ],
        compiler_params=params(),
        name="time_rows",
    )(got, time_weight, gain, weight)
    got = lax.all_to_all(second.reshape(clips, 8, -1), "clip", 0, 0, tiled=True).reshape(rows, -1)

    gram = pl.pallas_call(
        gram_kernel,
        grid=(1,),
        out_shape=shape((72, 128), F32),
        in_specs=[SMEM, HBM, HBM, ANY],
        out_specs=whole((72, 128)),
        scratch_shapes=[
            pltpu.VMEM(embed_weight.shape, BF),
            pltpu.VMEM(time_weight.shape, BF),
            pltpu.SemaphoreType.DMA((2,)),
        ],
        compiler_params=params(),
        name="gram",
    )(flow_times, embed_weight, time_weight, second)
    got, gram = lax.optimization_barrier((got, gram))

    folded = pl.pallas_call(
        head_rows_kernel,
        grid=(1,),
        out_shape=shape((peers, 560, 128), BF),
        in_specs=[whole((rows, 3 * width)), whole((192, 128))],
        out_specs=whole((peers, 560, 128)),
        compiler_params=params(),
        name="head_rows",
    )(got, conv)
    every = lax.all_to_all(folded, "seq", 0, 0, tiled=True)

    out, dout = pl.pallas_call(
        attention_kernel,
        grid=(1,),
        out_shape=[shape((128, peers * width), BF)] * 2,
        in_specs=[SMEM, whole((peers, 560, 128)), whole((72, 128))],
        out_specs=[whole((128, peers * width))] * 2,
        scratch_shapes=[pltpu.VMEM((144, tokens), F32), pltpu.VMEM((256, 256), BF)]
        + [pltpu.VMEM((256, tokens), BF)] * 2
        + [pltpu.VMEM((tokens, 256), BF)]
        + [
            pltpu.VMEM((heads * 128, tokens), F32),
            pltpu.VMEM((heads * 128, tokens), F32),
            pltpu.VMEM((2 * heads * 128, tokens), BF),
            pltpu.VMEM((heads * 128, 128), F32),
        ]
        * 2,
        compiler_params=params(),
        name="attention",
    )(flow_times, every, gram)
    return (out[None], dout[None])


def solution(mesh):
    placed = (
        P("clip", None, "seq", None, None),
        P(),
        P("clip", None, "seq", None, None),
        P("clip", None),
        P(),
        P(),
        P(),
        P("clip", None, "seq"),
    )
    return jax.shard_map(
        local,
        mesh=mesh,
        in_specs=placed,
        out_specs=(P("clip", "seq", None), P("clip", "seq", None)),
        check_vma=False,
    )
```

```python
import jax
import jax.numpy as jnp
import numpy as np
from jax import lax
from jax.experimental import pallas as pl
from jax.experimental.pallas import tpu as pltpu
from jax.sharding import PartitionSpec as P

D = 5120
HD = 128
TFEAT = 256
TGRID = 1000
EPSILON = 1e-06
QUARTER = TFEAT // 4
F32 = jnp.float32
BF = jnp.bfloat16
HIGH = lax.Precision.HIGHEST
LOG2E = 1.4426950408889634
LN2 = 0.6931471805599453
VMEM = pl.BlockSpec(memory_space=pltpu.VMEM)
SMEM = pl.BlockSpec(memory_space=pltpu.SMEM)
ANY = pl.BlockSpec(memory_space=pl.ANY)
HBM = pl.BlockSpec(memory_space=pltpu.HBM)


def whole(shape):
    return pl.BlockSpec(shape, lambda i: (0,) * len(shape))


def params(limit=63):
    return pltpu.CompilerParams(vmem_limit_bytes=limit * 1024 * 1024)


def dot(a, b, dims=((1,), (0,)), precision=None):
    return lax.dot_general(a, b, (dims, ((), ())), preferred_element_type=F32, precision=precision)


def split(x):
    hi = x.astype(BF)
    return hi, (x - hi.astype(F32)).astype(BF)


def iota(shape, axis):
    return lax.broadcasted_iota(jnp.int32, shape, axis)


def fold_kernel(flow_ref, embed_ref, gain_ref, weight_ref, out_ref, e_ref, g_ref, w_ref, sems):
    rows = out_ref.shape[0]
    _, depth, width = weight_ref.shape
    window = e_ref.shape[1]
    at_clip = lax.axis_index("clip")
    odd = at_clip % 2
    base = pl.multiple_of(at_clip * depth - odd * 64, 128)
    copies = [
        pltpu.make_async_copy(embed_ref.at[:, pl.ds(base, window)], e_ref, sems.at[0]),
        pltpu.make_async_copy(gain_ref.at[:, pl.ds(base, window)], g_ref, sems.at[1]),
    ] + [pltpu.make_async_copy(weight_ref.at[i], w_ref.at[i], sems.at[2 + i]) for i in range(3)]
    for copy in copies:
        copy.start()
    lane = iota((rows, 128), 1)
    start, finish = flow_ref[0, 0], flow_ref[0, 1]
    coded = jnp.where(
        lane == 0,
        start // 256,
        jnp.where(lane == 1, start % 256, jnp.where(lane == 2, finish // 256, finish % 256)),
    )
    row, col = iota((rows, 64), 0), iota((rows, 64), 1)
    twice = jnp.where(col == (row // 8) * 4 + row % 4, 1.0, 0.0).astype(BF)
    copies[0].wait()
    copies[1].wait()
    scaled = dot(twice, e_ref[...]) * g_ref[...]
    scaled = jnp.where(odd == 1, scaled[:, 64 : 64 + depth], scaled[:, :depth])
    scaled_hi, scaled_lo = split(scaled)
    first = (iota((rows, 1), 0) // 4) % 2 == 0
    totals = []
    for i in range(3):
        copies[2 + i].wait()
        totals.append(dot(scaled_hi, w_ref[i]) + dot(scaled_lo, w_ref[i]))
    total = jnp.concatenate(totals + [coded.astype(F32)], axis=1)
    half = out_ref.shape[1]
    out_ref[...] = jnp.where(first, total[:, :half], total[:, half:]).astype(BF)


def frequencies():
    k = iota((1, 128), 1) % QUARTER
    return 8.0 * jnp.exp(k.astype(F32) * np.float32(-np.log(100.0) / QUARTER))


def time_kernel(got_ref, time_ref, gain_ref, weight_ref, out_ref, r_ref, t_ref, g_ref, w_ref, sems):
    rows = out_ref.shape[0]
    groups = rows // 8
    _, depth, width = weight_ref.shape
    window = t_ref.shape[1]
    at_clip = lax.axis_index("clip")
    odd = at_clip % 2
    base = pl.multiple_of(at_clip * depth - odd * 64, 128)
    copies = [
        pltpu.make_async_copy(got_ref, r_ref, sems.at[0]),
        pltpu.make_async_copy(gain_ref.at[:, pl.ds(base, window)], g_ref, sems.at[1]),
        pltpu.make_async_copy(time_ref.at[:, pl.ds(base, window)], t_ref, sems.at[2]),
    ] + [pltpu.make_async_copy(weight_ref.at[i], w_ref.at[i], sems.at[3 + i]) for i in range(3)]
    for copy in copies:
        copy.start()
    freqs = frequencies()
    half_width = r_ref.shape[1]
    copies[0].wait()
    codes = r_ref[:, 3 * width - half_width :].astype(F32)
    start = (codes[:, 0:1] * 256.0 + codes[:, 1:2]) / TGRID
    finish = (codes[:, 2:3] * 256.0 + codes[:, 3:4]) / TGRID
    half = iota((rows, 128), 1) < QUARTER
    angle = freqs * jnp.where(half, finish, finish - start)
    sines, cosines = jnp.sin(angle), jnp.cos(angle)
    place = iota((rows, 1), 0) % 8
    is_value = (place == 4) | (place == 5)
    is_tangent = place >= 6
    first = jnp.where(is_value, sines, jnp.where(is_tangent, freqs * cosines, 0.0))
    second = jnp.where(is_value, cosines, jnp.where(is_tangent, -freqs * sines, 0.0))
    first_hi, first_lo = split(first)
    second_hi, second_lo = split(second)
    copies[1].wait()
    copies[2].wait()
    q = QUARTER
    t_first = jnp.concatenate([t_ref[0:q], t_ref[2 * q : 3 * q]], axis=0)
    t_second = jnp.concatenate([t_ref[q : 2 * q], t_ref[3 * q : 4 * q]], axis=0)
    tau = dot(first_hi, t_first) + dot(first_lo, t_first) + dot(second_hi, t_second) + dot(second_lo, t_second)
    tau = tau * g_ref[...]
    tau = jnp.where(odd == 1, tau[:, 64 : 64 + depth], tau[:, :depth])
    tau_hi, tau_lo = split(tau)
    keep_hi = place % 2 == 0
    summed = r_ref[...].astype(F32).reshape(groups, 8, half_width).sum(axis=0)
    turned = jnp.concatenate([summed[4:], summed[:4]], axis=0)
    summed = jnp.concatenate([summed, turned], axis=1)
    for i in range(3):
        cols = slice(i * width, (i + 1) * width)
        copies[3 + i].wait()
        w = w_ref[i]
        part = dot(tau_hi, w) + dot(tau_lo, w)
        hi = part.astype(BF).astype(F32)
        part = jnp.where(keep_hi, hi, part - hi)
        mine = jnp.concatenate([summed[:, cols]] * groups, axis=0)
        out_ref[:, cols] = jnp.where(place < 4, mine, part).astype(BF)


def head_rows_kernel(got_ref, conv_ref, out_ref):
    rows = got_ref.shape[0]
    heads = 3
    row, col = iota((128, rows), 0), iota((128, rows), 1)
    patch = (row < 64) & (col == (row // 4) * 8 + row % 4)
    place = col % 8
    value = (row >= 64) & (row < 68) & ((place == 4) | (place == 5))
    tangent = (row >= 68) & (row < 72) & (place >= 6)
    pick = jnp.where(patch | value | tangent, 1.0, 0.0).astype(BF)
    total = dot(pick, got_ref[...])
    width = total.shape[1] // 3
    low_row = lambda r: (r == 67) | (r == 71)
    r, l = iota((80, HD), 0), iota((80, HD), 1)
    products, values = [], []
    for h in range(heads):
        part = lambda i: total[:, i * width + h * HD : i * width + (h + 1) * HD]
        q_hi, q_lo = split(part(0)[:80])
        k_hi, k_lo = split(part(1))
        nt = ((1,), (1,))
        product = dot(q_hi, k_hi, nt) + dot(q_lo, k_hi, nt) + dot(q_hi, k_lo, nt)
        hi = product.astype(BF).astype(F32)
        lo = product - hi
        product = jnp.where(low_row(l), jnp.where(r < 64, lo, 0.0), jnp.where(low_row(r), lo, hi))
        products.append(product)
        v = part(2)[:80]
        v_hi = v.astype(BF).astype(F32)
        values.append(jnp.where(low_row(r), v - v_hi, v_hi))
    one, two, three = products
    first = jnp.where(l < 64, one, pltpu.roll(two, 64, 1))
    second = jnp.where(
        l < 64,
        three,
        jnp.where(
            l < 72,
            one,
            jnp.where(l < 80, pltpu.roll(two, 8, 1), jnp.where(l < 88, pltpu.roll(three, 16, 1), 0.0)),
        ),
    )
    blocks = [first, second] + values
    times = jnp.concatenate([b[64:72] for b in blocks] + [jnp.zeros((8, HD), F32)], axis=0).astype(BF)
    for i in range(out_ref.shape[0]):
        for b, block in enumerate(blocks):
            out_ref[i, b * 64 : (b + 1) * 64, :] = block[:64].astype(BF)
        out_ref[i, 320:368, :] = times
        out_ref[i, 368:560, :] = conv_ref[...]


def conv_kernel(x_hbm, w_hbm, noise_hbm, after_ref, out_ref, xp_ref, wt_ref, x_ref, w_ref, noise_ref, sems):
    copies = [
        pltpu.make_async_copy(x_hbm, x_ref, sems.at[0]),
        pltpu.make_async_copy(w_hbm, w_ref, sems.at[1]),
        pltpu.make_async_copy(noise_hbm, noise_ref, sems.at[2]),
    ]
    for copy in copies:
        copy.start()
    for copy in copies:
        copy.wait()
    chans = x_ref.shape[2]
    row, col = iota((128, 128), 0), iota((128, 128), 1)
    row_w = 2 * (row % 32) + (row // 32) % 2
    same = (row // 64) == (col // 64)
    for e in range(3):
        perm = jnp.where(same & (col % 64 == row_w + (e - 1)), 1.0, 0.0).astype(BF)
        for f in range(4):
            moved = dot(perm, x_ref[f]).astype(BF)
            for g in range(4):
                xp_ref[g * 128 + f * 32 : g * 128 + f * 32 + 32, e * chans : (e + 1) * chans] = moved[
                    g * 32 : g * 32 + 32
                ]
        for ab in range(9):
            tap = (ab * 3 + e) * 16
            wt_ref[ab * 16 : ab * 16 + 16, e * chans : (e + 1) * chans] = w_ref[tap : tap + 16, :]
    y = dot(wt_ref[...], xp_ref[...], ((1,), (1,)))
    lane = iota((16, 128), 1)

    def part(a, b, p, q):
        at = (a * 3 + b) * 16
        g = p * 2 + q
        return y[at : at + 16, g * 128 : (g + 1) * 128]

    def frames(of):
        one = jnp.where(lane >= 32, pltpu.roll(of(1), 32, 1), 0.0)
        two = jnp.where(lane >= 64, pltpu.roll(of(0), 64, 1), 0.0)
        return of(2) + one + two

    for q in range(2):
        own0 = frames(lambda a: part(a, 1, 0, q) + part(a, 2, 1, q))
        own1 = frames(lambda a: part(a, 0, 0, q) + part(a, 1, 1, q))
        down = frames(lambda a: part(a, 0, 1, q))
        up = frames(lambda a: part(a, 2, 0, q))
        out_ref[q * 16 : q * 16 + 16, :] = own0.astype(BF)
        out_ref[32 + q * 16 : 48 + q * 16, :] = own1.astype(BF)
        out_ref[128 + q * 16 : 144 + q * 16, :] = down.astype(BF)
        out_ref[160 + q * 16 : 176 + q * 16, :] = up.astype(BF)
    r2, c2 = iota((256, 256), 0), iota((256, 256), 1)
    spread = ((r2 // 64) == (c2 // 32) % 4) & (r2 % 64 == 2 * (c2 % 32) + c2 // 128)
    spread = jnp.where(spread, 1.0, 0.0)
    noise = jnp.concatenate(
        [jnp.concatenate([noise_ref[f, p] for f in range(4)], axis=1) for p in range(2)], axis=0
    )
    moved = dot(noise, spread, precision=HIGH)
    for p in range(2):
        for q in range(2):
            at = 64 + (p * 2 + q) * 16
            out_ref[at : at + 16, :] = moved[p * 16 : p * 16 + 16, q * 128 : (q + 1) * 128].astype(BF)


def gram_kernel(flow_ref, embed_hbm, time_hbm, after_ref, out_ref, embed_ref, time_ref, sems):
    copies = [
        pltpu.make_async_copy(time_hbm, time_ref, sems.at[0]),
        pltpu.make_async_copy(embed_hbm, embed_ref, sems.at[1]),
    ]
    for copy in copies:
        copy.start()
    start = flow_ref[0, 0].astype(F32) / TGRID
    finish = flow_ref[0, 1].astype(F32) / TGRID
    freqs = frequencies()
    angle = freqs * jnp.where(iota((8, 128), 1) < QUARTER, finish, finish - start)
    sines, cosines = jnp.sin(angle), jnp.cos(angle)
    row = iota((8, 128), 0)
    first = jnp.where(row == 0, sines, jnp.where(row == 1, freqs * cosines, 0.0))
    second = jnp.where(row == 0, cosines, jnp.where(row == 1, -freqs * sines, 0.0))
    q = QUARTER
    feats = jnp.concatenate([first[:, :q], second[:, :q], first[:, q:], second[:, q:]], axis=1)
    feat_hi, feat_lo = split(feats)
    feat_mid = (feats - feat_hi.astype(F32) - feat_lo.astype(F32)).astype(BF)
    feats = jnp.concatenate([feat_hi, feat_lo, feat_mid, jnp.zeros_like(feat_hi)], axis=0)
    for copy in copies:
        copy.wait()
    tau = dot(feats, time_ref[...])
    tau = tau[0:8] + tau[8:16] + tau[16:24]
    embed = embed_ref[...]
    out_ref[0:64, 0:64] = dot(embed, embed, ((1,), (1,)))
    tau_hi, tau_lo = split(tau)
    tau_mid = (tau - tau_hi.astype(F32) - tau_lo.astype(F32)).astype(BF)
    taus = jnp.concatenate([tau_hi, tau_lo, tau_mid, jnp.zeros_like(tau_hi)], axis=0)
    cross = dot(embed, taus, ((1,), (1,)))
    out_ref[0:64, 64:128] = jnp.concatenate(
        [cross[:, 0:8] + cross[:, 8:16] + cross[:, 16:24], jnp.zeros((64, 56), F32)], axis=1
    )
    out_ref[64:72, :] = jnp.sum(tau * tau[0:1], axis=1, keepdims=True) + jnp.zeros((8, 128), F32)


def time_coefs(s_hi, s_lo, c_hi, c_lo, kind):
    r = iota((8, s_hi.shape[1]), 0)

    def coefs(high, low):
        if kind == 0:
            return jnp.where((r % 4 == 0) | (r % 4 == 3), high, jnp.where(r % 4 == 1, low, 0.0))
        return jnp.where(r % 4 == 2, low, high)

    plain = jnp.where(r < 4, coefs(s_hi, s_lo), 0.0)
    tangent = jnp.where(r < 4, coefs(c_hi, c_lo), coefs(s_hi, s_lo))
    return plain, tangent


def attention_kernel(flow_ref, n_ref, gram_ref, out_ref, dout_ref, keep_ref, aq_ref, as_ref, ad_ref, av_ref, *scratch):
    peers = n_ref.shape[0]
    tokens = peers * 128
    heads = 3
    rows = heads * 128
    chunk = 16
    zero = lambda r, c=HD: jnp.zeros((r, c), BF)
    cat = lambda xs, axis=0: jnp.concatenate(xs, axis=axis)
    up = lambda x: x.astype(BF).astype(F32)

    flow_t = flow_ref[0, 1].astype(F32) / TGRID
    patches, tangents = [], []
    none = jnp.zeros((32, 128), F32)
    for i in range(peers):
        above = n_ref[i - 1, 496:528].astype(F32) if i > 0 else none
        below = n_ref[i + 1, 528:560].astype(F32) if i + 1 < peers else none
        latent = n_ref[i, 368:432].astype(F32) + cat([above, below])
        noise = n_ref[i, 432:496].astype(F32)
        patches.append((1.0 - flow_t) * latent + flow_t * noise)
        tangents.append(noise - latent)
    p, dp = cat(patches, 1), cat(tangents, 1)
    gp = dot(gram_ref[0:64, 0:64], p, precision=HIGH)
    e_tau, e_dtau = gram_ref[0:64, 64:65], gram_ref[0:64, 65:66]
    mean_sq = jnp.sum(p * (gp + 2.0 * e_tau), axis=0, keepdims=True) + gram_ref[64:65, 0:1]
    mean_sq = jnp.maximum(mean_sq * (1.0 / D), 0.0)
    mixed = jnp.sum(gp * dp + p * e_dtau + dp * e_tau, axis=0, keepdims=True) + gram_ref[65:66, 0:1]
    s = lax.rsqrt(mean_sq + EPSILON)
    c = -(s * s * s) * (mixed * (1.0 / D))
    a = p * s
    da = dp * s + p * c
    a_hi, da_hi = up(a), up(da)
    s_hi, c_hi = up(s), up(c)
    coefs = (s_hi, s - s_hi, c_hi, c - c_hi)
    m_s, m_d = time_coefs(*coefs, 1)
    v_s, v_d = time_coefs(*coefs, 0)
    gap = lambda n: jnp.zeros((n, tokens), F32)
    as_ref[...] = cat([a_hi, a_hi, a - a_hi, m_s, gap(56)]).astype(BF)
    ad_ref[...] = cat([a_hi, da_hi, a_hi, m_s, gap(8), m_d, gap(40)]).astype(BF)
    av_ref[...] = cat([a_hi, a_hi, da_hi, v_s, v_d, v_s, v_d, gap(32)]).T.astype(BF)
    keep_ref[...] = cat([a, da, v_s, v_d])
    own = pl.multiple_of(lax.axis_index("seq") * 128, 128)
    mine = keep_ref[:, pl.ds(own, 128)]
    a, da = mine[0:64], mine[64:128]
    a_hi, da_hi = up(a), up(da)
    gap = jnp.zeros((120, 128), F32)
    aq_ref[0:128, :] = cat([a_hi, a - a_hi, mine[128:136], gap]).T.astype(BF)
    aq_ref[128:256, :] = cat([da_hi, da - da_hi, mine[136:144], gap]).T.astype(BF)

    lane = iota((128, 256), 1)
    low_s = ((lane >= 64) & (lane < 128)) | (lane == 193) | (lane == 197)
    low_d = ((lane >= 128) & (lane < 192)) | (lane == 193) | (lane == 209) | (lane == 213)
    from_q = ((lane >= 64) & (lane < 128)) | (lane >= 200)
    lane = iota((256, 256), 1)
    low_r = ((lane >= 64) & (lane < 128)) | (lane >= 208)
    l = iota((72, HD), 1)

    def times(g, block):
        return n_ref[g, 320:368].astype(F32)[8 * block : 8 * block + 8]

    def scores(g):
        s_ref, d_ref = scratch[4 * (g % 2) : 4 * (g % 2) + 2]
        made = {}

        def absorb(h):
            first = cat([n_ref[g, 0:64].astype(F32), times(g, 0)])
            second = cat([n_ref[g, 64:128].astype(F32), times(g, 1)])
            block = (first, pltpu.roll(first, 64, 1), second)[h]
            swapped = (pltpu.roll(first, 64, 1), first, pltpu.roll(second, 64, 1))[h]
            early = pltpu.roll(second, HD - 8 * h, 1) if h else second
            late = pltpu.roll(second, 16 - 8 * h, 1) if h < 2 else second
            again = jnp.where(
                l < 64, block, jnp.where(l < 72, early, jnp.where((l >= 80) & (l < 88), late, 0.0))
            )
            b = cat([jnp.where(l < 64, block, swapped), again], 1)
            b = cat([b, jnp.zeros((8, 256), F32)]).astype(BF)
            b = cat([b[:64], b[:64], b[64:], zero(112, 256)])
            absorbed = dot(aq_ref[...], b) * (LOG2E * HD ** -0.5)
            hi = absorbed.astype(BF).astype(F32)
            lo = absorbed - hi
            x = jnp.where(low_s, lo[:128], hi[:128]).astype(BF)
            low = jnp.where(from_q, lo[:128], lo[128:])
            high = jnp.where(from_q, hi[:128], hi[128:])
            made[h] = (x, jnp.where(low_d, low, high).astype(BF))

        def score(j, which):
            cols = slice(j * 256, (j + 1) * 256)
            x = cat([made[h][which] for h in range(heads)])
            if which == 0:
                s_ref[:, cols] = dot(x, as_ref[:, cols])
            else:
                d_ref[:, cols] = dot(x, ad_ref[:, cols])

        parts = [lambda h=h: absorb(h) for h in range(heads)]
        tiles = as_ref.shape[1] // 256
        return parts + [lambda j=j, w=w: score(j, w) for w in (0, 1) for j in range(tiles)]

    def softmax(g):
        s_ref, d_ref, et_ref, l_ref = scratch[4 * (g % 2) : 4 * (g % 2) + 4]

        def step(i):
            r = slice(i * chunk, (i + 1) * chunk)
            s = s_ref[r]
            e = jnp.exp2(s - jnp.max(s, axis=1, keepdims=True))
            d = d_ref[r]
            inv = 1.0 / jnp.sum(e, axis=1, keepdims=True)
            mean = jnp.sum(e * d, axis=1, keepdims=True) * inv
            et_ref[r] = e.astype(BF)
            et_ref[rows + i * chunk : rows + (i + 1) * chunk] = (e * (d - mean)).astype(BF)
            l_ref[r] = jnp.broadcast_to(inv, (chunk, 128))

        return [lambda i=i: step(i) for i in range(rows // chunk)]

    def outputs(g):
        et_ref, l_ref = scratch[4 * (g % 2) + 2 : 4 * (g % 2) + 4]
        made = {}

        def mixing():
            made[0] = cat([dot(et_ref[k * 128 : (k + 1) * 128], av_ref[...]) for k in range(2 * heads)])

        def output(h):
            mixes = made[0]
            at = 128 + h * 64
            mv = n_ref[g, at : at + 64]
            t = times(g, 2 + h)
            blank = jnp.zeros((8, HD), F32)
            early, late = cat([t, blank]).astype(BF), cat([blank, t]).astype(BF)
            inv = l_ref[h * 128 : (h + 1) * 128, 0:1]
            mix = mixes[h * 128 : (h + 1) * 128] * inv
            mix_t = mixes[rows + h * 128 : rows + (h + 1) * 128] * (inv * LN2)
            nx = cat([mv, mv, zero(64), early, early, zero(32)])
            ny = cat([zero(128), mv, late, late, zero(32)])
            both = cat([mix, mix_t])
            hi = both.astype(BF).astype(F32)
            both = jnp.where(low_r, both - hi, hi).astype(BF)
            z = dot(both, cat([nx, ny], 1))
            cols = slice((g * heads + h) * HD, (g * heads + h + 1) * HD)
            out_ref[:, cols] = z[:128, :HD].astype(BF)
            dout_ref[:, cols] = (z[128:, :HD] + z[:128, HD:]).astype(BF)

        return [mixing] + [lambda h=h: output(h) for h in range(heads)]

    for part in scores(0):
        part()
    for g in range(peers):
        matmuls = (outputs(g - 1) if g > 0 else []) + (scores(g + 1) if g + 1 < peers else [])
        steps = softmax(g)
        done = 0
        for i, step in enumerate(steps):
            while done < len(matmuls) and done * len(steps) <= i * len(matmuls):
                matmuls[done]()
                done += 1
            step()
        for part in matmuls[done:]:
            part()
    for part in outputs(peers - 1):
        part()


def local(clip_features, enc_weight, noise_field, flow_times, embed_weight, time_weight, norm_gain, qkv_weight):
    clips = lax.axis_size("clip")
    peers = lax.axis_size("seq")
    depth = qkv_weight.shape[0]
    width = qkv_weight.shape[2]
    weight = qkv_weight.transpose(1, 0, 2)
    gain = norm_gain[None]
    shape = jax.ShapeDtypeStruct
    rows = 8 * clips
    heads = width // HD
    tokens = 128 * peers
    window = depth + 64
    half = (3 * width + 128) // 2

    partial = pl.pallas_call(
        fold_kernel,
        grid=(1,),
        out_shape=shape((rows, half), BF),
        in_specs=[SMEM, HBM, HBM, HBM],
        out_specs=whole((rows, half)),
        scratch_shapes=[
            pltpu.VMEM((64, window), BF),
            pltpu.VMEM((1, window), F32),
            pltpu.VMEM((3, depth, width), BF),
            pltpu.SemaphoreType.DMA((5,)),
        ],
        compiler_params=params(),
        name="fold",
    )(flow_times, embed_weight, gain, weight)
    got = lax.all_to_all(partial.reshape(clips, 8, -1), "clip", 0, 0, tiled=True).reshape(rows, -1)

    conv = pl.pallas_call(
        conv_kernel,
        grid=(1,),
        out_shape=shape((192, 128), BF),
        in_specs=[HBM, HBM, HBM, ANY],
        out_specs=whole((192, 128)),
        scratch_shapes=[
            pltpu.VMEM((512, 3 * 384), BF),
            pltpu.VMEM((144, 3 * 384), BF),
            pltpu.VMEM((4, 128, 384), BF),
            pltpu.VMEM((432, 384), BF),
            pltpu.VMEM((4, 2, 16, 64), F32),
            pltpu.SemaphoreType.DMA((3,)),
        ],
        compiler_params=params(24),
        name="conv",
    )(
        clip_features.reshape(4, 128, 384),
        enc_weight.transpose(0, 1, 2, 4, 3).reshape(432, 384),
        noise_field[0].transpose(0, 1, 3, 2),
        partial,
    )
    got, conv = lax.optimization_barrier((got, conv))

    second = pl.pallas_call(
        time_kernel,
        grid=(1,),
        out_shape=shape((rows, 3 * width), BF),
        in_specs=[ANY, HBM, HBM, HBM],
        out_specs=whole((rows, 3 * width)),
        scratch_shapes=[
            pltpu.VMEM((rows, half), BF),
            pltpu.VMEM((TFEAT, window), BF),
            pltpu.VMEM((1, window), F32),
            pltpu.VMEM((3, depth, width), BF),
            pltpu.SemaphoreType.DMA((6,)),
        ],
        compiler_params=params(24),
        name="time_rows",
    )(got, time_weight, gain, weight)
    got = lax.all_to_all(second.reshape(clips, 8, -1), "clip", 0, 0, tiled=True).reshape(rows, -1)

    gram = pl.pallas_call(
        gram_kernel,
        grid=(1,),
        out_shape=shape((72, 128), F32),
        in_specs=[SMEM, HBM, HBM, ANY],
        out_specs=whole((72, 128)),
        scratch_shapes=[
            pltpu.VMEM(embed_weight.shape, BF),
            pltpu.VMEM(time_weight.shape, BF),
            pltpu.SemaphoreType.DMA((2,)),
        ],
        compiler_params=params(24),
        name="gram",
    )(flow_times, embed_weight, time_weight, second)
    got, gram = lax.optimization_barrier((got, gram))

    folded = pl.pallas_call(
        head_rows_kernel,
        grid=(1,),
        out_shape=shape((peers, 560, 128), BF),
        in_specs=[whole((rows, 3 * width)), whole((192, 128))],
        out_specs=whole((peers, 560, 128)),
        compiler_params=params(24),
        name="head_rows",
    )(got, conv)
    every = lax.all_to_all(folded, "seq", 0, 0, tiled=True)

    out, dout = pl.pallas_call(
        attention_kernel,
        grid=(1,),
        out_shape=[shape((128, peers * width), BF)] * 2,
        in_specs=[SMEM, whole((peers, 560, 128)), whole((72, 128))],
        out_specs=[whole((128, peers * width))] * 2,
        scratch_shapes=[pltpu.VMEM((144, tokens), F32), pltpu.VMEM((256, 256), BF)]
        + [pltpu.VMEM((256, tokens), BF)] * 2
        + [pltpu.VMEM((tokens, 256), BF)]
        + [
            pltpu.VMEM((heads * 128, tokens), F32),
            pltpu.VMEM((heads * 128, tokens), F32),
            pltpu.VMEM((2 * heads * 128, tokens), BF),
            pltpu.VMEM((heads * 128, 128), F32),
        ]
        * 2,
        compiler_params=params(),
        name="attention",
    )(flow_times, every, gram)
    return (out[None], dout[None])


def solution(mesh):
    placed = (
        P("clip", None, "seq", None, None),
        P(),
        P("clip", None, "seq", None, None),
        P("clip", None),
        P(),
        P(),
        P(),
        P("clip", None, "seq"),
    )
    return jax.shard_map(
        local,
        mesh=mesh,
        in_specs=placed,
        out_specs=(P("clip", "seq", None), P("clip", "seq", None)),
        check_vma=False,
    )
```

```python
import jax
import jax.numpy as jnp
import numpy as np
from jax import lax
from jax.experimental import pallas as pl
from jax.experimental.pallas import tpu as pltpu
from jax.sharding import PartitionSpec as P

D = 5120
HD = 128
TFEAT = 256
TGRID = 1000
EPSILON = 1e-06
QUARTER = TFEAT // 4
F32 = jnp.float32
BF = jnp.bfloat16
HIGH = lax.Precision.HIGHEST
LOG2E = 1.4426950408889634
LN2 = 0.6931471805599453
VMEM = pl.BlockSpec(memory_space=pltpu.VMEM)
SMEM = pl.BlockSpec(memory_space=pltpu.SMEM)
ANY = pl.BlockSpec(memory_space=pl.ANY)
HBM = pl.BlockSpec(memory_space=pltpu.HBM)


def whole(shape):
    return pl.BlockSpec(shape, lambda i: (0,) * len(shape))


def params(limit=63):
    return pltpu.CompilerParams(vmem_limit_bytes=limit * 1024 * 1024)


def dot(a, b, dims=((1,), (0,)), precision=None):
    return lax.dot_general(a, b, (dims, ((), ())), preferred_element_type=F32, precision=precision)


def split(x):
    hi = x.astype(BF)
    return hi, (x - hi.astype(F32)).astype(BF)


def iota(shape, axis):
    return lax.broadcasted_iota(jnp.int32, shape, axis)


def fold_kernel(flow_ref, embed_ref, gain_ref, weight_ref, out_ref, e_ref, g_ref, w_ref, sems):
    rows = out_ref.shape[0]
    _, depth, width = weight_ref.shape
    window = e_ref.shape[1]
    at_clip = lax.axis_index("clip")
    odd = at_clip % 2
    base = pl.multiple_of(at_clip * depth - odd * 64, 128)
    copies = [
        pltpu.make_async_copy(embed_ref.at[:, pl.ds(base, window)], e_ref, sems.at[0]),
        pltpu.make_async_copy(gain_ref.at[:, pl.ds(base, window)], g_ref, sems.at[1]),
    ] + [pltpu.make_async_copy(weight_ref.at[i], w_ref.at[i], sems.at[2 + i]) for i in range(3)]
    for copy in copies:
        copy.start()
    lane = iota((rows, 128), 1)
    start, finish = flow_ref[0, 0], flow_ref[0, 1]
    coded = jnp.where(
        lane == 0,
        start // 256,
        jnp.where(lane == 1, start % 256, jnp.where(lane == 2, finish // 256, finish % 256)),
    )
    row, col = iota((rows, 64), 0), iota((rows, 64), 1)
    twice = jnp.where(col == (row // 8) * 4 + row % 4, 1.0, 0.0).astype(BF)
    copies[0].wait()
    copies[1].wait()
    scaled = dot(twice, e_ref[...]) * g_ref[...]
    scaled = jnp.where(odd == 1, scaled[:, 64 : 64 + depth], scaled[:, :depth])
    scaled_hi, scaled_lo = split(scaled)
    first = (iota((rows, 1), 0) // 4) % 2 == 0
    totals = []
    for i in range(3):
        copies[2 + i].wait()
        totals.append(dot(scaled_hi, w_ref[i]) + dot(scaled_lo, w_ref[i]))
    total = jnp.concatenate(totals + [coded.astype(F32)], axis=1)
    half = out_ref.shape[1]
    out_ref[...] = jnp.where(first, total[:, :half], total[:, half:]).astype(BF)


def frequencies():
    k = iota((1, 128), 1) % QUARTER
    return 8.0 * jnp.exp(k.astype(F32) * np.float32(-np.log(100.0) / QUARTER))


def time_kernel(got_ref, time_ref, gain_ref, weight_ref, out_ref, r_ref, t_ref, g_ref, w_ref, sems):
    rows = out_ref.shape[0]
    groups = rows // 8
    _, depth, width = weight_ref.shape
    window = t_ref.shape[1]
    at_clip = lax.axis_index("clip")
    odd = at_clip % 2
    base = pl.multiple_of(at_clip * depth - odd * 64, 128)
    copies = [
        pltpu.make_async_copy(got_ref, r_ref, sems.at[0]),
        pltpu.make_async_copy(gain_ref.at[:, pl.ds(base, window)], g_ref, sems.at[1]),
        pltpu.make_async_copy(time_ref.at[:, pl.ds(base, window)], t_ref, sems.at[2]),
    ] + [pltpu.make_async_copy(weight_ref.at[i], w_ref.at[i], sems.at[3 + i]) for i in range(3)]
    for copy in copies:
        copy.start()
    freqs = frequencies()
    half_width = r_ref.shape[1]
    copies[0].wait()
    codes = r_ref[:, 3 * width - half_width :].astype(F32)
    start = (codes[:, 0:1] * 256.0 + codes[:, 1:2]) / TGRID
    finish = (codes[:, 2:3] * 256.0 + codes[:, 3:4]) / TGRID
    half = iota((rows, 128), 1) < QUARTER
    angle = freqs * jnp.where(half, finish, finish - start)
    sines, cosines = jnp.sin(angle), jnp.cos(angle)
    place = iota((rows, 1), 0) % 8
    is_value = (place == 4) | (place == 5)
    is_tangent = place >= 6
    first = jnp.where(is_value, sines, jnp.where(is_tangent, freqs * cosines, 0.0))
    second = jnp.where(is_value, cosines, jnp.where(is_tangent, -freqs * sines, 0.0))
    first_hi, first_lo = split(first)
    second_hi, second_lo = split(second)
    copies[1].wait()
    copies[2].wait()
    q = QUARTER
    t_first = jnp.concatenate([t_ref[0:q], t_ref[2 * q : 3 * q]], axis=0)
    t_second = jnp.concatenate([t_ref[q : 2 * q], t_ref[3 * q : 4 * q]], axis=0)
    tau = dot(first_hi, t_first) + dot(first_lo, t_first) + dot(second_hi, t_second) + dot(second_lo, t_second)
    tau = tau * g_ref[...]
    tau = jnp.where(odd == 1, tau[:, 64 : 64 + depth], tau[:, :depth])
    tau_hi, tau_lo = split(tau)
    keep_hi = place % 2 == 0
    summed = r_ref[...].astype(F32).reshape(groups, 8, half_width).sum(axis=0)
    turned = jnp.concatenate([summed[4:], summed[:4]], axis=0)
    summed = jnp.concatenate([summed, turned], axis=1)
    for i in range(3):
        cols = slice(i * width, (i + 1) * width)
        copies[3 + i].wait()
        w = w_ref[i]
        part = dot(tau_hi, w) + dot(tau_lo, w)
        hi = part.astype(BF).astype(F32)
        part = jnp.where(keep_hi, hi, part - hi)
        mine = jnp.concatenate([summed[:, cols]] * groups, axis=0)
        out_ref[:, cols] = jnp.where(place < 4, mine, part).astype(BF)


def head_rows_kernel(got_ref, conv_ref, out_ref):
    rows = got_ref.shape[0]
    heads = 3
    row, col = iota((128, rows), 0), iota((128, rows), 1)
    patch = (row < 64) & (col == (row // 4) * 8 + row % 4)
    place = col % 8
    value = (row >= 64) & (row < 68) & ((place == 4) | (place == 5))
    tangent = (row >= 68) & (row < 72) & (place >= 6)
    pick = jnp.where(patch | value | tangent, 1.0, 0.0).astype(BF)
    total = dot(pick, got_ref[...])
    width = total.shape[1] // 3
    low_row = lambda r: (r == 67) | (r == 71)
    r, l = iota((80, HD), 0), iota((80, HD), 1)
    products, values = [], []
    for h in range(heads):
        part = lambda i: total[:, i * width + h * HD : i * width + (h + 1) * HD]
        q_hi, q_lo = split(part(0)[:80])
        k_hi, k_lo = split(part(1))
        nt = ((1,), (1,))
        product = dot(q_hi, k_hi, nt) + dot(q_lo, k_hi, nt) + dot(q_hi, k_lo, nt)
        hi = product.astype(BF).astype(F32)
        lo = product - hi
        product = jnp.where(low_row(l), jnp.where(r < 64, lo, 0.0), jnp.where(low_row(r), lo, hi))
        products.append(product)
        v = part(2)[:80]
        v_hi = v.astype(BF).astype(F32)
        values.append(jnp.where(low_row(r), v - v_hi, v_hi))
    one, two, three = products
    first = jnp.where(l < 64, one, pltpu.roll(two, 64, 1))
    second = jnp.where(
        l < 64,
        three,
        jnp.where(
            l < 72,
            one,
            jnp.where(l < 80, pltpu.roll(two, 8, 1), jnp.where(l < 88, pltpu.roll(three, 16, 1), 0.0)),
        ),
    )
    blocks = [first, second] + values
    times = jnp.concatenate([b[64:72] for b in blocks] + [jnp.zeros((8, HD), F32)], axis=0).astype(BF)
    for i in range(out_ref.shape[0]):
        for b, block in enumerate(blocks):
            out_ref[i, b * 64 : (b + 1) * 64, :] = block[:64].astype(BF)
        out_ref[i, 320:368, :] = times
        out_ref[i, 368:560, :] = conv_ref[...]


def conv_kernel(x_hbm, w_hbm, noise_hbm, after_ref, out_ref, xp_ref, wt_ref, x_ref, w_ref, noise_ref, sems):
    copies = [
        pltpu.make_async_copy(x_hbm, x_ref, sems.at[0]),
        pltpu.make_async_copy(w_hbm, w_ref, sems.at[1]),
        pltpu.make_async_copy(noise_hbm, noise_ref, sems.at[2]),
    ]
    for copy in copies:
        copy.start()
    for copy in copies:
        copy.wait()
    chans = x_ref.shape[2]
    row, col = iota((128, 128), 0), iota((128, 128), 1)
    row_w = 2 * (row % 32) + (row // 32) % 2
    same = (row // 64) == (col // 64)
    for e in range(3):
        perm = jnp.where(same & (col % 64 == row_w + (e - 1)), 1.0, 0.0).astype(BF)
        for f in range(4):
            moved = dot(perm, x_ref[f]).astype(BF)
            for g in range(4):
                xp_ref[g * 128 + f * 32 : g * 128 + f * 32 + 32, e * chans : (e + 1) * chans] = moved[
                    g * 32 : g * 32 + 32
                ]
        for ab in range(9):
            tap = (ab * 3 + e) * 16
            wt_ref[ab * 16 : ab * 16 + 16, e * chans : (e + 1) * chans] = w_ref[tap : tap + 16, :]
    y = dot(wt_ref[...], xp_ref[...], ((1,), (1,)))
    lane = iota((16, 128), 1)

    def part(a, b, p, q):
        at = (a * 3 + b) * 16
        g = p * 2 + q
        return y[at : at + 16, g * 128 : (g + 1) * 128]

    def frames(of):
        one = jnp.where(lane >= 32, pltpu.roll(of(1), 32, 1), 0.0)
        two = jnp.where(lane >= 64, pltpu.roll(of(0), 64, 1), 0.0)
        return of(2) + one + two

    for q in range(2):
        own0 = frames(lambda a: part(a, 1, 0, q) + part(a, 2, 1, q))
        own1 = frames(lambda a: part(a, 0, 0, q) + part(a, 1, 1, q))
        down = frames(lambda a: part(a, 0, 1, q))
        up = frames(lambda a: part(a, 2, 0, q))
        out_ref[q * 16 : q * 16 + 16, :] = own0.astype(BF)
        out_ref[32 + q * 16 : 48 + q * 16, :] = own1.astype(BF)
        out_ref[128 + q * 16 : 144 + q * 16, :] = down.astype(BF)
        out_ref[160 + q * 16 : 176 + q * 16, :] = up.astype(BF)
    r2, c2 = iota((256, 256), 0), iota((256, 256), 1)
    spread = ((r2 // 64) == (c2 // 32) % 4) & (r2 % 64 == 2 * (c2 % 32) + c2 // 128)
    spread = jnp.where(spread, 1.0, 0.0)
    noise = jnp.concatenate(
        [jnp.concatenate([noise_ref[f, p] for f in range(4)], axis=1) for p in range(2)], axis=0
    )
    moved = dot(noise, spread, precision=HIGH)
    for p in range(2):
        for q in range(2):
            at = 64 + (p * 2 + q) * 16
            out_ref[at : at + 16, :] = moved[p * 16 : p * 16 + 16, q * 128 : (q + 1) * 128].astype(BF)


def gram_kernel(flow_ref, embed_hbm, time_hbm, after_ref, out_ref, embed_ref, time_ref, sems):
    copies = [
        pltpu.make_async_copy(time_hbm, time_ref, sems.at[0]),
        pltpu.make_async_copy(embed_hbm, embed_ref, sems.at[1]),
    ]
    for copy in copies:
        copy.start()
    start = flow_ref[0, 0].astype(F32) / TGRID
    finish = flow_ref[0, 1].astype(F32) / TGRID
    freqs = frequencies()
    angle = freqs * jnp.where(iota((8, 128), 1) < QUARTER, finish, finish - start)
    sines, cosines = jnp.sin(angle), jnp.cos(angle)
    row = iota((8, 128), 0)
    first = jnp.where(row == 0, sines, jnp.where(row == 1, freqs * cosines, 0.0))
    second = jnp.where(row == 0, cosines, jnp.where(row == 1, -freqs * sines, 0.0))
    q = QUARTER
    feats = jnp.concatenate([first[:, :q], second[:, :q], first[:, q:], second[:, q:]], axis=1)
    feat_hi, feat_lo = split(feats)
    feat_mid = (feats - feat_hi.astype(F32) - feat_lo.astype(F32)).astype(BF)
    feats = jnp.concatenate([feat_hi, feat_lo, feat_mid, jnp.zeros_like(feat_hi)], axis=0)
    for copy in copies:
        copy.wait()
    tau = dot(feats, time_ref[...])
    tau = tau[0:8] + tau[8:16] + tau[16:24]
    embed = embed_ref[...]
    out_ref[0:64, 0:64] = dot(embed, embed, ((1,), (1,)))
    tau_hi, tau_lo = split(tau)
    tau_mid = (tau - tau_hi.astype(F32) - tau_lo.astype(F32)).astype(BF)
    taus = jnp.concatenate([tau_hi, tau_lo, tau_mid, jnp.zeros_like(tau_hi)], axis=0)
    cross = dot(embed, taus, ((1,), (1,)))
    out_ref[0:64, 64:128] = jnp.concatenate(
        [cross[:, 0:8] + cross[:, 8:16] + cross[:, 16:24], jnp.zeros((64, 56), F32)], axis=1
    )
    out_ref[64:72, :] = jnp.sum(tau * tau[0:1], axis=1, keepdims=True) + jnp.zeros((8, 128), F32)


def time_coefs(s_hi, s_lo, c_hi, c_lo, kind):
    r = iota((8, s_hi.shape[1]), 0)

    def coefs(high, low):
        if kind == 0:
            return jnp.where((r % 4 == 0) | (r % 4 == 3), high, jnp.where(r % 4 == 1, low, 0.0))
        return jnp.where(r % 4 == 2, low, high)

    plain = jnp.where(r < 4, coefs(s_hi, s_lo), 0.0)
    tangent = jnp.where(r < 4, coefs(c_hi, c_lo), coefs(s_hi, s_lo))
    return plain, tangent


def attention_kernel(flow_ref, n_ref, gram_ref, out_ref, dout_ref, keep_ref, aq_ref, as_ref, ad_ref, av_ref, *scratch):
    peers = n_ref.shape[0]
    tokens = peers * 128
    heads = 3
    rows = heads * 128
    chunk = 16
    zero = lambda r, c=HD: jnp.zeros((r, c), BF)
    cat = lambda xs, axis=0: jnp.concatenate(xs, axis=axis)
    up = lambda x: x.astype(BF).astype(F32)

    flow_t = flow_ref[0, 1].astype(F32) / TGRID
    patches, tangents = [], []
    none = jnp.zeros((32, 128), F32)
    for i in range(peers):
        above = n_ref[i - 1, 496:528].astype(F32) if i > 0 else none
        below = n_ref[i + 1, 528:560].astype(F32) if i + 1 < peers else none
        latent = n_ref[i, 368:432].astype(F32) + cat([above, below])
        noise = n_ref[i, 432:496].astype(F32)
        patches.append((1.0 - flow_t) * latent + flow_t * noise)
        tangents.append(noise - latent)
    p, dp = cat(patches, 1), cat(tangents, 1)
    gp = dot(gram_ref[0:64, 0:64], p, precision=HIGH)
    e_tau, e_dtau = gram_ref[0:64, 64:65], gram_ref[0:64, 65:66]
    mean_sq = jnp.sum(p * (gp + 2.0 * e_tau), axis=0, keepdims=True) + gram_ref[64:65, 0:1]
    mean_sq = jnp.maximum(mean_sq * (1.0 / D), 0.0)
    mixed = jnp.sum(gp * dp + p * e_dtau + dp * e_tau, axis=0, keepdims=True) + gram_ref[65:66, 0:1]
    s = lax.rsqrt(mean_sq + EPSILON)
    c = -(s * s * s) * (mixed * (1.0 / D))
    a = p * s
    da = dp * s + p * c
    a_hi, da_hi = up(a), up(da)
    s_hi, c_hi = up(s), up(c)
    coefs = (s_hi, s - s_hi, c_hi, c - c_hi)
    m_s, m_d = time_coefs(*coefs, 1)
    v_s, v_d = time_coefs(*coefs, 0)
    gap = lambda n: jnp.zeros((n, tokens), F32)
    as_ref[...] = cat([a_hi, a_hi, a - a_hi, m_s, gap(56)]).astype(BF)
    ad_ref[...] = cat([a_hi, da_hi, a_hi, m_s, gap(8), m_d, gap(40)]).astype(BF)
    av_ref[...] = cat([a_hi, a_hi, da_hi, v_s, v_d, v_s, v_d, gap(32)]).T.astype(BF)
    keep_ref[...] = cat([a, da, v_s, v_d])
    own = pl.multiple_of(lax.axis_index("seq") * 128, 128)
    mine = keep_ref[:, pl.ds(own, 128)]
    a, da = mine[0:64], mine[64:128]
    a_hi, da_hi = up(a), up(da)
    gap = jnp.zeros((120, 128), F32)
    aq_ref[0:128, :] = cat([a_hi, a - a_hi, mine[128:136], gap]).T.astype(BF)
    aq_ref[128:256, :] = cat([da_hi, da - da_hi, mine[136:144], gap]).T.astype(BF)

    lane = iota((128, 256), 1)
    low_s = ((lane >= 64) & (lane < 128)) | (lane == 193) | (lane == 197)
    low_d = ((lane >= 128) & (lane < 192)) | (lane == 193) | (lane == 209) | (lane == 213)
    from_q = ((lane >= 64) & (lane < 128)) | (lane >= 200)
    lane = iota((256, 256), 1)
    low_r = ((lane >= 64) & (lane < 128)) | (lane >= 208)
    l = iota((72, HD), 1)

    def times(g, block):
        return n_ref[g, 320:368].astype(F32)[8 * block : 8 * block + 8]

    def scores(g):
        s_ref, d_ref = scratch[4 * (g % 2) : 4 * (g % 2) + 2]
        made = {}

        def absorb(h):
            first = cat([n_ref[g, 0:64].astype(F32), times(g, 0)])
            second = cat([n_ref[g, 64:128].astype(F32), times(g, 1)])
            block = (first, pltpu.roll(first, 64, 1), second)[h]
            swapped = (pltpu.roll(first, 64, 1), first, pltpu.roll(second, 64, 1))[h]
            early = pltpu.roll(second, HD - 8 * h, 1) if h else second
            late = pltpu.roll(second, 16 - 8 * h, 1) if h < 2 else second
            again = jnp.where(
                l < 64, block, jnp.where(l < 72, early, jnp.where((l >= 80) & (l < 88), late, 0.0))
            )
            b = cat([jnp.where(l < 64, block, swapped), again], 1)
            b = cat([b, jnp.zeros((8, 256), F32)]).astype(BF)
            b = cat([b[:64], b[:64], b[64:], zero(112, 256)])
            absorbed = dot(aq_ref[...], b) * (LOG2E * HD ** -0.5)
            hi = absorbed.astype(BF).astype(F32)
            lo = absorbed - hi
            x = jnp.where(low_s, lo[:128], hi[:128]).astype(BF)
            low = jnp.where(from_q, lo[:128], lo[128:])
            high = jnp.where(from_q, hi[:128], hi[128:])
            made[h] = (x, jnp.where(low_d, low, high).astype(BF))

        def score(j, which):
            cols = slice(j * 256, (j + 1) * 256)
            x = cat([made[h][which] for h in range(heads)])
            if which == 0:
                s_ref[:, cols] = dot(x, as_ref[:, cols])
            else:
                d_ref[:, cols] = dot(x, ad_ref[:, cols])

        parts = [lambda h=h: absorb(h) for h in range(heads)]
        tiles = as_ref.shape[1] // 256
        return parts + [lambda j=j, w=w: score(j, w) for w in (0, 1) for j in range(tiles)]

    def softmax(g):
        s_ref, d_ref, et_ref, l_ref = scratch[4 * (g % 2) : 4 * (g % 2) + 4]

        def step(i):
            r = slice(i * chunk, (i + 1) * chunk)
            s = s_ref[r]
            e = jnp.exp2(s - jnp.max(s, axis=1, keepdims=True))
            d = d_ref[r]
            inv = 1.0 / jnp.sum(e, axis=1, keepdims=True)
            mean = jnp.sum(e * d, axis=1, keepdims=True) * inv
            et_ref[r] = e.astype(BF)
            et_ref[rows + i * chunk : rows + (i + 1) * chunk] = (e * (d - mean)).astype(BF)
            l_ref[r] = jnp.broadcast_to(inv, (chunk, 128))

        return [lambda i=i: step(i) for i in range(rows // chunk)]

    def outputs(g):
        et_ref, l_ref = scratch[4 * (g % 2) + 2 : 4 * (g % 2) + 4]
        made = {}

        def mixing():
            made[0] = cat([dot(et_ref[k * 128 : (k + 1) * 128], av_ref[...]) for k in range(2 * heads)])

        def output(h):
            mixes = made[0]
            at = 128 + h * 64
            mv = n_ref[g, at : at + 64]
            t = times(g, 2 + h)
            blank = jnp.zeros((8, HD), F32)
            early, late = cat([t, blank]).astype(BF), cat([blank, t]).astype(BF)
            inv = l_ref[h * 128 : (h + 1) * 128, 0:1]
            mix = mixes[h * 128 : (h + 1) * 128] * inv
            mix_t = mixes[rows + h * 128 : rows + (h + 1) * 128] * (inv * LN2)
            nx = cat([mv, mv, zero(64), early, early, zero(32)])
            ny = cat([zero(128), mv, late, late, zero(32)])
            both = cat([mix, mix_t])
            hi = both.astype(BF).astype(F32)
            both = jnp.where(low_r, both - hi, hi).astype(BF)
            z = dot(both, cat([nx, ny], 1))
            cols = slice((g * heads + h) * HD, (g * heads + h + 1) * HD)
            out_ref[:, cols] = z[:128, :HD].astype(BF)
            dout_ref[:, cols] = (z[128:, :HD] + z[:128, HD:]).astype(BF)

        return [mixing] + [lambda h=h: output(h) for h in range(heads)]

    for part in scores(0):
        part()
    for g in range(peers):
        matmuls = (outputs(g - 1) if g > 0 else []) + (scores(g + 1) if g + 1 < peers else [])
        steps = softmax(g)
        done = 0
        for i, step in enumerate(steps):
            while done < len(matmuls) and done * len(steps) <= i * len(matmuls):
                matmuls[done]()
                done += 1
            step()
        for part in matmuls[done:]:
            part()
    for part in outputs(peers - 1):
        part()


def local(clip_features, enc_weight, noise_field, flow_times, embed_weight, time_weight, norm_gain, qkv_weight):
    clips = lax.axis_size("clip")
    peers = lax.axis_size("seq")
    depth = qkv_weight.shape[0]
    width = qkv_weight.shape[2]
    weight = qkv_weight.transpose(1, 0, 2)
    gain = norm_gain[None]
    shape = jax.ShapeDtypeStruct
    rows = 8 * clips
    heads = width // HD
    tokens = 128 * peers
    window = depth + 64
    half = (3 * width + 128) // 2

    partial = pl.pallas_call(
        fold_kernel,
        grid=(1,),
        out_shape=shape((rows, half), BF),
        in_specs=[SMEM, HBM, HBM, HBM],
        out_specs=whole((rows, half)),
        scratch_shapes=[
            pltpu.VMEM((64, window), BF),
            pltpu.VMEM((1, window), F32),
            pltpu.VMEM((3, depth, width), BF),
            pltpu.SemaphoreType.DMA((5,)),
        ],
        compiler_params=params(),
        name="fold",
    )(flow_times, embed_weight, gain, weight)
    got = lax.all_to_all(partial.reshape(clips, 8, -1), "clip", 0, 0, tiled=True).reshape(rows, -1)

    conv = pl.pallas_call(
        conv_kernel,
        grid=(1,),
        out_shape=shape((192, 128), BF),
        in_specs=[HBM, HBM, HBM, ANY],
        out_specs=whole((192, 128)),
        scratch_shapes=[
            pltpu.VMEM((512, 3 * 384), BF),
            pltpu.VMEM((144, 3 * 384), BF),
            pltpu.VMEM((4, 128, 384), BF),
            pltpu.VMEM((432, 384), BF),
            pltpu.VMEM((4, 2, 16, 64), F32),
            pltpu.SemaphoreType.DMA((3,)),
        ],
        compiler_params=params(),
        name="conv",
    )(
        clip_features.reshape(4, 128, 384),
        enc_weight.transpose(0, 1, 2, 4, 3).reshape(432, 384),
        noise_field[0].transpose(0, 1, 3, 2),
        partial,
    )
    got, conv = lax.optimization_barrier((got, conv))

    second = pl.pallas_call(
        time_kernel,
        grid=(1,),
        out_shape=shape((rows, 3 * width), BF),
        in_specs=[ANY, HBM, HBM, HBM],
        out_specs=whole((rows, 3 * width)),
        scratch_shapes=[
            pltpu.VMEM((rows, half), BF),
            pltpu.VMEM((TFEAT, window), BF),
            pltpu.VMEM((1, window), F32),
            pltpu.VMEM((3, depth, width), BF),
            pltpu.SemaphoreType.DMA((6,)),
        ],
        compiler_params=params(62),
        name="time_rows",
    )(got, time_weight, gain, weight)
    got = lax.all_to_all(second.reshape(clips, 8, -1), "clip", 0, 0, tiled=True).reshape(rows, -1)

    gram = pl.pallas_call(
        gram_kernel,
        grid=(1,),
        out_shape=shape((72, 128), F32),
        in_specs=[SMEM, HBM, HBM, ANY],
        out_specs=whole((72, 128)),
        scratch_shapes=[
            pltpu.VMEM(embed_weight.shape, BF),
            pltpu.VMEM(time_weight.shape, BF),
            pltpu.SemaphoreType.DMA((2,)),
        ],
        compiler_params=params(),
        name="gram",
    )(flow_times, embed_weight, time_weight, second)
    got, gram = lax.optimization_barrier((got, gram))

    folded = pl.pallas_call(
        head_rows_kernel,
        grid=(1,),
        out_shape=shape((peers, 560, 128), BF),
        in_specs=[whole((rows, 3 * width)), whole((192, 128))],
        out_specs=whole((peers, 560, 128)),
        compiler_params=params(24),
        name="head_rows",
    )(got, conv)
    every = lax.all_to_all(folded, "seq", 0, 0, tiled=True)

    out, dout = pl.pallas_call(
        attention_kernel,
        grid=(1,),
        out_shape=[shape((128, peers * width), BF)] * 2,
        in_specs=[SMEM, whole((peers, 560, 128)), whole((72, 128))],
        out_specs=[whole((128, peers * width))] * 2,
        scratch_shapes=[pltpu.VMEM((144, tokens), F32), pltpu.VMEM((256, 256), BF)]
        + [pltpu.VMEM((256, tokens), BF)] * 2
        + [pltpu.VMEM((tokens, 256), BF)]
        + [
            pltpu.VMEM((heads * 128, tokens), F32),
            pltpu.VMEM((heads * 128, tokens), F32),
            pltpu.VMEM((2 * heads * 128, tokens), BF),
            pltpu.VMEM((heads * 128, 128), F32),
        ]
        * 2,
        compiler_params=params(),
        name="attention",
    )(flow_times, every, gram)
    return (out[None], dout[None])


def solution(mesh):
    placed = (
        P("clip", None, "seq", None, None),
        P(),
        P("clip", None, "seq", None, None),
        P("clip", None),
        P(),
        P(),
        P(),
        P("clip", None, "seq"),
    )
    return jax.shard_map(
        local,
        mesh=mesh,
        in_specs=placed,
        out_specs=(P("clip", "seq", None), P("clip", "seq", None)),
        check_vma=False,
    )
```

```python
import jax
import jax.numpy as jnp
import numpy as np
from jax import lax
from jax.experimental import pallas as pl
from jax.experimental.pallas import tpu as pltpu
from jax.sharding import PartitionSpec as P

D = 5120
HD = 128
TFEAT = 256
TGRID = 1000
EPSILON = 1e-06
QUARTER = TFEAT // 4
F32 = jnp.float32
BF = jnp.bfloat16
HIGH = lax.Precision.HIGHEST
LOG2E = 1.4426950408889634
LN2 = 0.6931471805599453
VMEM = pl.BlockSpec(memory_space=pltpu.VMEM)
SMEM = pl.BlockSpec(memory_space=pltpu.SMEM)
ANY = pl.BlockSpec(memory_space=pl.ANY)
HBM = pl.BlockSpec(memory_space=pltpu.HBM)


def whole(shape):
    return pl.BlockSpec(shape, lambda i: (0,) * len(shape))


def params(limit=63):
    return pltpu.CompilerParams(vmem_limit_bytes=limit * 1024 * 1024)


def dot(a, b, dims=((1,), (0,)), precision=None):
    return lax.dot_general(a, b, (dims, ((), ())), preferred_element_type=F32, precision=precision)


def split(x):
    hi = x.astype(BF)
    return hi, (x - hi.astype(F32)).astype(BF)


def iota(shape, axis):
    return lax.broadcasted_iota(jnp.int32, shape, axis)


def fold_kernel(flow_ref, embed_ref, gain_ref, weight_ref, out_ref, e_ref, g_ref, w_ref, sems):
    rows = out_ref.shape[0]
    _, depth, width = weight_ref.shape
    window = e_ref.shape[1]
    at_clip = lax.axis_index("clip")
    odd = at_clip % 2
    base = pl.multiple_of(at_clip * depth - odd * 64, 128)
    copies = [
        pltpu.make_async_copy(embed_ref.at[:, pl.ds(base, window)], e_ref, sems.at[0]),
        pltpu.make_async_copy(gain_ref.at[:, pl.ds(base, window)], g_ref, sems.at[1]),
    ] + [pltpu.make_async_copy(weight_ref.at[i], w_ref.at[i], sems.at[2 + i]) for i in range(3)]
    for copy in copies:
        copy.start()
    lane = iota((rows, 128), 1)
    start, finish = flow_ref[0, 0], flow_ref[0, 1]
    coded = jnp.where(
        lane == 0,
        start // 256,
        jnp.where(lane == 1, start % 256, jnp.where(lane == 2, finish // 256, finish % 256)),
    )
    row, col = iota((rows, 64), 0), iota((rows, 64), 1)
    twice = jnp.where(col == (row // 8) * 4 + row % 4, 1.0, 0.0).astype(BF)
    copies[0].wait()
    copies[1].wait()
    scaled = dot(twice, e_ref[...]) * g_ref[...]
    scaled = jnp.where(odd == 1, scaled[:, 64 : 64 + depth], scaled[:, :depth])
    scaled_hi, scaled_lo = split(scaled)
    first = (iota((rows, 1), 0) // 4) % 2 == 0
    totals = []
    for i in range(3):
        copies[2 + i].wait()
        totals.append(dot(scaled_hi, w_ref[i]) + dot(scaled_lo, w_ref[i]))
    total = jnp.concatenate(totals + [coded.astype(F32)], axis=1)
    half = out_ref.shape[1]
    out_ref[...] = jnp.where(first, total[:, :half], total[:, half:]).astype(BF)


def frequencies():
    k = iota((1, 128), 1) % QUARTER
    return 8.0 * jnp.exp(k.astype(F32) * np.float32(-np.log(100.0) / QUARTER))


def time_kernel(got_ref, time_ref, gain_ref, weight_ref, out_ref, r_ref, t_ref, g_ref, w_ref, sems):
    rows = out_ref.shape[0]
    groups = rows // 8
    _, depth, width = weight_ref.shape
    window = t_ref.shape[1]
    at_clip = lax.axis_index("clip")
    odd = at_clip % 2
    base = pl.multiple_of(at_clip * depth - odd * 64, 128)
    copies = [
        pltpu.make_async_copy(got_ref, r_ref, sems.at[0]),
        pltpu.make_async_copy(gain_ref.at[:, pl.ds(base, window)], g_ref, sems.at[1]),
        pltpu.make_async_copy(time_ref.at[:, pl.ds(base, window)], t_ref, sems.at[2]),
    ] + [pltpu.make_async_copy(weight_ref.at[i], w_ref.at[i], sems.at[3 + i]) for i in range(3)]
    for copy in copies:
        copy.start()
    freqs = frequencies()
    half_width = r_ref.shape[1]
    copies[0].wait()
    codes = r_ref[:, 3 * width - half_width :].astype(F32)
    start = (codes[:, 0:1] * 256.0 + codes[:, 1:2]) / TGRID
    finish = (codes[:, 2:3] * 256.0 + codes[:, 3:4]) / TGRID
    half = iota((rows, 128), 1) < QUARTER
    angle = freqs * jnp.where(half, finish, finish - start)
    sines, cosines = jnp.sin(angle), jnp.cos(angle)
    place = iota((rows, 1), 0) % 8
    is_value = (place == 4) | (place == 5)
    is_tangent = place >= 6
    first = jnp.where(is_value, sines, jnp.where(is_tangent, freqs * cosines, 0.0))
    second = jnp.where(is_value, cosines, jnp.where(is_tangent, -freqs * sines, 0.0))
    first_hi, first_lo = split(first)
    second_hi, second_lo = split(second)
    copies[1].wait()
    copies[2].wait()
    q = QUARTER
    t_first = jnp.concatenate([t_ref[0:q], t_ref[2 * q : 3 * q]], axis=0)
    t_second = jnp.concatenate([t_ref[q : 2 * q], t_ref[3 * q : 4 * q]], axis=0)
    tau = dot(first_hi, t_first) + dot(first_lo, t_first) + dot(second_hi, t_second) + dot(second_lo, t_second)
    tau = tau * g_ref[...]
    tau = jnp.where(odd == 1, tau[:, 64 : 64 + depth], tau[:, :depth])
    tau_hi, tau_lo = split(tau)
    keep_hi = place % 2 == 0
    summed = r_ref[...].astype(F32).reshape(groups, 8, half_width).sum(axis=0)
    turned = jnp.concatenate([summed[4:], summed[:4]], axis=0)
    summed = jnp.concatenate([summed, turned], axis=1)
    for i in range(3):
        cols = slice(i * width, (i + 1) * width)
        copies[3 + i].wait()
        w = w_ref[i]
        part = dot(tau_hi, w) + dot(tau_lo, w)
        hi = part.astype(BF).astype(F32)
        part = jnp.where(keep_hi, hi, part - hi)
        mine = jnp.concatenate([summed[:, cols]] * groups, axis=0)
        out_ref[:, cols] = jnp.where(place < 4, mine, part).astype(BF)


def head_rows_kernel(got_ref, conv_ref, out_ref):
    rows = got_ref.shape[0]
    heads = 3
    row, col = iota((128, rows), 0), iota((128, rows), 1)
    patch = (row < 64) & (col == (row // 4) * 8 + row % 4)
    place = col % 8
    value = (row >= 64) & (row < 68) & ((place == 4) | (place == 5))
    tangent = (row >= 68) & (row < 72) & (place >= 6)
    pick = jnp.where(patch | value | tangent, 1.0, 0.0).astype(BF)
    total = dot(pick, got_ref[...])
    width = total.shape[1] // 3
    low_row = lambda r: (r == 67) | (r == 71)
    r, l = iota((80, HD), 0), iota((80, HD), 1)
    products, values = [], []
    for h in range(heads):
        part = lambda i: total[:, i * width + h * HD : i * width + (h + 1) * HD]
        q_hi, q_lo = split(part(0)[:80])
        k_hi, k_lo = split(part(1))
        nt = ((1,), (1,))
        product = dot(q_hi, k_hi, nt) + dot(q_lo, k_hi, nt) + dot(q_hi, k_lo, nt)
        hi = product.astype(BF).astype(F32)
        lo = product - hi
        product = jnp.where(low_row(l), jnp.where(r < 64, lo, 0.0), jnp.where(low_row(r), lo, hi))
        products.append(product)
        v = part(2)[:80]
        v_hi = v.astype(BF).astype(F32)
        values.append(jnp.where(low_row(r), v - v_hi, v_hi))
    one, two, three = products
    first = jnp.where(l < 64, one, pltpu.roll(two, 64, 1))
    second = jnp.where(
        l < 64,
        three,
        jnp.where(
            l < 72,
            one,
            jnp.where(l < 80, pltpu.roll(two, 8, 1), jnp.where(l < 88, pltpu.roll(three, 16, 1), 0.0)),
        ),
    )
    blocks = [first, second] + values
    times = jnp.concatenate([b[64:72] for b in blocks] + [jnp.zeros((8, HD), F32)], axis=0).astype(BF)
    for i in range(out_ref.shape[0]):
        for b, block in enumerate(blocks):
            out_ref[i, b * 64 : (b + 1) * 64, :] = block[:64].astype(BF)
        out_ref[i, 320:368, :] = times
        out_ref[i, 368:560, :] = conv_ref[...]


def conv_kernel(x_hbm, w_hbm, noise_hbm, after_ref, out_ref, xp_ref, wt_ref, x_ref, w_ref, noise_ref, sems):
    copies = [
        pltpu.make_async_copy(x_hbm, x_ref, sems.at[0]),
        pltpu.make_async_copy(w_hbm, w_ref, sems.at[1]),
        pltpu.make_async_copy(noise_hbm, noise_ref, sems.at[2]),
    ]
    for copy in copies:
        copy.start()
    for copy in copies:
        copy.wait()
    chans = x_ref.shape[2]
    row, col = iota((128, 128), 0), iota((128, 128), 1)
    row_w = 2 * (row % 32) + (row // 32) % 2
    same = (row // 64) == (col // 64)
    for e in range(3):
        perm = jnp.where(same & (col % 64 == row_w + (e - 1)), 1.0, 0.0).astype(BF)
        for f in range(4):
            moved = dot(perm, x_ref[f]).astype(BF)
            for g in range(4):
                xp_ref[g * 128 + f * 32 : g * 128 + f * 32 + 32, e * chans : (e + 1) * chans] = moved[
                    g * 32 : g * 32 + 32
                ]
        for ab in range(9):
            tap = (ab * 3 + e) * 16
            wt_ref[ab * 16 : ab * 16 + 16, e * chans : (e + 1) * chans] = w_ref[tap : tap + 16, :]
    y = dot(wt_ref[...], xp_ref[...], ((1,), (1,)))
    lane = iota((16, 128), 1)

    def part(a, b, p, q):
        at = (a * 3 + b) * 16
        g = p * 2 + q
        return y[at : at + 16, g * 128 : (g + 1) * 128]

    def frames(of):
        one = jnp.where(lane >= 32, pltpu.roll(of(1), 32, 1), 0.0)
        two = jnp.where(lane >= 64, pltpu.roll(of(0), 64, 1), 0.0)
        return of(2) + one + two

    for q in range(2):
        own0 = frames(lambda a: part(a, 1, 0, q) + part(a, 2, 1, q))
        own1 = frames(lambda a: part(a, 0, 0, q) + part(a, 1, 1, q))
        down = frames(lambda a: part(a, 0, 1, q))
        up = frames(lambda a: part(a, 2, 0, q))
        out_ref[q * 16 : q * 16 + 16, :] = own0.astype(BF)
        out_ref[32 + q * 16 : 48 + q * 16, :] = own1.astype(BF)
        out_ref[128 + q * 16 : 144 + q * 16, :] = down.astype(BF)
        out_ref[160 + q * 16 : 176 + q * 16, :] = up.astype(BF)
    r2, c2 = iota((256, 256), 0), iota((256, 256), 1)
    spread = ((r2 // 64) == (c2 // 32) % 4) & (r2 % 64 == 2 * (c2 % 32) + c2 // 128)
    spread = jnp.where(spread, 1.0, 0.0)
    noise = jnp.concatenate(
        [jnp.concatenate([noise_ref[f, p] for f in range(4)], axis=1) for p in range(2)], axis=0
    )
    moved = dot(noise, spread, precision=HIGH)
    for p in range(2):
        for q in range(2):
            at = 64 + (p * 2 + q) * 16
            out_ref[at : at + 16, :] = moved[p * 16 : p * 16 + 16, q * 128 : (q + 1) * 128].astype(BF)


def gram_kernel(flow_ref, embed_hbm, time_hbm, after_ref, out_ref, embed_ref, time_ref, sems):
    copies = [
        pltpu.make_async_copy(time_hbm, time_ref, sems.at[0]),
        pltpu.make_async_copy(embed_hbm, embed_ref, sems.at[1]),
    ]
    for copy in copies:
        copy.start()
    start = flow_ref[0, 0].astype(F32) / TGRID
    finish = flow_ref[0, 1].astype(F32) / TGRID
    freqs = frequencies()
    angle = freqs * jnp.where(iota((8, 128), 1) < QUARTER, finish, finish - start)
    sines, cosines = jnp.sin(angle), jnp.cos(angle)
    row = iota((8, 128), 0)
    first = jnp.where(row == 0, sines, jnp.where(row == 1, freqs * cosines, 0.0))
    second = jnp.where(row == 0, cosines, jnp.where(row == 1, -freqs * sines, 0.0))
    q = QUARTER
    feats = jnp.concatenate([first[:, :q], second[:, :q], first[:, q:], second[:, q:]], axis=1)
    feat_hi, feat_lo = split(feats)
    feat_mid = (feats - feat_hi.astype(F32) - feat_lo.astype(F32)).astype(BF)
    feats = jnp.concatenate([feat_hi, feat_lo, feat_mid, jnp.zeros_like(feat_hi)], axis=0)
    for copy in copies:
        copy.wait()
    tau = dot(feats, time_ref[...])
    tau = tau[0:8] + tau[8:16] + tau[16:24]
    embed = embed_ref[...]
    out_ref[0:64, 0:64] = dot(embed, embed, ((1,), (1,)))
    tau_hi, tau_lo = split(tau)
    tau_mid = (tau - tau_hi.astype(F32) - tau_lo.astype(F32)).astype(BF)
    taus = jnp.concatenate([tau_hi, tau_lo, tau_mid, jnp.zeros_like(tau_hi)], axis=0)
    cross = dot(embed, taus, ((1,), (1,)))
    out_ref[0:64, 64:128] = jnp.concatenate(
        [cross[:, 0:8] + cross[:, 8:16] + cross[:, 16:24], jnp.zeros((64, 56), F32)], axis=1
    )
    out_ref[64:72, :] = jnp.sum(tau * tau[0:1], axis=1, keepdims=True) + jnp.zeros((8, 128), F32)


def time_coefs(s_hi, s_lo, c_hi, c_lo, kind):
    r = iota((8, s_hi.shape[1]), 0)

    def coefs(high, low):
        if kind == 0:
            return jnp.where((r % 4 == 0) | (r % 4 == 3), high, jnp.where(r % 4 == 1, low, 0.0))
        return jnp.where(r % 4 == 2, low, high)

    plain = jnp.where(r < 4, coefs(s_hi, s_lo), 0.0)
    tangent = jnp.where(r < 4, coefs(c_hi, c_lo), coefs(s_hi, s_lo))
    return plain, tangent


def attention_kernel(flow_ref, n_ref, gram_ref, out_ref, dout_ref, keep_ref, aq_ref, as_ref, ad_ref, av_ref, *scratch):
    peers = n_ref.shape[0]
    tokens = peers * 128
    heads = 3
    rows = heads * 128
    chunk = 16
    zero = lambda r, c=HD: jnp.zeros((r, c), BF)
    cat = lambda xs, axis=0: jnp.concatenate(xs, axis=axis)
    up = lambda x: x.astype(BF).astype(F32)

    flow_t = flow_ref[0, 1].astype(F32) / TGRID
    patches, tangents = [], []
    none = jnp.zeros((32, 128), F32)
    for i in range(peers):
        above = n_ref[i - 1, 496:528].astype(F32) if i > 0 else none
        below = n_ref[i + 1, 528:560].astype(F32) if i + 1 < peers else none
        latent = n_ref[i, 368:432].astype(F32) + cat([above, below])
        noise = n_ref[i, 432:496].astype(F32)
        patches.append((1.0 - flow_t) * latent + flow_t * noise)
        tangents.append(noise - latent)
    p, dp = cat(patches, 1), cat(tangents, 1)
    gp = dot(gram_ref[0:64, 0:64], p, precision=HIGH)
    e_tau, e_dtau = gram_ref[0:64, 64:65], gram_ref[0:64, 65:66]
    mean_sq = jnp.sum(p * (gp + 2.0 * e_tau), axis=0, keepdims=True) + gram_ref[64:65, 0:1]
    mean_sq = jnp.maximum(mean_sq * (1.0 / D), 0.0)
    mixed = jnp.sum(gp * dp + p * e_dtau + dp * e_tau, axis=0, keepdims=True) + gram_ref[65:66, 0:1]
    s = lax.rsqrt(mean_sq + EPSILON)
    c = -(s * s * s) * (mixed * (1.0 / D))
    a = p * s
    da = dp * s + p * c
    a_hi, da_hi = up(a), up(da)
    s_hi, c_hi = up(s), up(c)
    coefs = (s_hi, s - s_hi, c_hi, c - c_hi)
    m_s, m_d = time_coefs(*coefs, 1)
    v_s, v_d = time_coefs(*coefs, 0)
    gap = lambda n: jnp.zeros((n, tokens), F32)
    as_ref[...] = cat([a_hi, a_hi, a - a_hi, m_s, gap(56)]).astype(BF)
    ad_ref[...] = cat([a_hi, da_hi, a_hi, m_s, gap(8), m_d, gap(40)]).astype(BF)
    av_ref[...] = cat([a_hi, a_hi, da_hi, v_s, v_d, v_s, v_d, gap(32)]).T.astype(BF)
    keep_ref[...] = cat([a, da, v_s, v_d])
    own = pl.multiple_of(lax.axis_index("seq") * 128, 128)
    mine = keep_ref[:, pl.ds(own, 128)]
    a, da = mine[0:64], mine[64:128]
    a_hi, da_hi = up(a), up(da)
    gap = jnp.zeros((120, 128), F32)
    aq_ref[0:128, :] = cat([a_hi, a - a_hi, mine[128:136], gap]).T.astype(BF)
    aq_ref[128:256, :] = cat([da_hi, da - da_hi, mine[136:144], gap]).T.astype(BF)

    lane = iota((128, 256), 1)
    low_s = ((lane >= 64) & (lane < 128)) | (lane == 193) | (lane == 197)
    low_d = ((lane >= 128) & (lane < 192)) | (lane == 193) | (lane == 209) | (lane == 213)
    from_q = ((lane >= 64) & (lane < 128)) | (lane >= 200)
    lane = iota((256, 256), 1)
    low_r = ((lane >= 64) & (lane < 128)) | (lane >= 208)
    l = iota((72, HD), 1)

    def times(g, block):
        return n_ref[g, 320:368].astype(F32)[8 * block : 8 * block + 8]

    def scores(g):
        s_ref, d_ref = scratch[4 * (g % 2) : 4 * (g % 2) + 2]
        made = {}

        def absorb(h):
            first = cat([n_ref[g, 0:64].astype(F32), times(g, 0)])
            second = cat([n_ref[g, 64:128].astype(F32), times(g, 1)])
            block = (first, pltpu.roll(first, 64, 1), second)[h]
            swapped = (pltpu.roll(first, 64, 1), first, pltpu.roll(second, 64, 1))[h]
            early = pltpu.roll(second, HD - 8 * h, 1) if h else second
            late = pltpu.roll(second, 16 - 8 * h, 1) if h < 2 else second
            again = jnp.where(
                l < 64, block, jnp.where(l < 72, early, jnp.where((l >= 80) & (l < 88), late, 0.0))
            )
            b = cat([jnp.where(l < 64, block, swapped), again], 1)
            b = cat([b, jnp.zeros((8, 256), F32)]).astype(BF)
            b = cat([b[:64], b[:64], b[64:], zero(112, 256)])
            absorbed = dot(aq_ref[...], b) * (LOG2E * HD ** -0.5)
            hi = absorbed.astype(BF).astype(F32)
            lo = absorbed - hi
            x = jnp.where(low_s, lo[:128], hi[:128]).astype(BF)
            low = jnp.where(from_q, lo[:128], lo[128:])
            high = jnp.where(from_q, hi[:128], hi[128:])
            made[h] = (x, jnp.where(low_d, low, high).astype(BF))

        def score(j, which):
            cols = slice(j * 256, (j + 1) * 256)
            x = cat([made[h][which] for h in range(heads)])
            if which == 0:
                s_ref[:, cols] = dot(x, as_ref[:, cols])
            else:
                d_ref[:, cols] = dot(x, ad_ref[:, cols])

        parts = [lambda h=h: absorb(h) for h in range(heads)]
        tiles = as_ref.shape[1] // 256
        return parts + [lambda j=j, w=w: score(j, w) for w in (0, 1) for j in range(tiles)]

    def softmax(g):
        s_ref, d_ref, et_ref, l_ref = scratch[4 * (g % 2) : 4 * (g % 2) + 4]

        def step(i):
            r = slice(i * chunk, (i + 1) * chunk)
            s = s_ref[r]
            e = jnp.exp2(s - jnp.max(s, axis=1, keepdims=True))
            d = d_ref[r]
            inv = 1.0 / jnp.sum(e, axis=1, keepdims=True)
            mean = jnp.sum(e * d, axis=1, keepdims=True) * inv
            et_ref[r] = e.astype(BF)
            et_ref[rows + i * chunk : rows + (i + 1) * chunk] = (e * (d - mean)).astype(BF)
            l_ref[r] = jnp.broadcast_to(inv, (chunk, 128))

        return [lambda i=i: step(i) for i in range(rows // chunk)]

    def outputs(g):
        et_ref, l_ref = scratch[4 * (g % 2) + 2 : 4 * (g % 2) + 4]
        made = {}

        def mixing():
            made[0] = cat([dot(et_ref[k * 128 : (k + 1) * 128], av_ref[...]) for k in range(2 * heads)])

        def output(h):
            mixes = made[0]
            at = 128 + h * 64
            mv = n_ref[g, at : at + 64]
            t = times(g, 2 + h)
            blank = jnp.zeros((8, HD), F32)
            early, late = cat([t, blank]).astype(BF), cat([blank, t]).astype(BF)
            inv = l_ref[h * 128 : (h + 1) * 128, 0:1]
            mix = mixes[h * 128 : (h + 1) * 128] * inv
            mix_t = mixes[rows + h * 128 : rows + (h + 1) * 128] * (inv * LN2)
            nx = cat([mv, mv, zero(64), early, early, zero(32)])
            ny = cat([zero(128), mv, late, late, zero(32)])
            both = cat([mix, mix_t])
            hi = both.astype(BF).astype(F32)
            both = jnp.where(low_r, both - hi, hi).astype(BF)
            z = dot(both, cat([nx, ny], 1))
            cols = slice((g * heads + h) * HD, (g * heads + h + 1) * HD)
            out_ref[:, cols] = z[:128, :HD].astype(BF)
            dout_ref[:, cols] = (z[128:, :HD] + z[:128, HD:]).astype(BF)

        return [mixing] + [lambda h=h: output(h) for h in range(heads)]

    for part in scores(0):
        part()
    for g in range(peers):
        matmuls = (outputs(g - 1) if g > 0 else []) + (scores(g + 1) if g + 1 < peers else [])
        steps = softmax(g)
        done = 0
        for i, step in enumerate(steps):
            while done < len(matmuls) and done * len(steps) <= i * len(matmuls):
                matmuls[done]()
                done += 1
            step()
        for part in matmuls[done:]:
            part()
    for part in outputs(peers - 1):
        part()


def local(clip_features, enc_weight, noise_field, flow_times, embed_weight, time_weight, norm_gain, qkv_weight):
    clips = lax.axis_size("clip")
    peers = lax.axis_size("seq")
    depth = qkv_weight.shape[0]
    width = qkv_weight.shape[2]
    weight = qkv_weight.transpose(1, 0, 2)
    gain = norm_gain[None]
    shape = jax.ShapeDtypeStruct
    rows = 8 * clips
    heads = width // HD
    tokens = 128 * peers
    window = depth + 64
    half = (3 * width + 128) // 2

    partial = pl.pallas_call(
        fold_kernel,
        grid=(1,),
        out_shape=shape((rows, half), BF),
        in_specs=[SMEM, HBM, HBM, HBM],
        out_specs=whole((rows, half)),
        scratch_shapes=[
            pltpu.VMEM((64, window), BF),
            pltpu.VMEM((1, window), F32),
            pltpu.VMEM((3, depth, width), BF),
            pltpu.SemaphoreType.DMA((5,)),
        ],
        compiler_params=params(),
        name="fold",
    )(flow_times, embed_weight, gain, weight)
    got = lax.all_to_all(partial.reshape(clips, 8, -1), "clip", 0, 0, tiled=True).reshape(rows, -1)

    conv = pl.pallas_call(
        conv_kernel,
        grid=(1,),
        out_shape=shape((192, 128), BF),
        in_specs=[HBM, HBM, HBM, ANY],
        out_specs=whole((192, 128)),
        scratch_shapes=[
            pltpu.VMEM((512, 3 * 384), BF),
            pltpu.VMEM((144, 3 * 384), BF),
            pltpu.VMEM((4, 128, 384), BF),
            pltpu.VMEM((432, 384), BF),
            pltpu.VMEM((4, 2, 16, 64), F32),
            pltpu.SemaphoreType.DMA((3,)),
        ],
        compiler_params=params(),
        name="conv",
    )(
        clip_features.reshape(4, 128, 384),
        enc_weight.transpose(0, 1, 2, 4, 3).reshape(432, 384),
        noise_field[0].transpose(0, 1, 3, 2),
        partial,
    )
    got, conv = lax.optimization_barrier((got, conv))

    second = pl.pallas_call(
        time_kernel,
        grid=(1,),
        out_shape=shape((rows, 3 * width), BF),
        in_specs=[ANY, HBM, HBM, HBM],
        out_specs=whole((rows, 3 * width)),
        scratch_shapes=[
            pltpu.VMEM((rows, half), BF),
            pltpu.VMEM((TFEAT, window), BF),
            pltpu.VMEM((1, window), F32),
            pltpu.VMEM((3, depth, width), BF),
            pltpu.SemaphoreType.DMA((6,)),
        ],
        compiler_params=params(60),
        name="time_rows",
    )(got, time_weight, gain, weight)
    got = lax.all_to_all(second.reshape(clips, 8, -1), "clip", 0, 0, tiled=True).reshape(rows, -1)

    gram = pl.pallas_call(
        gram_kernel,
        grid=(1,),
        out_shape=shape((72, 128), F32),
        in_specs=[SMEM, HBM, HBM, ANY],
        out_specs=whole((72, 128)),
        scratch_shapes=[
            pltpu.VMEM(embed_weight.shape, BF),
            pltpu.VMEM(time_weight.shape, BF),
            pltpu.SemaphoreType.DMA((2,)),
        ],
        compiler_params=params(),
        name="gram",
    )(flow_times, embed_weight, time_weight, second)
    got, gram = lax.optimization_barrier((got, gram))

    folded = pl.pallas_call(
        head_rows_kernel,
        grid=(1,),
        out_shape=shape((peers, 560, 128), BF),
        in_specs=[whole((rows, 3 * width)), whole((192, 128))],
        out_specs=whole((peers, 560, 128)),
        compiler_params=params(24),
        name="head_rows",
    )(got, conv)
    every = lax.all_to_all(folded, "seq", 0, 0, tiled=True)

    out, dout = pl.pallas_call(
        attention_kernel,
        grid=(1,),
        out_shape=[shape((128, peers * width), BF)] * 2,
        in_specs=[SMEM, whole((peers, 560, 128)), whole((72, 128))],
        out_specs=[whole((128, peers * width))] * 2,
        scratch_shapes=[pltpu.VMEM((144, tokens), F32), pltpu.VMEM((256, 256), BF)]
        + [pltpu.VMEM((256, tokens), BF)] * 2
        + [pltpu.VMEM((tokens, 256), BF)]
        + [
            pltpu.VMEM((heads * 128, tokens), F32),
            pltpu.VMEM((heads * 128, tokens), F32),
            pltpu.VMEM((2 * heads * 128, tokens), BF),
            pltpu.VMEM((heads * 128, 128), F32),
        ]
        * 2,
        compiler_params=params(),
        name="attention",
    )(flow_times, every, gram)
    return (out[None], dout[None])


def solution(mesh):
    placed = (
        P("clip", None, "seq", None, None),
        P(),
        P("clip", None, "seq", None, None),
        P("clip", None),
        P(),
        P(),
        P(),
        P("clip", None, "seq"),
    )
    return jax.shard_map(
        local,
        mesh=mesh,
        in_specs=placed,
        out_specs=(P("clip", "seq", None), P("clip", "seq", None)),
        check_vma=False,
    )
```

```python
import jax
import jax.numpy as jnp
import numpy as np
from jax import lax
from jax.experimental import pallas as pl
from jax.experimental.pallas import tpu as pltpu
from jax.sharding import PartitionSpec as P

D = 5120
HD = 128
TFEAT = 256
TGRID = 1000
EPSILON = 1e-06
QUARTER = TFEAT // 4
F32 = jnp.float32
BF = jnp.bfloat16
HIGH = lax.Precision.HIGHEST
LOG2E = 1.4426950408889634
LN2 = 0.6931471805599453
VMEM = pl.BlockSpec(memory_space=pltpu.VMEM)
SMEM = pl.BlockSpec(memory_space=pltpu.SMEM)
ANY = pl.BlockSpec(memory_space=pl.ANY)
HBM = pl.BlockSpec(memory_space=pltpu.HBM)


def whole(shape):
    return pl.BlockSpec(shape, lambda i: (0,) * len(shape))


def params(limit=63):
    return pltpu.CompilerParams(vmem_limit_bytes=limit * 1024 * 1024)


def dot(a, b, dims=((1,), (0,)), precision=None):
    return lax.dot_general(a, b, (dims, ((), ())), preferred_element_type=F32, precision=precision)


def split(x):
    hi = x.astype(BF)
    return hi, (x - hi.astype(F32)).astype(BF)


def iota(shape, axis):
    return lax.broadcasted_iota(jnp.int32, shape, axis)


def fold_kernel(flow_ref, embed_ref, gain_ref, weight_ref, out_ref, e_ref, g_ref, w_ref, sems):
    rows = out_ref.shape[0]
    _, depth, width = weight_ref.shape
    window = e_ref.shape[1]
    at_clip = lax.axis_index("clip")
    odd = at_clip % 2
    base = pl.multiple_of(at_clip * depth - odd * 64, 128)
    copies = [
        pltpu.make_async_copy(embed_ref.at[:, pl.ds(base, window)], e_ref, sems.at[0]),
        pltpu.make_async_copy(gain_ref.at[:, pl.ds(base, window)], g_ref, sems.at[1]),
    ] + [pltpu.make_async_copy(weight_ref.at[i], w_ref.at[i], sems.at[2 + i]) for i in range(3)]
    for copy in copies:
        copy.start()
    lane = iota((rows, 128), 1)
    start, finish = flow_ref[0, 0], flow_ref[0, 1]
    coded = jnp.where(
        lane == 0,
        start // 256,
        jnp.where(lane == 1, start % 256, jnp.where(lane == 2, finish // 256, finish % 256)),
    )
    row, col = iota((rows, 64), 0), iota((rows, 64), 1)
    twice = jnp.where(col == (row // 8) * 4 + row % 4, 1.0, 0.0).astype(BF)
    copies[0].wait()
    copies[1].wait()
    scaled = dot(twice, e_ref[...]) * g_ref[...]
    scaled = jnp.where(odd == 1, scaled[:, 64 : 64 + depth], scaled[:, :depth])
    scaled_hi, scaled_lo = split(scaled)
    first = (iota((rows, 1), 0) // 4) % 2 == 0
    totals = []
    for i in range(3):
        copies[2 + i].wait()
        totals.append(dot(scaled_hi, w_ref[i]) + dot(scaled_lo, w_ref[i]))
    total = jnp.concatenate(totals + [coded.astype(F32)], axis=1)
    half = out_ref.shape[1]
    out_ref[...] = jnp.where(first, total[:, :half], total[:, half:]).astype(BF)


def frequencies():
    k = iota((1, 128), 1) % QUARTER
    return 8.0 * jnp.exp(k.astype(F32) * np.float32(-np.log(100.0) / QUARTER))


def time_kernel(got_ref, time_ref, gain_ref, weight_ref, out_ref, r_ref, t_ref, g_ref, w_ref, sems):
    rows = out_ref.shape[0]
    groups = rows // 8
    _, depth, width = weight_ref.shape
    window = t_ref.shape[1]
    at_clip = lax.axis_index("clip")
    odd = at_clip % 2
    base = pl.multiple_of(at_clip * depth - odd * 64, 128)
    copies = [
        pltpu.make_async_copy(got_ref, r_ref, sems.at[0]),
        pltpu.make_async_copy(gain_ref.at[:, pl.ds(base, window)], g_ref, sems.at[1]),
        pltpu.make_async_copy(time_ref.at[:, pl.ds(base, window)], t_ref, sems.at[2]),
    ] + [pltpu.make_async_copy(weight_ref.at[i], w_ref.at[i], sems.at[3 + i]) for i in range(3)]
    for copy in copies:
        copy.start()
    freqs = frequencies()
    half_width = r_ref.shape[1]
    copies[0].wait()
    codes = r_ref[:, 3 * width - half_width :].astype(F32)
    start = (codes[:, 0:1] * 256.0 + codes[:, 1:2]) / TGRID
    finish = (codes[:, 2:3] * 256.0 + codes[:, 3:4]) / TGRID
    half = iota((rows, 128), 1) < QUARTER
    angle = freqs * jnp.where(half, finish, finish - start)
    sines, cosines = jnp.sin(angle), jnp.cos(angle)
    place = iota((rows, 1), 0) % 8
    is_value = (place == 4) | (place == 5)
    is_tangent = place >= 6
    first = jnp.where(is_value, sines, jnp.where(is_tangent, freqs * cosines, 0.0))
    second = jnp.where(is_value, cosines, jnp.where(is_tangent, -freqs * sines, 0.0))
    first_hi, first_lo = split(first)
    second_hi, second_lo = split(second)
    copies[1].wait()
    copies[2].wait()
    q = QUARTER
    t_first = jnp.concatenate([t_ref[0:q], t_ref[2 * q : 3 * q]], axis=0)
    t_second = jnp.concatenate([t_ref[q : 2 * q], t_ref[3 * q : 4 * q]], axis=0)
    tau = dot(first_hi, t_first) + dot(first_lo, t_first) + dot(second_hi, t_second) + dot(second_lo, t_second)
    tau = tau * g_ref[...]
    tau = jnp.where(odd == 1, tau[:, 64 : 64 + depth], tau[:, :depth])
    tau_hi, tau_lo = split(tau)
    keep_hi = place % 2 == 0
    summed = r_ref[...].astype(F32).reshape(groups, 8, half_width).sum(axis=0)
    turned = jnp.concatenate([summed[4:], summed[:4]], axis=0)
    summed = jnp.concatenate([summed, turned], axis=1)
    for i in range(3):
        cols = slice(i * width, (i + 1) * width)
        copies[3 + i].wait()
        w = w_ref[i]
        part = dot(tau_hi, w) + dot(tau_lo, w)
        hi = part.astype(BF).astype(F32)
        part = jnp.where(keep_hi, hi, part - hi)
        mine = jnp.concatenate([summed[:, cols]] * groups, axis=0)
        out_ref[:, cols] = jnp.where(place < 4, mine, part).astype(BF)


def head_rows_kernel(got_ref, conv_ref, out_ref):
    rows = got_ref.shape[0]
    heads = 3
    row, col = iota((128, rows), 0), iota((128, rows), 1)
    patch = (row < 64) & (col == (row // 4) * 8 + row % 4)
    place = col % 8
    value = (row >= 64) & (row < 68) & ((place == 4) | (place == 5))
    tangent = (row >= 68) & (row < 72) & (place >= 6)
    pick = jnp.where(patch | value | tangent, 1.0, 0.0).astype(BF)
    total = dot(pick, got_ref[...])
    width = total.shape[1] // 3
    low_row = lambda r: (r == 67) | (r == 71)
    r, l = iota((80, HD), 0), iota((80, HD), 1)
    products, values = [], []
    for h in range(heads):
        part = lambda i: total[:, i * width + h * HD : i * width + (h + 1) * HD]
        q_hi, q_lo = split(part(0)[:80])
        k_hi, k_lo = split(part(1))
        nt = ((1,), (1,))
        product = dot(q_hi, k_hi, nt) + dot(q_lo, k_hi, nt) + dot(q_hi, k_lo, nt)
        hi = product.astype(BF).astype(F32)
        lo = product - hi
        product = jnp.where(low_row(l), jnp.where(r < 64, lo, 0.0), jnp.where(low_row(r), lo, hi))
        products.append(product)
        v = part(2)[:80]
        v_hi = v.astype(BF).astype(F32)
        values.append(jnp.where(low_row(r), v - v_hi, v_hi))
    one, two, three = products
    first = jnp.where(l < 64, one, pltpu.roll(two, 64, 1))
    second = jnp.where(
        l < 64,
        three,
        jnp.where(
            l < 72,
            one,
            jnp.where(l < 80, pltpu.roll(two, 8, 1), jnp.where(l < 88, pltpu.roll(three, 16, 1), 0.0)),
        ),
    )
    blocks = [first, second] + values
    times = jnp.concatenate([b[64:72] for b in blocks] + [jnp.zeros((8, HD), F32)], axis=0).astype(BF)
    for i in range(out_ref.shape[0]):
        for b, block in enumerate(blocks):
            out_ref[i, b * 64 : (b + 1) * 64, :] = block[:64].astype(BF)
        out_ref[i, 320:368, :] = times
        out_ref[i, 368:560, :] = conv_ref[...]


def conv_kernel(x_hbm, w_hbm, noise_hbm, after_ref, out_ref, xp_ref, wt_ref, x_ref, w_ref, noise_ref, sems):
    copies = [
        pltpu.make_async_copy(x_hbm, x_ref, sems.at[0]),
        pltpu.make_async_copy(w_hbm, w_ref, sems.at[1]),
        pltpu.make_async_copy(noise_hbm, noise_ref, sems.at[2]),
    ]
    for copy in copies:
        copy.start()
    for copy in copies:
        copy.wait()
    chans = x_ref.shape[2]
    row, col = iota((128, 128), 0), iota((128, 128), 1)
    row_w = 2 * (row % 32) + (row // 32) % 2
    same = (row // 64) == (col // 64)
    for e in range(3):
        perm = jnp.where(same & (col % 64 == row_w + (e - 1)), 1.0, 0.0).astype(BF)
        for f in range(4):
            moved = dot(perm, x_ref[f]).astype(BF)
            for g in range(4):
                xp_ref[g * 128 + f * 32 : g * 128 + f * 32 + 32, e * chans : (e + 1) * chans] = moved[
                    g * 32 : g * 32 + 32
                ]
        for ab in range(9):
            tap = (ab * 3 + e) * 16
            wt_ref[ab * 16 : ab * 16 + 16, e * chans : (e + 1) * chans] = w_ref[tap : tap + 16, :]
    y = dot(wt_ref[...], xp_ref[...], ((1,), (1,)))
    lane = iota((16, 128), 1)

    def part(a, b, p, q):
        at = (a * 3 + b) * 16
        g = p * 2 + q
        return y[at : at + 16, g * 128 : (g + 1) * 128]

    def frames(of):
        one = jnp.where(lane >= 32, pltpu.roll(of(1), 32, 1), 0.0)
        two = jnp.where(lane >= 64, pltpu.roll(of(0), 64, 1), 0.0)
        return of(2) + one + two

    for q in range(2):
        own0 = frames(lambda a: part(a, 1, 0, q) + part(a, 2, 1, q))
        own1 = frames(lambda a: part(a, 0, 0, q) + part(a, 1, 1, q))
        down = frames(lambda a: part(a, 0, 1, q))
        up = frames(lambda a: part(a, 2, 0, q))
        out_ref[q * 16 : q * 16 + 16, :] = own0.astype(BF)
        out_ref[32 + q * 16 : 48 + q * 16, :] = own1.astype(BF)
        out_ref[128 + q * 16 : 144 + q * 16, :] = down.astype(BF)
        out_ref[160 + q * 16 : 176 + q * 16, :] = up.astype(BF)
    r2, c2 = iota((256, 256), 0), iota((256, 256), 1)
    spread = ((r2 // 64) == (c2 // 32) % 4) & (r2 % 64 == 2 * (c2 % 32) + c2 // 128)
    spread = jnp.where(spread, 1.0, 0.0)
    noise = jnp.concatenate(
        [jnp.concatenate([noise_ref[f, p] for f in range(4)], axis=1) for p in range(2)], axis=0
    )
    moved = dot(noise, spread, precision=HIGH)
    for p in range(2):
        for q in range(2):
            at = 64 + (p * 2 + q) * 16
            out_ref[at : at + 16, :] = moved[p * 16 : p * 16 + 16, q * 128 : (q + 1) * 128].astype(BF)


def gram_kernel(flow_ref, embed_hbm, time_hbm, after_ref, out_ref, embed_ref, time_ref, sems):
    copies = [
        pltpu.make_async_copy(time_hbm, time_ref, sems.at[0]),
        pltpu.make_async_copy(embed_hbm, embed_ref, sems.at[1]),
    ]
    for copy in copies:
        copy.start()
    start = flow_ref[0, 0].astype(F32) / TGRID
    finish = flow_ref[0, 1].astype(F32) / TGRID
    freqs = frequencies()
    angle = freqs * jnp.where(iota((8, 128), 1) < QUARTER, finish, finish - start)
    sines, cosines = jnp.sin(angle), jnp.cos(angle)
    row = iota((8, 128), 0)
    first = jnp.where(row == 0, sines, jnp.where(row == 1, freqs * cosines, 0.0))
    second = jnp.where(row == 0, cosines, jnp.where(row == 1, -freqs * sines, 0.0))
    q = QUARTER
    feats = jnp.concatenate([first[:, :q], second[:, :q], first[:, q:], second[:, q:]], axis=1)
    feat_hi, feat_lo = split(feats)
    feat_mid = (feats - feat_hi.astype(F32) - feat_lo.astype(F32)).astype(BF)
    feats = jnp.concatenate([feat_hi, feat_lo, feat_mid, jnp.zeros_like(feat_hi)], axis=0)
    for copy in copies:
        copy.wait()
    tau = dot(feats, time_ref[...])
    tau = tau[0:8] + tau[8:16] + tau[16:24]
    embed = embed_ref[...]
    out_ref[0:64, 0:64] = dot(embed, embed, ((1,), (1,)))
    tau_hi, tau_lo = split(tau)
    tau_mid = (tau - tau_hi.astype(F32) - tau_lo.astype(F32)).astype(BF)
    taus = jnp.concatenate([tau_hi, tau_lo, tau_mid, jnp.zeros_like(tau_hi)], axis=0)
    cross = dot(embed, taus, ((1,), (1,)))
    out_ref[0:64, 64:128] = jnp.concatenate(
        [cross[:, 0:8] + cross[:, 8:16] + cross[:, 16:24], jnp.zeros((64, 56), F32)], axis=1
    )
    out_ref[64:72, :] = jnp.sum(tau * tau[0:1], axis=1, keepdims=True) + jnp.zeros((8, 128), F32)


def time_coefs(s_hi, s_lo, c_hi, c_lo, kind):
    r = iota((8, s_hi.shape[1]), 0)

    def coefs(high, low):
        if kind == 0:
            return jnp.where((r % 4 == 0) | (r % 4 == 3), high, jnp.where(r % 4 == 1, low, 0.0))
        return jnp.where(r % 4 == 2, low, high)

    plain = jnp.where(r < 4, coefs(s_hi, s_lo), 0.0)
    tangent = jnp.where(r < 4, coefs(c_hi, c_lo), coefs(s_hi, s_lo))
    return plain, tangent


def attention_kernel(
    flow_ref, n_ref, gram_ref, out_hbm, dout_hbm, out_ref, dout_ref, sems, keep_ref, aq_ref, as_ref, ad_ref, av_ref, *scratch):
    peers = n_ref.shape[0]
    tokens = peers * 128
    heads = 3
    rows = heads * 128
    chunk = 16
    zero = lambda r, c=HD: jnp.zeros((r, c), BF)
    cat = lambda xs, axis=0: jnp.concatenate(xs, axis=axis)
    up = lambda x: x.astype(BF).astype(F32)

    flow_t = flow_ref[0, 1].astype(F32) / TGRID
    patches, tangents = [], []
    none = jnp.zeros((32, 128), F32)
    for i in range(peers):
        above = n_ref[i - 1, 496:528].astype(F32) if i > 0 else none
        below = n_ref[i + 1, 528:560].astype(F32) if i + 1 < peers else none
        latent = n_ref[i, 368:432].astype(F32) + cat([above, below])
        noise = n_ref[i, 432:496].astype(F32)
        patches.append((1.0 - flow_t) * latent + flow_t * noise)
        tangents.append(noise - latent)
    p, dp = cat(patches, 1), cat(tangents, 1)
    gp = dot(gram_ref[0:64, 0:64], p, precision=HIGH)
    e_tau, e_dtau = gram_ref[0:64, 64:65], gram_ref[0:64, 65:66]
    mean_sq = jnp.sum(p * (gp + 2.0 * e_tau), axis=0, keepdims=True) + gram_ref[64:65, 0:1]
    mean_sq = jnp.maximum(mean_sq * (1.0 / D), 0.0)
    mixed = jnp.sum(gp * dp + p * e_dtau + dp * e_tau, axis=0, keepdims=True) + gram_ref[65:66, 0:1]
    s = lax.rsqrt(mean_sq + EPSILON)
    c = -(s * s * s) * (mixed * (1.0 / D))
    a = p * s
    da = dp * s + p * c
    a_hi, da_hi = up(a), up(da)
    s_hi, c_hi = up(s), up(c)
    coefs = (s_hi, s - s_hi, c_hi, c - c_hi)
    m_s, m_d = time_coefs(*coefs, 1)
    v_s, v_d = time_coefs(*coefs, 0)
    gap = lambda n: jnp.zeros((n, tokens), F32)
    as_ref[...] = cat([a_hi, a_hi, a - a_hi, m_s, gap(56)]).astype(BF)
    ad_ref[...] = cat([a_hi, da_hi, a_hi, m_s, gap(8), m_d, gap(40)]).astype(BF)
    av_ref[...] = cat([a_hi, a_hi, da_hi, v_s, v_d, v_s, v_d, gap(32)]).T.astype(BF)
    keep_ref[...] = cat([a, da, v_s, v_d])
    own = pl.multiple_of(lax.axis_index("seq") * 128, 128)
    mine = keep_ref[:, pl.ds(own, 128)]
    a, da = mine[0:64], mine[64:128]
    a_hi, da_hi = up(a), up(da)
    gap = jnp.zeros((120, 128), F32)
    aq_ref[0:128, :] = cat([a_hi, a - a_hi, mine[128:136], gap]).T.astype(BF)
    aq_ref[128:256, :] = cat([da_hi, da - da_hi, mine[136:144], gap]).T.astype(BF)

    lane = iota((128, 256), 1)
    low_s = ((lane >= 64) & (lane < 128)) | (lane == 193) | (lane == 197)
    low_d = ((lane >= 128) & (lane < 192)) | (lane == 193) | (lane == 209) | (lane == 213)
    from_q = ((lane >= 64) & (lane < 128)) | (lane >= 200)
    lane = iota((256, 256), 1)
    low_r = ((lane >= 64) & (lane < 128)) | (lane >= 208)
    l = iota((72, HD), 1)

    def times(g, block):
        return n_ref[g, 320:368].astype(F32)[8 * block : 8 * block + 8]

    def scores(g):
        s_ref, d_ref = scratch[4 * (g % 2) : 4 * (g % 2) + 2]
        made = {}

        def absorb(h):
            first = cat([n_ref[g, 0:64].astype(F32), times(g, 0)])
            second = cat([n_ref[g, 64:128].astype(F32), times(g, 1)])
            block = (first, pltpu.roll(first, 64, 1), second)[h]
            swapped = (pltpu.roll(first, 64, 1), first, pltpu.roll(second, 64, 1))[h]
            early = pltpu.roll(second, HD - 8 * h, 1) if h else second
            late = pltpu.roll(second, 16 - 8 * h, 1) if h < 2 else second
            again = jnp.where(
                l < 64, block, jnp.where(l < 72, early, jnp.where((l >= 80) & (l < 88), late, 0.0))
            )
            b = cat([jnp.where(l < 64, block, swapped), again], 1)
            b = cat([b, jnp.zeros((8, 256), F32)]).astype(BF)
            b = cat([b[:64], b[:64], b[64:], zero(112, 256)])
            absorbed = dot(aq_ref[...], b) * (LOG2E * HD ** -0.5)
            hi = absorbed.astype(BF).astype(F32)
            lo = absorbed - hi
            x = jnp.where(low_s, lo[:128], hi[:128]).astype(BF)
            low = jnp.where(from_q, lo[:128], lo[128:])
            high = jnp.where(from_q, hi[:128], hi[128:])
            made[h] = (x, jnp.where(low_d, low, high).astype(BF))

        def score(j, which):
            cols = slice(j * 256, (j + 1) * 256)
            x = cat([made[h][which] for h in range(heads)])
            if which == 0:
                s_ref[:, cols] = dot(x, as_ref[:, cols])
            else:
                d_ref[:, cols] = dot(x, ad_ref[:, cols])

        parts = [lambda h=h: absorb(h) for h in range(heads)]
        tiles = as_ref.shape[1] // 256
        return parts + [lambda j=j, w=w: score(j, w) for w in (0, 1) for j in range(tiles)]

    def softmax(g):
        s_ref, d_ref, et_ref, l_ref = scratch[4 * (g % 2) : 4 * (g % 2) + 4]

        def step(i):
            r = slice(i * chunk, (i + 1) * chunk)
            s = s_ref[r]
            e = jnp.exp2(s - jnp.max(s, axis=1, keepdims=True))
            d = d_ref[r]
            inv = 1.0 / jnp.sum(e, axis=1, keepdims=True)
            mean = jnp.sum(e * d, axis=1, keepdims=True) * inv
            et_ref[r] = e.astype(BF)
            et_ref[rows + i * chunk : rows + (i + 1) * chunk] = (e * (d - mean)).astype(BF)
            l_ref[r] = jnp.broadcast_to(inv, (chunk, 128))

        return [lambda i=i: step(i) for i in range(rows // chunk)]

    def outputs(g):
        et_ref, l_ref = scratch[4 * (g % 2) + 2 : 4 * (g % 2) + 4]
        made = {}

        def mixing():
            made[0] = cat([dot(et_ref[k * 128 : (k + 1) * 128], av_ref[...]) for k in range(2 * heads)])

        def output(h):
            mixes = made[0]
            at = 128 + h * 64
            mv = n_ref[g, at : at + 64]
            t = times(g, 2 + h)
            blank = jnp.zeros((8, HD), F32)
            early, late = cat([t, blank]).astype(BF), cat([blank, t]).astype(BF)
            inv = l_ref[h * 128 : (h + 1) * 128, 0:1]
            mix = mixes[h * 128 : (h + 1) * 128] * inv
            mix_t = mixes[rows + h * 128 : rows + (h + 1) * 128] * (inv * LN2)
            nx = cat([mv, mv, zero(64), early, early, zero(32)])
            ny = cat([zero(128), mv, late, late, zero(32)])
            both = cat([mix, mix_t])
            hi = both.astype(BF).astype(F32)
            both = jnp.where(low_r, both - hi, hi).astype(BF)
            z = dot(both, cat([nx, ny], 1))
            cols = slice((g * heads + h) * HD, (g * heads + h + 1) * HD)
            out_ref[:, cols] = z[:128, :HD].astype(BF)
            dout_ref[:, cols] = (z[128:, :HD] + z[:128, HD:]).astype(BF)

        return [mixing] + [lambda h=h: output(h) for h in range(heads)]

    copies = []

    def send(g):
        cols = slice(g * heads * HD, (g + 1) * heads * HD)
        for k, (src, dst) in enumerate(((out_ref, out_hbm), (dout_ref, dout_hbm))):
            copy = pltpu.make_async_copy(src.at[:, cols], dst.at[:, cols], sems.at[k, g])
            copy.start()
            copies.append(copy)

    for part in scores(0):
        part()
    for g in range(peers):
        matmuls = (outputs(g - 1) if g > 0 else []) + (scores(g + 1) if g + 1 < peers else [])
        steps = softmax(g)
        done = 0
        for i, step in enumerate(steps):
            while done < len(matmuls) and done * len(steps) <= i * len(matmuls):
                matmuls[done]()
                done += 1
            step()
        for part in matmuls[done:]:
            part()
        if g > 0:
            send(g - 1)
    for part in outputs(peers - 1):
        part()
    send(peers - 1)
    for copy in copies:
        copy.wait()


def local(clip_features, enc_weight, noise_field, flow_times, embed_weight, time_weight, norm_gain, qkv_weight):
    clips = lax.axis_size("clip")
    peers = lax.axis_size("seq")
    depth = qkv_weight.shape[0]
    width = qkv_weight.shape[2]
    weight = qkv_weight.transpose(1, 0, 2)
    gain = norm_gain[None]
    shape = jax.ShapeDtypeStruct
    rows = 8 * clips
    heads = width // HD
    tokens = 128 * peers
    window = depth + 64
    half = (3 * width + 128) // 2

    partial = pl.pallas_call(
        fold_kernel,
        grid=(1,),
        out_shape=shape((rows, half), BF),
        in_specs=[SMEM, HBM, HBM, HBM],
        out_specs=whole((rows, half)),
        scratch_shapes=[
            pltpu.VMEM((64, window), BF),
            pltpu.VMEM((1, window), F32),
            pltpu.VMEM((3, depth, width), BF),
            pltpu.SemaphoreType.DMA((5,)),
        ],
        compiler_params=params(),
        name="fold",
    )(flow_times, embed_weight, gain, weight)
    got = lax.all_to_all(partial.reshape(clips, 8, -1), "clip", 0, 0, tiled=True).reshape(rows, -1)

    conv = pl.pallas_call(
        conv_kernel,
        grid=(1,),
        out_shape=shape((192, 128), BF),
        in_specs=[HBM, HBM, HBM, ANY],
        out_specs=whole((192, 128)),
        scratch_shapes=[
            pltpu.VMEM((512, 3 * 384), BF),
            pltpu.VMEM((144, 3 * 384), BF),
            pltpu.VMEM((4, 128, 384), BF),
            pltpu.VMEM((432, 384), BF),
            pltpu.VMEM((4, 2, 16, 64), F32),
            pltpu.SemaphoreType.DMA((3,)),
        ],
        compiler_params=params(),
        name="conv",
    )(
        clip_features.reshape(4, 128, 384),
        enc_weight.transpose(0, 1, 2, 4, 3).reshape(432, 384),
        noise_field[0].transpose(0, 1, 3, 2),
        partial,
    )
    got, conv = lax.optimization_barrier((got, conv))

    second = pl.pallas_call(
        time_kernel,
        grid=(1,),
        out_shape=shape((rows, 3 * width), BF),
        in_specs=[ANY, HBM, HBM, HBM],
        out_specs=whole((rows, 3 * width)),
        scratch_shapes=[
            pltpu.VMEM((rows, half), BF),
            pltpu.VMEM((TFEAT, window), BF),
            pltpu.VMEM((1, window), F32),
            pltpu.VMEM((3, depth, width), BF),
            pltpu.SemaphoreType.DMA((6,)),
        ],
        compiler_params=params(60),
        name="time_rows",
    )(got, time_weight, gain, weight)
    got = lax.all_to_all(second.reshape(clips, 8, -1), "clip", 0, 0, tiled=True).reshape(rows, -1)

    gram = pl.pallas_call(
        gram_kernel,
        grid=(1,),
        out_shape=shape((72, 128), F32),
        in_specs=[SMEM, HBM, HBM, ANY],
        out_specs=whole((72, 128)),
        scratch_shapes=[
            pltpu.VMEM(embed_weight.shape, BF),
            pltpu.VMEM(time_weight.shape, BF),
            pltpu.SemaphoreType.DMA((2,)),
        ],
        compiler_params=params(),
        name="gram",
    )(flow_times, embed_weight, time_weight, second)
    got, gram = lax.optimization_barrier((got, gram))

    folded = pl.pallas_call(
        head_rows_kernel,
        grid=(1,),
        out_shape=shape((peers, 560, 128), BF),
        in_specs=[whole((rows, 3 * width)), whole((192, 128))],
        out_specs=whole((peers, 560, 128)),
        compiler_params=params(24),
        name="head_rows",
    )(got, conv)
    every = lax.all_to_all(folded, "seq", 0, 0, tiled=True)

    out, dout = pl.pallas_call(
        attention_kernel,
        grid=(1,),
        out_shape=[shape((128, peers * width), BF)] * 2,
        in_specs=[SMEM, whole((peers, 560, 128)), whole((72, 128))],
        out_specs=[ANY] * 2,
        scratch_shapes=[pltpu.VMEM((128, peers * width), BF)] * 2
        + [pltpu.SemaphoreType.DMA((2, peers))]
        + [pltpu.VMEM((144, tokens), F32), pltpu.VMEM((256, 256), BF)]
        + [pltpu.VMEM((256, tokens), BF)] * 2
        + [pltpu.VMEM((tokens, 256), BF)]
        + [
            pltpu.VMEM((heads * 128, tokens), F32),
            pltpu.VMEM((heads * 128, tokens), F32),
            pltpu.VMEM((2 * heads * 128, tokens), BF),
            pltpu.VMEM((heads * 128, 128), F32),
        ]
        * 2,
        compiler_params=params(),
        name="attention",
    )(flow_times, every, gram)
    return (out[None], dout[None])


def solution(mesh):
    placed = (
        P("clip", None, "seq", None, None),
        P(),
        P("clip", None, "seq", None, None),
        P("clip", None),
        P(),
        P(),
        P(),
        P("clip", None, "seq"),
    )
    return jax.shard_map(
        local,
        mesh=mesh,
        in_specs=placed,
        out_specs=(P("clip", "seq", None), P("clip", "seq", None)),
        check_vma=False,
    )
```
